32 devices in a mesh: batch: 8 (over z, y), seq: 4 (over x, core).
Axes of the slice: x: 2, y: 2, z: 4, core: 2. Of those that a mesh axis runs over, the one named last changes fastest.
Arguments:
- sequence_input: bfloat16 [8, 1024, 768], P('batch', 'seq'), may hold values from -64 to 64
- bn_gain: float32 [768], replicated, may hold values from 0.1 to 1.9
- bn_bias: float32 [768], replicated, may hold values from -3 to 3
- conv_weight: bfloat16 [5, 768, 768], P(None, None, 'batch'), may hold values from -0.09375 to 0.09375
- conv_bias: float32 [768], replicated, may hold values from -3 to 3
- ln_gain: float32 [768], replicated, may hold values from 0.1 to 1.9
- ln_bias: float32 [768], replicated, may hold values from -3 to 3
- qkv_weight: bfloat16 [768, 1792], P(None, 'batch'), may hold values from -32 to 32
Outputs:
- pooled: bfloat16 [8, 512, 768], P('batch', 'seq')
- attended: bfloat16 [8, 512, 768], P('batch', 'seq')
The draws below stay inside these ranges and needn't reach their ends.
All inputs are finite; a program needn't handle non-finite values.
Results may differ from the reference program's by a relative error of at most 0.025.
The reference program's roundings to bfloat16 on the way (of `activated`, `normed`, `queries` and `weights`) count: a program that leaves them out, or rounds other values in their place, can miss the bound.
Values may be sent and summed in bfloat16 or wider, within the bound.
A program may use at most 64 MiB of HBM per device.

```python
import jax
import jax.numpy as jnp
from jax import lax

D = 768
HEADS = 8
KEY = 64
VAL = 96
KW = 5
RAW = 1024
BATCH = 8


def draw_sequence_input(key, part):
    base = jax.random.fold_in(key, 101)
    keys_list = jax.random.split(base, 4)
    chan_scale = jnp.exp(jax.random.uniform(keys_list[0], (D,), jnp.float32, jnp.log(0.3), jnp.log(3.0)))
    chan_mean = 0.7 * jax.random.normal(keys_list[1], (D,), jnp.float32)
    place = jnp.arange(RAW, dtype=jnp.float32) / RAW
    row_scale = 10.0 ** (place - 0.5)
    seq_place = jnp.arange(BATCH, dtype=jnp.float32) / max(BATCH - 1, 1)
    seq_scale = 3.0 ** (seq_place - 0.5)
    rough = jnp.exp(jax.random.uniform(keys_list[2], (BATCH, RAW, 1), jnp.float32, -0.35, 0.35))
    noise = jax.random.normal(keys_list[3], (BATCH, RAW, D), jnp.float32)
    values_out = (noise * chan_scale + chan_mean) * rough * row_scale[None, :, None] * seq_scale[:, None, None]
    return jnp.clip(values_out, -64.0, 64.0).astype(jnp.bfloat16)


def draw_qkv_weight(key, part):
    base = jax.random.fold_in(key, 202)
    keys_list = jax.random.split(base, 3)
    factor = D ** (-0.5)
    query_part = jax.random.normal(keys_list[0], (D, HEADS * KEY), jnp.float32) * factor
    key_part = jax.random.normal(keys_list[1], (D, HEADS * KEY), jnp.float32) * factor
    value_part = jax.random.normal(keys_list[2], (D, HEADS * VAL), jnp.float32) * factor
    query_part = 2.5 * query_part
    joined = jnp.concatenate([query_part, key_part, value_part], axis=1)
    return jnp.clip(joined, -32.0, 32.0).astype(jnp.bfloat16)


def block_scale(rng, dims, shards, low, top_value):
    factor_of = 1.0
    for axis_at, shards_of in shards:
        draws = jax.random.uniform(jax.random.fold_in(jax.random.fold_in(rng, 6), axis_at), (shards_of,), jnp.float32, low / len(shards), top_value / len(shards))
        factor_of = factor_of * jnp.repeat(jnp.exp(draws), dims[axis_at] // shards_of).reshape((-1,) + (1,) * (len(dims) - 1 - axis_at))
    return factor_of


def scatter_about(stream_key, dims, scale, reach, cuts=(), kind=jnp.bfloat16):
    level = block_scale(stream_key, dims, cuts, -0.22, 0.18) if cuts else 1.0
    values = jax.random.normal(stream_key, dims, jnp.float32) * scale * level
    return jnp.minimum(jnp.maximum(values, -reach), reach).astype(kind)


def setup_inputs(seed: int = 0) -> dict:
    streams_of = jax.random.split(jax.random.key(seed), 9)
    sequence_input = draw_sequence_input(jax.random.fold_in(streams_of[8], 71), 0)
    bn_gain = jnp.clip(1.0 + 0.18 * jax.random.normal(streams_of[1], (D,), jnp.float32), 0.1, 1.9)
    bn_bias = scatter_about(streams_of[2], (D,), 0.5, 3.0, (), jnp.float32)
    conv_weight = scatter_about(streams_of[3], (KW, D, D), (KW * D) ** -0.5, 0.09375, ((2, 8),))
    conv_bias = scatter_about(streams_of[4], (D,), 0.5, 3.0, (), jnp.float32)
    ln_gain = jnp.clip(1.0 + 0.18 * jax.random.normal(streams_of[5], (D,), jnp.float32), 0.1, 1.9)
    ln_bias = scatter_about(streams_of[6], (D,), 0.5, 3.0, (), jnp.float32)
    qkv_weight = draw_qkv_weight(jax.random.fold_in(streams_of[8], 71), 0)
    return {"sequence_input": sequence_input, "bn_gain": bn_gain, "bn_bias": bn_bias, "conv_weight": conv_weight, "conv_bias": conv_bias, "ln_gain": ln_gain, "ln_bias": ln_bias, "qkv_weight": qkv_weight}


epsilon = 1e-05

def reference(sequence_input, bn_gain, bn_bias, conv_weight, conv_bias, ln_gain, ln_bias, qkv_weight):
    whole = sequence_input.astype(jnp.float32)
    count = whole.shape[0] * whole.shape[1]
    total = lax.optimization_barrier(jnp.sum(whole, axis=(0, 1)))
    squares = lax.optimization_barrier(jnp.sum(whole * whole, axis=(0, 1)))
    mean = total / count
    var = squares / count - mean * mean
    head_keys = HEADS * KEY

    def one_sequence(single):
        values_in = single.astype(jnp.float32)
        activated = jax.nn.gelu((values_in - mean) * lax.rsqrt(var + epsilon) * bn_gain + bn_bias, approximate=True).astype(jnp.bfloat16)
        positions = activated.shape[0]
        padded = jnp.pad(activated, ((2, 2), (0, 0)))
        conv_out = jnp.zeros((positions, conv_weight.shape[2]), jnp.float32) + conv_bias
        for tap_index in range(conv_weight.shape[0]):
            conv_out = conv_out + jnp.dot(padded[tap_index:tap_index + positions], conv_weight[tap_index], preferred_element_type=jnp.float32)
        pooled = conv_out.reshape(positions // 2, 2, conv_out.shape[1]).max(axis=1).astype(jnp.bfloat16)
        pooled_wide = pooled.astype(jnp.float32)
        centre = lax.optimization_barrier(jnp.mean(pooled_wide, axis=-1, keepdims=True))
        spread = lax.optimization_barrier(jnp.mean((pooled_wide - centre) ** 2, axis=-1, keepdims=True))
        normed = ((pooled_wide - centre) * lax.rsqrt(spread + epsilon) * ln_gain + ln_bias).astype(jnp.bfloat16)
        proj = jnp.dot(normed, qkv_weight, preferred_element_type=jnp.float32)
        bins = proj.shape[0]
        queries = (proj[:, :head_keys] * KEY ** (-0.5)).astype(jnp.bfloat16)
        key_rows = proj[:, head_keys:2 * head_keys].astype(jnp.bfloat16)
        value_rows = proj[:, 2 * head_keys:].astype(jnp.bfloat16)
        queries, key_rows, value_rows = lax.optimization_barrier((queries, key_rows, value_rows))
        query_wide = queries.astype(jnp.float32).reshape(bins, HEADS, KEY)
        key_wide = key_rows.astype(jnp.float32).reshape(bins, HEADS, KEY)
        value_wide = value_rows.astype(jnp.float32).reshape(bins, HEADS, VAL)
        scores = jnp.einsum('qhk,jhk->hqj', query_wide, key_wide)
        largest = lax.optimization_barrier(jnp.max(scores, axis=-1, keepdims=True))
        exps = jnp.exp(scores - largest)
        denominator = lax.optimization_barrier(jnp.sum(exps, axis=-1))
        weights = lax.optimization_barrier(exps.astype(jnp.bfloat16)).astype(jnp.float32)
        summed = jnp.einsum('hqj,jhv->hqv', weights, value_wide)
        attended = (summed / denominator[..., None]).transpose(1, 0, 2).reshape(bins, HEADS * VAL).astype(jnp.bfloat16)
        return (pooled, attended)
    pooled, attended = lax.map(one_sequence, sequence_input)
    return (pooled, attended)
```

```python
import jax
import jax.numpy as jnp
from jax import lax
from jax.experimental import pallas as pl
from jax.experimental.pallas import tpu as pltpu
from jax.sharding import PartitionSpec as P

HEADS = 8
KEY = 64
VAL = 96


epsilon = 1e-05


def extended(cells, sides, width):
    for axis, dim in sides:
        count = lax.axis_size(axis)
        ends = count - 1
        head = lax.slice_in_dim(cells, 0, width, axis=dim)
        tail = lax.slice_in_dim(cells, cells.shape[dim] - width, cells.shape[dim], axis=dim)
        cells = jnp.concatenate(
            [
                lax.ppermute(tail, axis, [(i, (i + 1) % count) for i in range(ends)]),
                cells,
                lax.ppermute(head, axis, [((i + 1) % count, i) for i in range(ends)]),
            ],
            axis=dim,
        )
    return cells


def conv_taps(padded, kernel, positions):
    result = None
    for tap_index in range(kernel.shape[0]):
        window = padded[:, tap_index : tap_index + positions]
        product = jnp.einsum(
            "slc,co->slo", window, kernel[tap_index], preferred_element_type=jnp.float32
        )
        result = product if result is None else result + product
    return result


def online_step(carry, query_rows, key_block, value_block):
    best, weight_sum, accum = carry
    scores = jnp.einsum(
        "sqhk,sjhk->shqj", query_rows, key_block, preferred_element_type=jnp.float32
    )
    newest = jnp.maximum(best, jnp.max(scores, axis=-1))
    fade = jnp.exp(best - newest)
    weights = jnp.exp(scores - newest[..., None])
    weight_sum = weight_sum * fade + jnp.sum(weights, axis=-1)
    accum = accum * fade[..., None] + jnp.einsum(
        "shqj,sjhv->shqv",
        weights.astype(jnp.bfloat16),
        value_block,
        preferred_element_type=jnp.float32,
    )
    return (newest, weight_sum, accum)


def blocked_attend(carry, query_rows, key_piece, value_piece):
    rows = key_piece.shape[1]
    block = min(rows, 512)
    for first in range(0, rows, block):
        carry = online_step(
            carry,
            query_rows,
            key_piece[:, first : first + block],
            value_piece[:, first : first + block],
        )
    return carry


def empty_state(seqs_here, heads_here, rows):
    return (
        jnp.full((seqs_here, heads_here, rows), -jnp.inf, jnp.float32),
        jnp.zeros((seqs_here, heads_here, rows), jnp.float32),
        jnp.zeros((seqs_here, heads_here, rows, VAL), jnp.float32),
    )


def on_device(
    sequence_input, bn_gain, bn_bias, conv_weight, conv_bias, ln_gain, ln_bias, qkv_weight
):
    seqs_here = sequence_input.shape[0]
    positions = sequence_input.shape[1]
    channels = sequence_input.shape[2]
    values_in = sequence_input.astype(jnp.float32)
    total, squares = lax.psum(
        (jnp.sum(values_in, axis=(0, 1)), jnp.sum(values_in * values_in, axis=(0, 1))),
        ("batch", "seq"),
    )
    count = float(seqs_here * positions * lax.axis_size("batch") * lax.axis_size("seq"))
    mean = total / count
    var = squares / count - mean * mean
    activated = jax.nn.gelu(
        (values_in - mean) * lax.rsqrt(var + epsilon) * bn_gain + bn_bias, approximate=True
    ).astype(jnp.bfloat16)
    padded = extended(activated, (("seq", 1),), 2)
    conv_out = conv_taps(
        padded, lax.all_gather(conv_weight, "batch", axis=2, tiled=True), positions
    )
    conv_out = conv_out + conv_bias
    bins_here = positions // 2
    pooled = conv_out.reshape(seqs_here, bins_here, 2, channels).max(axis=2).astype(jnp.bfloat16)
    pooled_wide = pooled.astype(jnp.float32)
    centre = jnp.mean(pooled_wide, axis=-1, keepdims=True)
    spread = jnp.mean((pooled_wide - centre) ** 2, axis=-1, keepdims=True)
    normed = ((pooled_wide - centre) * lax.rsqrt(spread + epsilon) * ln_gain + ln_bias).astype(
        jnp.bfloat16
    )
    proj = jnp.einsum(
        "sbd,dk->sbk",
        normed,
        lax.all_gather(qkv_weight, "batch", axis=1, tiled=True),
        preferred_element_type=jnp.float32,
    )
    head_keys = HEADS * KEY
    queries = (proj[..., :head_keys] * KEY ** (-0.5)).astype(jnp.bfloat16)
    key_rows = proj[..., head_keys : 2 * head_keys].astype(jnp.bfloat16)
    value_rows = proj[..., 2 * head_keys :].astype(jnp.bfloat16)
    query_heads = queries.reshape(seqs_here, bins_here, HEADS, KEY)
    key_piece = lax.all_gather(key_rows, "seq", axis=1, tiled=True)
    value_piece = lax.all_gather(value_rows, "seq", axis=1, tiled=True)
    width_now = key_piece.shape[1]
    best, weight_sum, accum = blocked_attend(
        empty_state(seqs_here, HEADS, bins_here),
        query_heads,
        key_piece.reshape(seqs_here, width_now, HEADS, KEY),
        value_piece.reshape(seqs_here, width_now, HEADS, VAL),
    )
    attended = (
        (accum / weight_sum[..., None])
        .transpose(0, 2, 1, 3)
        .reshape(seqs_here, bins_here, HEADS * VAL)
        .astype(jnp.bfloat16)
    )
    return (pooled, attended)


LINES = 4
PLANES = 2
RUNS = 4
TAPS = 5
UNIT = 32
MESH = pl.DeviceIdType.MESH
GELU_IN = 0.7978845608028654


def unit_of(slot, s):
    quarter = HEADS * KEY // RUNS // UNIT
    values = HEADS * VAL // RUNS // UNIT
    if slot < quarter:
        return quarter * s + slot
    if slot < 2 * quarter:
        return RUNS * quarter + quarter * s + slot - quarter
    return 2 * RUNS * quarter + values * s + slot - 2 * quarter


def fused_kernel(
    x_ref,
    gain_ref,
    bias_ref,
    piece_ref,
    conv_bias_ref,
    ln_gain_ref,
    ln_bias_ref,
    units_ref,
    pooled_ref,
    attended_ref,
    x_all,
    sums_seq,
    sums_batch,
    act,
    pieces,
    units,
    pool_wide,
    pool_all,
    normed,
    q_rows,
    k_rows,
    v_rows,
    att_out,
    att_in,
    reorder,
    x_send,
    x_recv,
    ss_send,
    ss_recv,
    sb_send,
    sb_recv,
    c_send,
    c_recv,
    u_send,
    u_recv,
    p_send,
    p_recv,
    a_send,
    a_recv,
):
    b = lax.axis_index("batch")
    s = lax.axis_index("seq")
    z, y = b // PLANES, b % PLANES
    bins, wide = x_ref.shape
    channels = wide // 2
    rows = RUNS * bins
    n_batch = LINES * PLANES
    share = channels // RUNS
    part = share // n_batch
    count = float(n_batch * RUNS * bins * 2)
    n_units = units.shape[0]
    per_shard = units_ref.shape[0]

    sibling = s + 1 - 2 * (s % 2)
    across = (s + 2) % RUNS
    diagonal = (sibling + 2) % RUNS
    mate = z * PLANES + 1 - y

    def remote(src, dst, send, recv, to_b, to_s):
        return pltpu.make_async_remote_copy(
            src_ref=src,
            dst_ref=dst,
            send_sem=send,
            recv_sem=recv,
            device_id=(to_b, to_s),
            device_id_type=MESH,
        )

    barrier = pltpu.get_barrier_semaphore()
    for step in range(1, RUNS):
        pl.semaphore_signal(barrier, inc=1, device_id=(b, (s + step) % RUNS), device_id_type=MESH)
    for step in range(1, n_batch):
        pl.semaphore_signal(
            barrier, inc=1, device_id=((b + step) % n_batch, s), device_id_type=MESH
        )

    total = jnp.zeros((1, wide), jnp.float32)
    squares = jnp.zeros((1, wide), jnp.float32)

    def add_rows(i, carry):
        total, squares = carry
        block = x_ref[pl.ds(pl.multiple_of(i * 16, 16), 16), :].astype(jnp.float32)
        return (
            total + jnp.sum(block, axis=0, keepdims=True),
            squares + jnp.sum(block * block, axis=0, keepdims=True),
        )

    total, squares = lax.fori_loop(0, bins // 16, add_rows, (total, squares))
    sums_seq[s, 0:1, :] = total[:, :channels] + total[:, channels:]
    sums_seq[s, 1:2, :] = squares[:, :channels] + squares[:, channels:]

    pl.semaphore_wait(barrier, RUNS - 1 + n_batch - 1)

    started = []

    def go(copy):
        copy.start()
        started.append(copy)

    for step in range(1, RUNS):
        go(
            remote(
                sums_seq.at[s],
                sums_seq.at[s],
                ss_send.at[step],
                ss_recv.at[s],
                b,
                (s + step) % RUNS,
            )
        )
    for step in range(1, LINES):
        to = ((z + step) % LINES) * PLANES + y
        go(remote(piece_ref, pieces.at[b], c_send.at[step], c_recv.at[b], to, s))
    go(remote(piece_ref, pieces.at[b], c_send.at[0], c_recv.at[b], mate, s))
    go(remote(x_ref, x_all.at[s], x_send.at[0], x_recv.at[s], b, across))
    go(remote(x_ref, x_all.at[s], x_send.at[1], x_recv.at[s], b, sibling))
    own_x = pltpu.make_async_copy(x_ref, x_all.at[s], x_recv.at[s])
    own_x.start()
    own_piece = pltpu.make_async_copy(piece_ref, pieces.at[b], c_recv.at[b])
    own_piece.start()

    def arrived(dst, sem):
        pltpu.make_async_copy(dst, dst, sem).wait()

    for step in range(1, RUNS):
        other = (s + step) % RUNS
        arrived(sums_seq.at[other], ss_recv.at[other])
    sums_batch[b] = (sums_seq[0] + sums_seq[1]) + (sums_seq[2] + sums_seq[3])
    for step in range(1, n_batch):
        go(
            remote(
                sums_batch.at[b],
                sums_batch.at[b],
                sb_send.at[step],
                sb_recv.at[b],
                (b + step) % n_batch,
                s,
            )
        )

    for slot in range(n_units):
        unit = unit_of(slot, s)
        holder = unit // per_shard

        @pl.when(holder == b)
        def _(slot=slot, unit=unit):
            mine = units_ref.at[unit - per_shard * b]
            for step in range(1, LINES):
                to = ((z + step) % LINES) * PLANES + y
                remote(
                    mine, units.at[slot], u_send.at[slot, step], u_recv.at[slot], to, s
                ).start()
            remote(mine, units.at[slot], u_send.at[slot, 0], u_recv.at[slot], mate, s).start()
            pltpu.make_async_copy(mine, units.at[slot], u_recv.at[slot]).start()

    def forward_piece(step):
        source = ((z + step) % LINES) * PLANES + y
        arrived(pieces.at[source], c_recv.at[source])
        go(
            remote(
                pieces.at[source],
                pieces.at[source],
                c_send.at[LINES - 1 + step],
                c_recv.at[source],
                mate,
                s,
            )
        )

    for step in range(1, n_batch):
        other = (b + step) % n_batch
        arrived(sums_batch.at[other], sb_recv.at[other])
    sums = jnp.zeros((2, channels), jnp.float32)
    for i in range(n_batch):
        sums = sums + sums_batch[i]
    mean = sums[0:1] / count
    var = sums[1:2] / count - mean * mean
    scale = lax.rsqrt(var + epsilon) * gain_ref[...]
    shift = bias_ref[...]
    mean2 = jnp.concatenate([mean, mean], axis=1)
    scale2 = jnp.concatenate([scale, scale], axis=1)
    shift2 = jnp.concatenate([shift, shift], axis=1)

    def activate(run):
        def body(i, _):
            first = pl.multiple_of(i * 16, 16)
            v = x_all[run, pl.ds(first, 16), :].astype(jnp.float32)
            v = (v - mean2) * scale2 + shift2
            g = 0.5 * v * (1.0 + jnp.tanh(GELU_IN * (v + 0.044715 * (v * v * v))))
            act[pl.ds(pl.multiple_of(run * bins + first, 16), 16), :] = g.astype(jnp.bfloat16)
            return 0

        lax.fori_loop(0, bins // 16, body, 0)

    own_x.wait()
    activate(s)
    forward_piece(1)
    arrived(x_all.at[sibling], x_recv.at[sibling])
    activate(sibling)
    arrived(x_all.at[across], x_recv.at[across])
    go(
        remote(
            x_all.at[across], x_all.at[across], x_send.at[2], x_recv.at[across], b, sibling
        )
    )
    forward_piece(3)
    activate(across)
    forward_piece(2)
    arrived(x_all.at[diagonal], x_recv.at[diagonal])
    activate(diagonal)

    def back(v):
        lane = lax.broadcasted_iota(jnp.int32, v.shape, 1)
        return jnp.where(lane == 0, 0.0, pltpu.roll(v, 1, 1))

    def ahead(v):
        lane = lax.broadcasted_iota(jnp.int32, v.shape, 1)
        return jnp.where(lane == rows - 1, 0.0, pltpu.roll(v, rows - 1, 1))

    contract_last = (((1,), (1,)), ((), ()))

    def convolve(source):
        piece = pieces[source]
        even = lax.dot_general(
            piece, act[:, :channels], contract_last, preferred_element_type=jnp.float32
        )
        odd = lax.dot_general(
            piece, act[:, channels:], contract_last, preferred_element_type=jnp.float32
        )
        e = [even[t * part : (t + 1) * part] for t in range(TAPS)]
        o = [odd[t * part : (t + 1) * part] for t in range(TAPS)]
        first = back(e[0] + o[1]) + e[2] + o[3] + ahead(e[4])
        second = back(o[0]) + e[1] + o[2] + ahead(e[3] + o[4])
        pool_wide[pl.ds(pl.multiple_of(source * part, 8), part), :] = jnp.maximum(first, second)

    own_piece.wait()

    def near(step, _):
        convolve(((z + step) % LINES) * PLANES + y)
        return 0

    lax.fori_loop(0, LINES, near, 0)

    def far(step, _):
        source = ((z + step) % LINES) * PLANES + 1 - y
        arrived(pieces.at[source], c_recv.at[source])
        convolve(source)
        return 0

    lax.fori_loop(0, LINES, far, 0)

    pool_all[s] = (pool_wide[...] + conv_bias_ref[...]).astype(jnp.bfloat16)
    go(remote(pool_all.at[s], pool_all.at[s], p_send.at[0], p_recv.at[s], b, across))
    go(remote(pool_all.at[s], pool_all.at[s], p_send.at[1], p_recv.at[s], b, sibling))

    for slot in range(n_units):
        holder = unit_of(slot, s) // per_shard

        @pl.when(jnp.logical_and(holder != b, holder % PLANES == y))
        def _(slot=slot):
            arrived(units.at[slot], u_recv.at[slot])
            remote(
                units.at[slot], units.at[slot], u_send.at[slot, 0], u_recv.at[slot], mate, s
            ).start()

    arrived(pool_all.at[across], p_recv.at[across])
    go(
        remote(
            pool_all.at[across], pool_all.at[across], p_send.at[2], p_recv.at[across], b, sibling
        )
    )
    arrived(pool_all.at[sibling], p_recv.at[sibling])
    arrived(pool_all.at[diagonal], p_recv.at[diagonal])

    def norm(j, _):
        lanes = pl.ds(pl.multiple_of(j * bins, 128), bins)
        blocks = [pool_all[r, :, lanes].astype(jnp.float32) for r in range(RUNS)]
        centre = sum(jnp.sum(v, axis=0, keepdims=True) for v in blocks) / channels
        spread = sum(jnp.sum((v - centre) ** 2, axis=0, keepdims=True) for v in blocks) / channels
        inverse = lax.rsqrt(spread + epsilon)
        for r in range(RUNS):
            at = slice(r * share, (r + 1) * share)
            normed[at, lanes] = (
                (blocks[r] - centre) * inverse * ln_gain_ref[at] + ln_bias_ref[at]
            ).astype(jnp.bfloat16)
        return 0

    lax.fori_loop(0, RUNS, norm, 0)

    lanes = pl.ds(pl.multiple_of(s * bins, 128), bins)
    for r in range(RUNS):
        block = pool_all[r, :, lanes].astype(jnp.float32)
        for i in range(n_batch):
            first = i * RUNS * part + r * part
            reorder[first : first + part, :] = block[i * part : (i + 1) * part]
    pooled_ref[...] = jnp.transpose(reorder[...]).astype(jnp.bfloat16)

    for slot in range(n_units):
        holder = unit_of(slot, s) // per_shard

        @pl.when(jnp.logical_or(holder == b, holder % PLANES != y))
        def _(slot=slot):
            arrived(units.at[slot], u_recv.at[slot])

    here = HEADS // RUNS
    keys = here * KEY
    n_keys = keys // UNIT
    normed_now = normed[...]
    wq = units[0:n_keys].reshape(keys, channels)
    q_rows[...] = (
        jnp.dot(wq, normed_now, preferred_element_type=jnp.float32) * KEY ** (-0.5)
    ).astype(jnp.bfloat16)
    wk = units[n_keys : 2 * n_keys].reshape(keys, channels)
    k_rows[...] = jnp.transpose(
        jnp.dot(wk, normed_now, preferred_element_type=jnp.float32)
    ).astype(jnp.bfloat16)
    wv = units[2 * n_keys :].reshape(here * VAL, channels)
    v_rows[...] = jnp.dot(wv, normed_now, preferred_element_type=jnp.float32).astype(jnp.bfloat16)

    def attend(run):
        lanes = pl.ds(pl.multiple_of(run * bins, 128), bins)
        q_now = q_rows[:, lanes]
        row = lax.broadcasted_iota(jnp.int32, q_now.shape, 0)
        for h in range(here):
            q_head = jnp.where(row // KEY == h, q_now, jnp.zeros_like(q_now))
            scores = jnp.dot(k_rows[...], q_head, preferred_element_type=jnp.float32)
            weights = jnp.exp(scores - jnp.max(scores, axis=0, keepdims=True))
            below = jnp.sum(weights, axis=0, keepdims=True)
            above = jnp.dot(
                v_rows[h * VAL : (h + 1) * VAL, :],
                weights.astype(jnp.bfloat16),
                preferred_element_type=jnp.float32,
            )
            att_out[run, h * VAL : (h + 1) * VAL, :] = (above / below).astype(jnp.bfloat16)

    for run, k in ((across, 0), (diagonal, 1), (sibling, 2)):
        attend(run)
        go(remote(att_out.at[run], att_in.at[s], a_send.at[k], a_recv.at[s], b, run))
    attend(s)
    att_in[s] = att_out[s]
    for run in (across, diagonal, sibling):
        arrived(att_in.at[run], a_recv.at[run])
    gathered = jnp.concatenate([att_in[r].astype(jnp.float32) for r in range(RUNS)], axis=0)
    attended_ref[...] = jnp.transpose(gathered).astype(jnp.bfloat16)

    for copy in started:
        copy.wait_send()
    for slot in range(n_units):
        holder = unit_of(slot, s) // per_shard

        @pl.when(holder % PLANES == y)
        def _(slot=slot):
            remote(
                units.at[slot], units.at[slot], u_send.at[slot, 0], u_recv.at[slot], mate, s
            ).wait_send()

        @pl.when(holder == b)
        def _(slot=slot):
            for step in range(1, LINES):
                to = ((z + step) % LINES) * PLANES + y
                remote(
                    units.at[slot], units.at[slot], u_send.at[slot, step], u_recv.at[slot], to, s
                ).wait_send()


def fused_on_device(
    sequence_input, bn_gain, bn_bias, conv_weight, conv_bias, ln_gain, ln_bias, qkv_weight
):
    _, positions, channels = sequence_input.shape
    bins = positions // 2
    rows = RUNS * bins
    n_batch = LINES * PLANES
    share = channels // RUNS
    part = share // n_batch
    s = lax.axis_index("seq")
    taps = conv_weight.shape[0]
    x = sequence_input.reshape(bins, 2 * channels)
    piece = lax.dynamic_slice_in_dim(conv_weight, s * part, part, axis=2)
    piece = piece.transpose(0, 2, 1).reshape(taps * part, channels)
    padded = -(-taps * part // 16) * 16
    piece = jnp.pad(piece, ((0, padded - taps * part), (0, 0)))

    def by_seq(v):
        return v.reshape(n_batch, RUNS, part).transpose(1, 0, 2)

    bias_here = lax.dynamic_index_in_dim(by_seq(conv_bias), s, 0, keepdims=False)
    per_shard = qkv_weight.shape[1] // UNIT
    units = (
        qkv_weight.reshape(n_batch, RUNS, part, per_shard, UNIT)
        .transpose(3, 4, 1, 0, 2)
        .reshape(per_shard, UNIT, channels)
    )
    n_units = per_shard * n_batch // RUNS
    keys = HEADS * KEY // RUNS
    vals = HEADS * VAL // RUNS
    bf16, f32 = jnp.bfloat16, jnp.float32
    dma = pltpu.SemaphoreType.DMA
    pooled, attended = pl.pallas_call(
        fused_kernel,
        out_shape=(
            jax.ShapeDtypeStruct((bins, channels), bf16),
            jax.ShapeDtypeStruct((bins, channels), bf16),
        ),
        in_specs=[pl.BlockSpec(memory_space=pltpu.VMEM)] * 8,
        out_specs=(pl.BlockSpec(memory_space=pltpu.VMEM),) * 2,
        scratch_shapes=[
            pltpu.VMEM((RUNS, bins, 2 * channels), bf16),
            pltpu.VMEM((RUNS, 2, channels), f32),
            pltpu.VMEM((n_batch, 2, channels), f32),
            pltpu.VMEM((rows, 2 * channels), bf16),
            pltpu.VMEM((n_batch, padded, channels), bf16),
            pltpu.VMEM((n_units, UNIT, channels), bf16),
            pltpu.VMEM((share, rows), f32),
            pltpu.VMEM((RUNS, share, rows), bf16),
            pltpu.VMEM((channels, rows), bf16),
            pltpu.VMEM((keys, rows), bf16),
            pltpu.VMEM((rows, keys), bf16),
            pltpu.VMEM((vals, rows), bf16),
            pltpu.VMEM((RUNS, vals, bins), bf16),
            pltpu.VMEM((RUNS, vals, bins), bf16),
            pltpu.VMEM((channels, bins), f32),
            dma((3,)),
            dma((RUNS,)),
            dma((RUNS,)),
            dma((RUNS,)),
            dma((n_batch,)),
            dma((n_batch,)),
            dma((2 * LINES - 1,)),
            dma((n_batch,)),
            dma((n_units, LINES)),
            dma((n_units,)),
            dma((3,)),
            dma((RUNS,)),
            dma((3,)),
            dma((RUNS,)),
        ],
        compiler_params=pltpu.CompilerParams(
            collective_id=0, has_side_effects=True, vmem_limit_bytes=48 * 1024 * 1024
        ),
    )(
        x,
        bn_gain.reshape(1, channels),
        bn_bias.reshape(1, channels),
        piece,
        bias_here.reshape(share, 1),
        by_seq(ln_gain).reshape(channels, 1),
        by_seq(ln_bias).reshape(channels, 1),
        units,
    )
    return (pooled[None], attended[None])


def solution(mesh):
    placed = (
        P("batch", "seq", None),
        P(),
        P(),
        P(None, None, "batch"),
        P(),
        P(),
        P(),
        P(None, "batch"),
    )
    fused = mesh.shape["batch"] == LINES * PLANES and mesh.shape["seq"] == RUNS
    return jax.shard_map(
        fused_on_device if fused else on_device,
        mesh=mesh,
        in_specs=placed,
        out_specs=(P("batch", "seq", None), P("batch", "seq", None)),
        check_vma=False,
    )
```

```python
import jax
import jax.numpy as jnp
from jax import lax
from jax.experimental import pallas as pl
from jax.experimental.pallas import tpu as pltpu
from jax.sharding import PartitionSpec as P

HEADS = 8
KEY = 64
VAL = 96


epsilon = 1e-05


def extended(cells, sides, width):
    for axis, dim in sides:
        count = lax.axis_size(axis)
        ends = count - 1
        head = lax.slice_in_dim(cells, 0, width, axis=dim)
        tail = lax.slice_in_dim(cells, cells.shape[dim] - width, cells.shape[dim], axis=dim)
        cells = jnp.concatenate(
            [
                lax.ppermute(tail, axis, [(i, (i + 1) % count) for i in range(ends)]),
                cells,
                lax.ppermute(head, axis, [((i + 1) % count, i) for i in range(ends)]),
            ],
            axis=dim,
        )
    return cells


def conv_taps(padded, kernel, positions):
    result = None
    for tap_index in range(kernel.shape[0]):
        window = padded[:, tap_index : tap_index + positions]
        product = jnp.einsum(
            "slc,co->slo", window, kernel[tap_index], preferred_element_type=jnp.float32
        )
        result = product if result is None else result + product
    return result


def online_step(carry, query_rows, key_block, value_block):
    best, weight_sum, accum = carry
    scores = jnp.einsum(
        "sqhk,sjhk->shqj", query_rows, key_block, preferred_element_type=jnp.float32
    )
    newest = jnp.maximum(best, jnp.max(scores, axis=-1))
    fade = jnp.exp(best - newest)
    weights = jnp.exp(scores - newest[..., None])
    weight_sum = weight_sum * fade + jnp.sum(weights, axis=-1)
    accum = accum * fade[..., None] + jnp.einsum(
        "shqj,sjhv->shqv",
        weights.astype(jnp.bfloat16),
        value_block,
        preferred_element_type=jnp.float32,
    )
    return (newest, weight_sum, accum)


def blocked_attend(carry, query_rows, key_piece, value_piece):
    rows = key_piece.shape[1]
    block = min(rows, 512)
    for first in range(0, rows, block):
        carry = online_step(
            carry,
            query_rows,
            key_piece[:, first : first + block],
            value_piece[:, first : first + block],
        )
    return carry


def empty_state(seqs_here, heads_here, rows):
    return (
        jnp.full((seqs_here, heads_here, rows), -jnp.inf, jnp.float32),
        jnp.zeros((seqs_here, heads_here, rows), jnp.float32),
        jnp.zeros((seqs_here, heads_here, rows, VAL), jnp.float32),
    )


def on_device(
    sequence_input, bn_gain, bn_bias, conv_weight, conv_bias, ln_gain, ln_bias, qkv_weight
):
    seqs_here = sequence_input.shape[0]
    positions = sequence_input.shape[1]
    channels = sequence_input.shape[2]
    values_in = sequence_input.astype(jnp.float32)
    total, squares = lax.psum(
        (jnp.sum(values_in, axis=(0, 1)), jnp.sum(values_in * values_in, axis=(0, 1))),
        ("batch", "seq"),
    )
    count = float(seqs_here * positions * lax.axis_size("batch") * lax.axis_size("seq"))
    mean = total / count
    var = squares / count - mean * mean
    activated = jax.nn.gelu(
        (values_in - mean) * lax.rsqrt(var + epsilon) * bn_gain + bn_bias, approximate=True
    ).astype(jnp.bfloat16)
    padded = extended(activated, (("seq", 1),), 2)
    conv_out = conv_taps(
        padded, lax.all_gather(conv_weight, "batch", axis=2, tiled=True), positions
    )
    conv_out = conv_out + conv_bias
    bins_here = positions // 2
    pooled = conv_out.reshape(seqs_here, bins_here, 2, channels).max(axis=2).astype(jnp.bfloat16)
    pooled_wide = pooled.astype(jnp.float32)
    centre = jnp.mean(pooled_wide, axis=-1, keepdims=True)
    spread = jnp.mean((pooled_wide - centre) ** 2, axis=-1, keepdims=True)
    normed = ((pooled_wide - centre) * lax.rsqrt(spread + epsilon) * ln_gain + ln_bias).astype(
        jnp.bfloat16
    )
    proj = jnp.einsum(
        "sbd,dk->sbk",
        normed,
        lax.all_gather(qkv_weight, "batch", axis=1, tiled=True),
        preferred_element_type=jnp.float32,
    )
    head_keys = HEADS * KEY
    queries = (proj[..., :head_keys] * KEY ** (-0.5)).astype(jnp.bfloat16)
    key_rows = proj[..., head_keys : 2 * head_keys].astype(jnp.bfloat16)
    value_rows = proj[..., 2 * head_keys :].astype(jnp.bfloat16)
    query_heads = queries.reshape(seqs_here, bins_here, HEADS, KEY)
    key_piece = lax.all_gather(key_rows, "seq", axis=1, tiled=True)
    value_piece = lax.all_gather(value_rows, "seq", axis=1, tiled=True)
    width_now = key_piece.shape[1]
    best, weight_sum, accum = blocked_attend(
        empty_state(seqs_here, HEADS, bins_here),
        query_heads,
        key_piece.reshape(seqs_here, width_now, HEADS, KEY),
        value_piece.reshape(seqs_here, width_now, HEADS, VAL),
    )
    attended = (
        (accum / weight_sum[..., None])
        .transpose(0, 2, 1, 3)
        .reshape(seqs_here, bins_here, HEADS * VAL)
        .astype(jnp.bfloat16)
    )
    return (pooled, attended)


LINES = 4
PLANES = 2
RUNS = 4
TAPS = 5
CHUNKS = 4
UNIT = 32
MESH = pl.DeviceIdType.MESH
GELU_IN = 0.7978845608028654


def unit_of(slot, s):
    quarter = HEADS * KEY // RUNS // UNIT
    values = HEADS * VAL // RUNS // UNIT
    if slot < quarter:
        return quarter * s + slot
    if slot < 2 * quarter:
        return RUNS * quarter + quarter * s + slot - quarter
    return 2 * RUNS * quarter + values * s + slot - 2 * quarter


def fused_kernel(
    x_ref,
    gain_ref,
    bias_ref,
    piece_ref,
    conv_bias_ref,
    ln_gain_ref,
    ln_bias_ref,
    units_ref,
    pooled_ref,
    attended_ref,
    x_all,
    sums_seq,
    sums_batch,
    act,
    act_wide,
    even_rows,
    odd_rows,
    pieces,
    units,
    pool_wide,
    pool_all,
    wide,
    normed,
    q_rows,
    k_rows,
    v_rows,
    att_out,
    att_in,
    own_sem,
    x_send,
    x_recv,
    ss_send,
    ss_recv,
    sb_send,
    sb_recv,
    c_send,
    f_send,
    c_recv,
    u_send,
    u_recv,
    p_send,
    p_recv,
    a_send,
    a_recv,
):
    b = lax.axis_index("batch")
    s = lax.axis_index("seq")
    z, y = b // PLANES, b % PLANES
    positions, channels = x_ref.shape
    bins = positions // 2
    rows = RUNS * bins
    n_batch = LINES * PLANES
    share = channels // RUNS
    part = share // n_batch
    share_in = channels // n_batch
    count = float(n_batch * RUNS * bins * 2)
    n_units = units.shape[0]
    per_shard = units_ref.shape[0]

    sibling = s + 1 - 2 * (s % 2)
    across = (s + 2) % RUNS
    diagonal = (sibling + 2) % RUNS
    mate = z * PLANES + 1 - y

    def remote(src, dst, send, recv, to_b, to_s):
        return pltpu.make_async_remote_copy(
            src_ref=src,
            dst_ref=dst,
            send_sem=send,
            recv_sem=recv,
            device_id=(to_b, to_s),
            device_id_type=MESH,
        )

    barrier = pltpu.get_barrier_semaphore()
    for step in range(1, RUNS):
        pl.semaphore_signal(barrier, inc=1, device_id=(b, (s + step) % RUNS), device_id_type=MESH)
    for step in range(1, n_batch):
        pl.semaphore_signal(
            barrier, inc=1, device_id=((b + step) % n_batch, s), device_id_type=MESH
        )


    def add_rows(i, carry):
        total, squares = carry
        block = x_ref[pl.ds(pl.multiple_of(i * 16, 16), 16), :].astype(jnp.float32)
        return (
            total + jnp.sum(block, axis=0, keepdims=True),
            squares + jnp.sum(block * block, axis=0, keepdims=True),
        )

    nothing = jnp.zeros((1, channels), jnp.float32)
    total, squares = lax.fori_loop(0, positions // 16, add_rows, (nothing, nothing))
    sums_seq[s, 0:1, :] = total
    sums_seq[s, 1:2, :] = squares

    pl.semaphore_wait(barrier, RUNS - 1 + n_batch - 1)

    started = []

    def go(copy):
        copy.start()
        started.append(copy)

    for step in range(1, RUNS):
        go(
            remote(
                sums_seq.at[s],
                sums_seq.at[s],
                ss_send.at[step],
                ss_recv.at[s],
                b,
                (s + step) % RUNS,
            )
        )
    depth = piece_ref.shape[0] // CHUNKS

    def chunk(ref, c):
        return ref.at[pl.ds(c * depth, depth), :]

    def push_chunk(c):
        mine = chunk(piece_ref, c)
        for step in range(1, LINES):
            to = ((z + step) % LINES) * PLANES + y
            go(remote(mine, chunk(pieces.at[0, z], c), c_send.at[step, c], c_recv.at[0, z, c], to, s))
        go(remote(mine, chunk(pieces.at[1, z], c), c_send.at[0, c], c_recv.at[1, z, c], mate, s))

    push_chunk(0)
    go(remote(x_ref, x_all.at[s], x_send.at[0], x_recv.at[s], b, across))
    go(remote(x_ref, x_all.at[s], x_send.at[1], x_recv.at[s], b, sibling))
    for c in range(1, CHUNKS):
        push_chunk(c)
    own_x = pltpu.make_async_copy(x_ref, x_all.at[s], own_sem.at[0])
    own_x.start()
    own_piece = pltpu.make_async_copy(piece_ref, pieces.at[0, z], own_sem.at[1])
    own_piece.start()

    def arrived(dst, sem):
        pltpu.make_async_copy(dst, dst, sem).wait()

    for step in range(1, RUNS):
        other = (s + step) % RUNS
        arrived(sums_seq.at[other], ss_recv.at[other])
    sums_batch[b] = (sums_seq[0] + sums_seq[1]) + (sums_seq[2] + sums_seq[3])
    for step in range(1, n_batch):
        go(
            remote(
                sums_batch.at[b],
                sums_batch.at[b],
                sb_send.at[step],
                sb_recv.at[b],
                (b + step) % n_batch,
                s,
            )
        )

    def forward_chunk(c):
        for step in (1, 3, 2):
            line = (z + step) % LINES
            here = chunk(pieces.at[0, line], c)
            arrived(here, c_recv.at[0, line, c])
            go(
                remote(
                    here,
                    chunk(pieces.at[1, line], c),
                    f_send.at[step, c],
                    c_recv.at[1, line, c],
                    mate,
                    s,
                )
            )

    forward_chunk(0)
    for step in range(1, n_batch):
        other = (b + step) % n_batch
        arrived(sums_batch.at[other], sb_recv.at[other])
    sums = jnp.zeros((2, channels), jnp.float32)
    for i in range(n_batch):
        sums = sums + sums_batch[i]
    mean = sums[0:1] / count
    var = sums[1:2] / count - mean * mean
    scale = lax.rsqrt(var + epsilon) * gain_ref[...]
    shift = bias_ref[...]

    def activate(run):
        def body(i, _):
            first = pl.multiple_of(i * 32, 32)
            v = x_all[run, pl.ds(first, 32), :].astype(jnp.float32)
            v = (v - mean) * scale + shift
            g = 0.5 * v * (1.0 + jnp.tanh(GELU_IN * (v + 0.044715 * (v * v * v))))
            at = pl.ds(pl.multiple_of(run * bins + i * 16, 16), 16)
            for j in range(channels // 128):
                lanes = slice(j * 128, j * 128 + 128)
                act_wide[j, pl.ds(first, 32), :] = g[:, lanes]
                even = act_wide[j, pl.ds(first, 16, stride=2), :]
                odd = act_wide[j, pl.ds(first + 1, 16, stride=2), :]
                act[at, lanes] = even.astype(jnp.bfloat16)
                act[at, channels + j * 128 : channels + j * 128 + 128] = odd.astype(jnp.bfloat16)
            return 0

        lax.fori_loop(0, bins // 16, body, 0)

    own_x.wait()
    activate(s)
    forward_chunk(1)
    arrived(x_all.at[sibling], x_recv.at[sibling])
    activate(sibling)
    arrived(x_all.at[across], x_recv.at[across])
    go(
        remote(
            x_all.at[across], x_all.at[across], x_send.at[2], x_recv.at[across], b, sibling
        )
    )
    forward_chunk(2)
    activate(across)
    forward_chunk(3)

    for slot in range(n_units):
        unit = unit_of(slot, s)
        holder = unit // per_shard

        @pl.when(holder == b)
        def _(slot=slot, unit=unit):
            mine = units_ref.at[unit - per_shard * b]
            for step in range(1, LINES):
                to = ((z + step) % LINES) * PLANES + y
                remote(
                    mine, units.at[slot], u_send.at[slot, step], u_recv.at[slot], to, s
                ).start()
            remote(mine, units.at[slot], u_send.at[slot, 0], u_recv.at[slot], mate, s).start()
            pltpu.make_async_copy(mine, units.at[slot], u_recv.at[slot]).start()

    arrived(x_all.at[diagonal], x_recv.at[diagonal])
    activate(diagonal)

    def back(v):
        lane = lax.broadcasted_iota(jnp.int32, v.shape, 1)
        return jnp.where(lane == 0, 0.0, pltpu.roll(v, 1, 1))

    def ahead(v):
        lane = lax.broadcasted_iota(jnp.int32, v.shape, 1)
        return jnp.where(lane == rows - 1, 0.0, pltpu.roll(v, rows - 1, 1))

    contract_last = (((1,), (1,)), ((), ()))

    padded = piece_ref.shape[0]

    def convolve(half):
        stack = pieces[half].reshape(LINES * padded, channels)
        even_rows[...] = lax.dot_general(
            stack, act[:, :channels], contract_last, preferred_element_type=jnp.float32
        )
        odd_rows[...] = lax.dot_general(
            stack, act[:, channels:], contract_last, preferred_element_type=jnp.float32
        )

        def combine(line, _):
            taps = [
                pl.ds(pl.multiple_of(line * padded + t * part, 8), part) for t in range(TAPS)
            ]
            e = [even_rows[tap, :] for tap in taps]
            o = [odd_rows[tap, :] for tap in taps]
            first = back(e[0] + o[1]) + e[2] + o[3] + ahead(e[4])
            second = back(o[0]) + e[1] + o[2] + ahead(e[3] + o[4])
            source = line * PLANES + (y if half == 0 else 1 - y)
            at = pl.multiple_of(source * share_in + s * part, 8)
            offset = conv_bias_ref[pl.ds(at, part), :]
            pool_wide[pl.ds(pl.multiple_of(line * part, 8), part), :] = (
                jnp.maximum(first, second) + offset
            )
            return 0

        lax.fori_loop(0, LINES, combine, 0)
        pool_all[s, half] = pool_wide[...].astype(jnp.bfloat16)
        mine = pool_all.at[s, half]
        go(remote(mine, mine, p_send.at[half, 0], p_recv.at[half, s], b, across))
        go(remote(mine, mine, p_send.at[half, 1], p_recv.at[half, s], b, sibling))

    def pass_on(half):
        theirs = pool_all.at[across, half]
        arrived(theirs, p_recv.at[half, across])
        go(remote(theirs, theirs, p_send.at[half, 2], p_recv.at[half, across], b, sibling))

    def in_order(run, half):
        block = pool_all[run, half].astype(jnp.float32)
        for line in range(LINES):
            source = line * PLANES + (y if half == 0 else 1 - y)
            at = pl.multiple_of(source * share_in + run * part, 8)
            wide[pl.ds(at, part), :] = block[line * part : (line + 1) * part]

    own_piece.wait()
    convolve(0)
    pass_on(0)
    in_order(s, 0)
    in_order(across, 0)
    for run in (sibling, diagonal):
        arrived(pool_all.at[run, 0], p_recv.at[0, run])
        in_order(run, 0)
    for c in range(CHUNKS):
        for line in range(LINES):
            arrived(chunk(pieces.at[1, line], c), c_recv.at[1, line, c])
    convolve(1)

    for slot in range(n_units):
        holder = unit_of(slot, s) // per_shard

        @pl.when(jnp.logical_and(holder != b, holder % PLANES == y))
        def _(slot=slot):
            arrived(units.at[slot], u_recv.at[slot])
            remote(
                units.at[slot], units.at[slot], u_send.at[slot, 0], u_recv.at[slot], mate, s
            ).start()

    in_order(s, 1)
    pass_on(1)
    in_order(across, 1)
    for run in (sibling, diagonal):
        arrived(pool_all.at[run, 1], p_recv.at[1, run])
        in_order(run, 1)

    def norm(j, _):
        lanes = pl.ds(pl.multiple_of(j * bins, 128), bins)
        block = wide[:, lanes]
        centre = jnp.sum(block, axis=0, keepdims=True) / channels
        away = block - centre
        spread = jnp.sum(away * away, axis=0, keepdims=True) / channels
        normed[:, lanes] = (
            away * lax.rsqrt(spread + epsilon) * ln_gain_ref[...] + ln_bias_ref[...]
        ).astype(jnp.bfloat16)
        return 0

    lax.fori_loop(0, RUNS, norm, 0)
    lanes = pl.ds(pl.multiple_of(s * bins, 128), bins)
    pooled_ref[...] = jnp.transpose(wide[:, lanes]).astype(jnp.bfloat16)

    for slot in range(n_units):
        holder = unit_of(slot, s) // per_shard

        @pl.when(jnp.logical_or(holder == b, holder % PLANES != y))
        def _(slot=slot):
            arrived(units.at[slot], u_recv.at[slot])

    here = HEADS // RUNS
    keys = here * KEY
    n_keys = keys // UNIT
    normed_now = normed[...]
    wq = units[0:n_keys].reshape(keys, channels)
    q_rows[...] = (
        jnp.dot(wq, normed_now, preferred_element_type=jnp.float32) * KEY ** (-0.5)
    ).astype(jnp.bfloat16)
    wk = units[n_keys : 2 * n_keys].reshape(keys, channels)
    k_rows[...] = jnp.transpose(
        jnp.dot(wk, normed_now, preferred_element_type=jnp.float32)
    ).astype(jnp.bfloat16)
    wv = units[2 * n_keys :].reshape(here * VAL, channels)
    v_rows[...] = jnp.dot(wv, normed_now, preferred_element_type=jnp.float32).astype(jnp.bfloat16)

    def attend(run):
        lanes = pl.ds(pl.multiple_of(run * bins, 128), bins)
        q_now = q_rows[:, lanes]
        row = lax.broadcasted_iota(jnp.int32, q_now.shape, 0)
        for h in range(here):
            q_head = jnp.where(row // KEY == h, q_now, jnp.zeros_like(q_now))
            scores = jnp.dot(k_rows[...], q_head, preferred_element_type=jnp.float32)
            weights = jnp.exp(scores - jnp.max(scores, axis=0, keepdims=True))
            below = jnp.sum(weights, axis=0, keepdims=True)
            above = jnp.dot(
                v_rows[h * VAL : (h + 1) * VAL, :],
                weights.astype(jnp.bfloat16),
                preferred_element_type=jnp.float32,
            )
            att_out[run, h * VAL : (h + 1) * VAL, :] = (above / below).astype(jnp.bfloat16)

    for run, k in ((across, 0), (diagonal, 1), (sibling, 2)):
        attend(run)
        go(remote(att_out.at[run], att_in.at[s], a_send.at[k], a_recv.at[s], b, run))
    attend(s)
    att_in[s] = att_out[s]
    for run in (across, diagonal, sibling):
        arrived(att_in.at[run], a_recv.at[run])
    gathered = jnp.concatenate([att_in[r].astype(jnp.float32) for r in range(RUNS)], axis=0)
    attended_ref[...] = jnp.transpose(gathered).astype(jnp.bfloat16)

    for copy in started:
        copy.wait_send()
    for slot in range(n_units):
        holder = unit_of(slot, s) // per_shard

        @pl.when(holder % PLANES == y)
        def _(slot=slot):
            remote(
                units.at[slot], units.at[slot], u_send.at[slot, 0], u_recv.at[slot], mate, s
            ).wait_send()

        @pl.when(holder == b)
        def _(slot=slot):
            for step in range(1, LINES):
                to = ((z + step) % LINES) * PLANES + y
                remote(
                    units.at[slot], units.at[slot], u_send.at[slot, step], u_recv.at[slot], to, s
                ).wait_send()


def fused_on_device(
    sequence_input, bn_gain, bn_bias, conv_weight, conv_bias, ln_gain, ln_bias, qkv_weight
):
    _, positions, channels = sequence_input.shape
    bins = positions // 2
    rows = RUNS * bins
    n_batch = LINES * PLANES
    share = channels // RUNS
    part = share // n_batch
    s = lax.axis_index("seq")
    taps = conv_weight.shape[0]
    x = sequence_input.reshape(positions, channels)
    piece = lax.dynamic_slice_in_dim(conv_weight, s * part, part, axis=2)
    piece = piece.transpose(0, 2, 1).reshape(taps * part, channels)
    padded = -(-taps * part // 16) * 16
    piece = jnp.pad(piece, ((0, padded - taps * part), (0, 0)))

    per_shard = qkv_weight.shape[1] // UNIT
    units = qkv_weight.T.reshape(per_shard, UNIT, channels)
    n_units = per_shard * n_batch // RUNS
    keys = HEADS * KEY // RUNS
    vals = HEADS * VAL // RUNS
    bf16, f32 = jnp.bfloat16, jnp.float32
    dma = pltpu.SemaphoreType.DMA
    pooled, attended = pl.pallas_call(
        fused_kernel,
        out_shape=(
            jax.ShapeDtypeStruct((bins, channels), bf16),
            jax.ShapeDtypeStruct((bins, channels), bf16),
        ),
        in_specs=[pl.BlockSpec(memory_space=pltpu.VMEM)] * 8,
        out_specs=(pl.BlockSpec(memory_space=pltpu.VMEM),) * 2,
        scratch_shapes=[
            pltpu.VMEM((RUNS, positions, channels), bf16),
            pltpu.VMEM((RUNS, 2, channels), f32),
            pltpu.VMEM((n_batch, 2, channels), f32),
            pltpu.VMEM((rows, 2 * channels), bf16),
            pltpu.VMEM((channels // 128, positions, 128), f32),
            pltpu.VMEM((LINES * padded, rows), f32),
            pltpu.VMEM((LINES * padded, rows), f32),
            pltpu.VMEM((PLANES, LINES, padded, channels), bf16),
            pltpu.VMEM((n_units, UNIT, channels), bf16),
            pltpu.VMEM((share // PLANES, rows), f32),
            pltpu.VMEM((RUNS, PLANES, share // PLANES, rows), bf16),
            pltpu.VMEM((channels, rows), f32),
            pltpu.VMEM((channels, rows), bf16),
            pltpu.VMEM((keys, rows), bf16),
            pltpu.VMEM((rows, keys), bf16),
            pltpu.VMEM((vals, rows), bf16),
            pltpu.VMEM((RUNS, vals, bins), bf16),
            pltpu.VMEM((RUNS, vals, bins), bf16),
            dma((2,)),
            dma((3,)),
            dma((RUNS,)),
            dma((RUNS,)),
            dma((RUNS,)),
            dma((n_batch,)),
            dma((n_batch,)),
            dma((LINES, CHUNKS)),
            dma((LINES, CHUNKS)),
            dma((PLANES, LINES, CHUNKS)),
            dma((n_units, LINES)),
            dma((n_units,)),
            dma((PLANES, 3)),
            dma((PLANES, RUNS)),
            dma((3,)),
            dma((RUNS,)),
        ],
        compiler_params=pltpu.CompilerParams(
            collective_id=0, has_side_effects=True, vmem_limit_bytes=48 * 1024 * 1024
        ),
    )(
        x,
        bn_gain.reshape(1, channels),
        bn_bias.reshape(1, channels),
        piece,
        conv_bias.reshape(channels, 1),
        ln_gain.reshape(channels, 1),
        ln_bias.reshape(channels, 1),
        units,
    )
    return (pooled[None], attended[None])


def solution(mesh):
    placed = (
        P("batch", "seq", None),
        P(),
        P(),
        P(None, None, "batch"),
        P(),
        P(),
        P(),
        P(None, "batch"),
    )
    fused = mesh.shape["batch"] == LINES * PLANES and mesh.shape["seq"] == RUNS
    return jax.shard_map(
        fused_on_device if fused else on_device,
        mesh=mesh,
        in_specs=placed,
        out_specs=(P("batch", "seq", None), P("batch", "seq", None)),
        check_vma=False,
    )
```

```python
import jax
import jax.numpy as jnp
from jax import lax
from jax.experimental import pallas as pl
from jax.experimental.pallas import tpu as pltpu
from jax.sharding import PartitionSpec as P

HEADS = 8
KEY = 64
VAL = 96


epsilon = 1e-05


def extended(cells, sides, width):
    for axis, dim in sides:
        count = lax.axis_size(axis)
        ends = count - 1
        head = lax.slice_in_dim(cells, 0, width, axis=dim)
        tail = lax.slice_in_dim(cells, cells.shape[dim] - width, cells.shape[dim], axis=dim)
        cells = jnp.concatenate(
            [
                lax.ppermute(tail, axis, [(i, (i + 1) % count) for i in range(ends)]),
                cells,
                lax.ppermute(head, axis, [((i + 1) % count, i) for i in range(ends)]),
            ],
            axis=dim,
        )
    return cells


def conv_taps(padded, kernel, positions):
    result = None
    for tap_index in range(kernel.shape[0]):
        window = padded[:, tap_index : tap_index + positions]
        product = jnp.einsum(
            "slc,co->slo", window, kernel[tap_index], preferred_element_type=jnp.float32
        )
        result = product if result is None else result + product
    return result


def online_step(carry, query_rows, key_block, value_block):
    best, weight_sum, accum = carry
    scores = jnp.einsum(
        "sqhk,sjhk->shqj", query_rows, key_block, preferred_element_type=jnp.float32
    )
    newest = jnp.maximum(best, jnp.max(scores, axis=-1))
    fade = jnp.exp(best - newest)
    weights = jnp.exp(scores - newest[..., None])
    weight_sum = weight_sum * fade + jnp.sum(weights, axis=-1)
    accum = accum * fade[..., None] + jnp.einsum(
        "shqj,sjhv->shqv",
        weights.astype(jnp.bfloat16),
        value_block,
        preferred_element_type=jnp.float32,
    )
    return (newest, weight_sum, accum)


def blocked_attend(carry, query_rows, key_piece, value_piece):
    rows = key_piece.shape[1]
    block = min(rows, 512)
    for first in range(0, rows, block):
        carry = online_step(
            carry,
            query_rows,
            key_piece[:, first : first + block],
            value_piece[:, first : first + block],
        )
    return carry


def empty_state(seqs_here, heads_here, rows):
    return (
        jnp.full((seqs_here, heads_here, rows), -jnp.inf, jnp.float32),
        jnp.zeros((seqs_here, heads_here, rows), jnp.float32),
        jnp.zeros((seqs_here, heads_here, rows, VAL), jnp.float32),
    )


def on_device(
    sequence_input, bn_gain, bn_bias, conv_weight, conv_bias, ln_gain, ln_bias, qkv_weight
):
    seqs_here = sequence_input.shape[0]
    positions = sequence_input.shape[1]
    channels = sequence_input.shape[2]
    values_in = sequence_input.astype(jnp.float32)
    total, squares = lax.psum(
        (jnp.sum(values_in, axis=(0, 1)), jnp.sum(values_in * values_in, axis=(0, 1))),
        ("batch", "seq"),
    )
    count = float(seqs_here * positions * lax.axis_size("batch") * lax.axis_size("seq"))
    mean = total / count
    var = squares / count - mean * mean
    activated = jax.nn.gelu(
        (values_in - mean) * lax.rsqrt(var + epsilon) * bn_gain + bn_bias, approximate=True
    ).astype(jnp.bfloat16)
    padded = extended(activated, (("seq", 1),), 2)
    conv_out = conv_taps(
        padded, lax.all_gather(conv_weight, "batch", axis=2, tiled=True), positions
    )
    conv_out = conv_out + conv_bias
    bins_here = positions // 2
    pooled = conv_out.reshape(seqs_here, bins_here, 2, channels).max(axis=2).astype(jnp.bfloat16)
    pooled_wide = pooled.astype(jnp.float32)
    centre = jnp.mean(pooled_wide, axis=-1, keepdims=True)
    spread = jnp.mean((pooled_wide - centre) ** 2, axis=-1, keepdims=True)
    normed = ((pooled_wide - centre) * lax.rsqrt(spread + epsilon) * ln_gain + ln_bias).astype(
        jnp.bfloat16
    )
    proj = jnp.einsum(
        "sbd,dk->sbk",
        normed,
        lax.all_gather(qkv_weight, "batch", axis=1, tiled=True),
        preferred_element_type=jnp.float32,
    )
    head_keys = HEADS * KEY
    queries = (proj[..., :head_keys] * KEY ** (-0.5)).astype(jnp.bfloat16)
    key_rows = proj[..., head_keys : 2 * head_keys].astype(jnp.bfloat16)
    value_rows = proj[..., 2 * head_keys :].astype(jnp.bfloat16)
    query_heads = queries.reshape(seqs_here, bins_here, HEADS, KEY)
    key_piece = lax.all_gather(key_rows, "seq", axis=1, tiled=True)
    value_piece = lax.all_gather(value_rows, "seq", axis=1, tiled=True)
    width_now = key_piece.shape[1]
    best, weight_sum, accum = blocked_attend(
        empty_state(seqs_here, HEADS, bins_here),
        query_heads,
        key_piece.reshape(seqs_here, width_now, HEADS, KEY),
        value_piece.reshape(seqs_here, width_now, HEADS, VAL),
    )
    attended = (
        (accum / weight_sum[..., None])
        .transpose(0, 2, 1, 3)
        .reshape(seqs_here, bins_here, HEADS * VAL)
        .astype(jnp.bfloat16)
    )
    return (pooled, attended)


LINES = 4
PLANES = 2
RUNS = 4
TAPS = 5
CHUNKS = 4
UNIT = 32
MESH = pl.DeviceIdType.MESH
GELU_IN = 0.7978845608028654


def unit_of(slot, s):
    quarter = HEADS * KEY // RUNS // UNIT
    values = HEADS * VAL // RUNS // UNIT
    if slot < quarter:
        return quarter * s + slot
    if slot < 2 * quarter:
        return RUNS * quarter + quarter * s + slot - quarter
    return 2 * RUNS * quarter + values * s + slot - 2 * quarter


def fused_kernel(
    x_ref,
    gain_ref,
    bias_ref,
    conv_bias_ref,
    ln_gain_ref,
    ln_bias_ref,
    piece_ref,
    units_ref,
    pooled_ref,
    attended_ref,
    x_all,
    sums_seq,
    sums_batch,
    vector_0,
    vector_1,
    vector_2,
    vector_3,
    vector_4,
    columns,
    act,
    act_wide,
    even_rows,
    odd_rows,
    pieces,
    units,
    pool_wide,
    pool_all,
    wide,
    normed,
    q_rows,
    k_rows,
    v_rows,
    att_out,
    att_in,
    own_sem,
    x_send,
    x_recv,
    ss_send,
    ss_recv,
    sb_send,
    sb_recv,
    c_send,
    f_send,
    r_send,
    c_recv,
    u_send,
    u_recv,
    p_send,
    p_recv,
    a_send,
    a_recv,
):
    b = lax.axis_index("batch")
    s = lax.axis_index("seq")
    z, y = b // PLANES, b % PLANES
    positions, channels = x_ref.shape
    bins = positions // 2
    rows = RUNS * bins
    n_batch = LINES * PLANES
    share = channels // RUNS
    part = share // n_batch
    share_in = channels // n_batch
    count = float(n_batch * RUNS * bins * 2)
    n_units = units.shape[0]
    per_shard = units_ref.shape[0]

    sibling = s + 1 - 2 * (s % 2)
    across = (s + 2) % RUNS
    diagonal = (sibling + 2) % RUNS
    mate = z * PLANES + 1 - y
    partner = z + 1 - 2 * (z % 2)
    inner = jnp.logical_or(z == 1, z == 2)
    gateway = jnp.where(z < 2, 2, 1)
    beyond = 3 - 3 * (z // 2)

    def remote(src, dst, send, recv, to_b, to_s):
        return pltpu.make_async_remote_copy(
            src_ref=src,
            dst_ref=dst,
            send_sem=send,
            recv_sem=recv,
            device_id=(to_b, to_s),
            device_id_type=MESH,
        )

    own_x = pltpu.make_async_copy(x_ref, x_all.at[s], own_sem.at[0])
    own_x.start()
    vectors = (vector_0, vector_1, vector_2, vector_3, vector_4)
    given = (gain_ref, bias_ref, conv_bias_ref, ln_gain_ref, ln_bias_ref)
    fetched = [
        pltpu.make_async_copy(ref, vectors[i], own_sem.at[2 + i])
        for i, ref in enumerate(given)
    ]
    for copy in fetched:
        copy.start()
    barrier = pltpu.get_barrier_semaphore()
    for step in range(1, RUNS):
        pl.semaphore_signal(barrier, inc=1, device_id=(b, (s + step) % RUNS), device_id_type=MESH)
    for step in range(1, n_batch):
        pl.semaphore_signal(
            barrier, inc=1, device_id=((b + step) % n_batch, s), device_id_type=MESH
        )


    def add_rows(i, carry):
        total, squares = carry
        block = x_all[s, pl.ds(pl.multiple_of(i * 16, 16), 16), :].astype(jnp.float32)
        return (
            total + jnp.sum(block, axis=0, keepdims=True),
            squares + jnp.sum(block * block, axis=0, keepdims=True),
        )

    own_x.wait()
    nothing = jnp.zeros((1, channels), jnp.float32)
    total, squares = lax.fori_loop(0, positions // 16, add_rows, (nothing, nothing))
    sums_seq[s, 0:1, :] = total
    sums_seq[s, 1:2, :] = squares

    pl.semaphore_wait(barrier, RUNS - 1 + n_batch - 1)

    started = []

    def go(copy):
        copy.start()
        started.append(copy)

    for step in range(1, RUNS):
        go(
            remote(
                sums_seq.at[s],
                sums_seq.at[s],
                ss_send.at[step],
                ss_recv.at[s],
                b,
                (s + step) % RUNS,
            )
        )
    depth = piece_ref.shape[0] // CHUNKS

    def chunk(ref, c):
        return ref.at[pl.ds(c * depth, depth), :]

    def push_chunk(c):
        mine = chunk(piece_ref, c)
        for at, line in ((0, partner), (1, gateway)):
            to = line * PLANES + y
            go(remote(mine, chunk(pieces.at[0, z], c), c_send.at[at, c], c_recv.at[0, z, c], to, s))
        go(remote(mine, chunk(pieces.at[1, z], c), c_send.at[2, c], c_recv.at[1, z, c], mate, s))

    push_chunk(0)
    go(remote(x_all.at[s], x_all.at[s], x_send.at[0], x_recv.at[s], b, across))
    go(remote(x_all.at[s], x_all.at[s], x_send.at[1], x_recv.at[s], b, sibling))
    for c in range(1, CHUNKS):
        push_chunk(c)
    own_piece = pltpu.make_async_copy(piece_ref, pieces.at[0, z], own_sem.at[1])
    own_piece.start()

    def arrived(dst, sem):
        pltpu.make_async_copy(dst, dst, sem).wait()

    for step in range(1, RUNS):
        other = (s + step) % RUNS
        arrived(sums_seq.at[other], ss_recv.at[other])
    sums_batch[b] = (sums_seq[0] + sums_seq[1]) + (sums_seq[2] + sums_seq[3])
    for step in range(1, n_batch):
        go(
            remote(
                sums_batch.at[b],
                sums_batch.at[b],
                sb_send.at[step],
                sb_recv.at[b],
                (b + step) % n_batch,
                s,
            )
        )

    def forward_chunk(c):
        for at, line in ((0, partner), (1, gateway), (2, beyond)):
            here = chunk(pieces.at[0, line], c)
            arrived(here, c_recv.at[0, line, c])
            go(
                remote(
                    here,
                    chunk(pieces.at[1, line], c),
                    f_send.at[at, c],
                    c_recv.at[1, line, c],
                    mate,
                    s,
                )
            )
            if at > 0:

                @pl.when(inner)
                def _(at=at, here=here, line=line):
                    relay(here, line, at, c).start()

    def relay(here, line, at, c):
        return remote(
            here, here, r_send.at[at - 1, c], c_recv.at[0, line, c], partner * PLANES + y, s
        )

    forward_chunk(0)
    for copy in fetched:
        copy.wait()
    spare = jnp.zeros((128 - len(given), channels), jnp.float32)
    columns[...] = jnp.transpose(
        jnp.concatenate([v[...].reshape(1, channels) for v in vectors] + [spare], axis=0)
    )
    for step in range(1, n_batch):
        other = (b + step) % n_batch
        arrived(sums_batch.at[other], sb_recv.at[other])
    sums = jnp.zeros((2, channels), jnp.float32)
    for i in range(n_batch):
        sums = sums + sums_batch[i]
    mean = sums[0:1] / count
    var = sums[1:2] / count - mean * mean
    scale = lax.rsqrt(var + epsilon) * vector_0[...].reshape(1, channels)
    shift = vector_1[...].reshape(1, channels)

    def activate(run):
        def body(i, _):
            first = pl.multiple_of(i * 32, 32)
            v = x_all[run, pl.ds(first, 32), :].astype(jnp.float32)
            v = (v - mean) * scale + shift
            g = 0.5 * v * (1.0 + jnp.tanh(GELU_IN * (v + 0.044715 * (v * v * v))))
            at = pl.ds(pl.multiple_of(run * bins + i * 16, 16), 16)
            for j in range(channels // 128):
                lanes = slice(j * 128, j * 128 + 128)
                act_wide[j, pl.ds(first, 32), :] = g[:, lanes]
                even = act_wide[j, pl.ds(first, 16, stride=2), :]
                odd = act_wide[j, pl.ds(first + 1, 16, stride=2), :]
                act[at, lanes] = even.astype(jnp.bfloat16)
                act[at, channels + j * 128 : channels + j * 128 + 128] = odd.astype(jnp.bfloat16)
            return 0

        lax.fori_loop(0, bins // 16, body, 0)

    activate(s)
    forward_chunk(1)
    arrived(x_all.at[sibling], x_recv.at[sibling])
    activate(sibling)
    arrived(x_all.at[across], x_recv.at[across])
    go(
        remote(
            x_all.at[across], x_all.at[across], x_send.at[2], x_recv.at[across], b, sibling
        )
    )
    forward_chunk(2)
    activate(across)
    forward_chunk(3)

    for slot in range(n_units):
        unit = unit_of(slot, s)
        holder = unit // per_shard

        @pl.when(holder == b)
        def _(slot=slot, unit=unit):
            mine = units_ref.at[unit - per_shard * b]
            for step in range(1, LINES):
                to = ((z + step) % LINES) * PLANES + y
                remote(
                    mine, units.at[slot], u_send.at[slot, step], u_recv.at[slot], to, s
                ).start()
            pltpu.make_async_copy(mine, units.at[slot], u_recv.at[slot]).start()

    arrived(x_all.at[diagonal], x_recv.at[diagonal])
    activate(diagonal)

    def back(v):
        lane = lax.broadcasted_iota(jnp.int32, v.shape, 1)
        return jnp.where(lane == 0, 0.0, pltpu.roll(v, 1, 1))

    def ahead(v):
        lane = lax.broadcasted_iota(jnp.int32, v.shape, 1)
        return jnp.where(lane == rows - 1, 0.0, pltpu.roll(v, rows - 1, 1))

    contract_last = (((1,), (1,)), ((), ()))

    padded = piece_ref.shape[0]

    def multiply(stack, first, count):
        for result, lanes in (
            (even_rows, slice(0, channels)),
            (odd_rows, slice(channels, 2 * channels)),
        ):
            product = lax.dot_general(
                stack, act[:, lanes], contract_last, preferred_element_type=jnp.float32
            )
            for line in range(LINES):
                at = line * padded + first
                result[at : at + count, :] = product[line * count : (line + 1) * count]

    def convolve(half):
        def combine(line, _):
            taps = [
                pl.ds(pl.multiple_of(line * padded + t * part, 8), part) for t in range(TAPS)
            ]
            e = [even_rows[tap, :] for tap in taps]
            o = [odd_rows[tap, :] for tap in taps]
            first = back(e[0] + o[1]) + e[2] + o[3] + ahead(e[4])
            second = back(o[0]) + e[1] + o[2] + ahead(e[3] + o[4])
            source = line * PLANES + (y if half == 0 else 1 - y)
            at = pl.multiple_of(source * share_in + s * part, 8)
            offset = columns[pl.ds(at, part), 2:3]
            pool_wide[pl.ds(pl.multiple_of(line * part, 8), part), :] = (
                jnp.maximum(first, second) + offset
            )
            return 0

        lax.fori_loop(0, LINES, combine, 0)
        pool_all[s, half] = pool_wide[...].astype(jnp.bfloat16)
        mine = pool_all.at[s, half]
        go(remote(mine, mine, p_send.at[half, 0], p_recv.at[half, s], b, across))
        go(remote(mine, mine, p_send.at[half, 1], p_recv.at[half, s], b, sibling))

    def pass_on(half):
        theirs = pool_all.at[across, half]
        arrived(theirs, p_recv.at[half, across])
        go(remote(theirs, theirs, p_send.at[half, 2], p_recv.at[half, across], b, sibling))

    def in_order(run, half):
        block = pool_all[run, half].astype(jnp.float32)
        for line in range(LINES):
            source = line * PLANES + (y if half == 0 else 1 - y)
            at = pl.multiple_of(source * share_in + run * part, 8)
            wide[pl.ds(at, part), :] = block[line * part : (line + 1) * part]

    own_piece.wait()
    multiply(pieces[0].reshape(LINES * padded, channels), 0, padded)
    convolve(0)
    for slot in range(n_units):
        unit = unit_of(slot, s)

        @pl.when(unit // per_shard == b)
        def _(slot=slot, unit=unit):
            mine = units_ref.at[unit - per_shard * b]
            remote(mine, units.at[slot], u_send.at[slot, 0], u_recv.at[slot], mate, s).start()

    pass_on(0)
    in_order(s, 0)
    in_order(across, 0)
    for run in (sibling, diagonal):
        arrived(pool_all.at[run, 0], p_recv.at[0, run])
        in_order(run, 0)
    for c in range(CHUNKS):
        for line in range(LINES):
            arrived(chunk(pieces.at[1, line], c), c_recv.at[1, line, c])
        part_now = pieces[1, :, c * depth : (c + 1) * depth, :].reshape(LINES * depth, channels)
        multiply(part_now, c * depth, depth)
    convolve(1)

    for slot in range(n_units):
        holder = unit_of(slot, s) // per_shard

        @pl.when(jnp.logical_and(holder != b, holder % PLANES == y))
        def _(slot=slot):
            arrived(units.at[slot], u_recv.at[slot])
            remote(
                units.at[slot], units.at[slot], u_send.at[slot, 0], u_recv.at[slot], mate, s
            ).start()

    in_order(s, 1)
    pass_on(1)
    in_order(across, 1)
    for run in (sibling, diagonal):
        arrived(pool_all.at[run, 1], p_recv.at[1, run])
        in_order(run, 1)

    def norm(j, _):
        lanes = pl.ds(pl.multiple_of(j * bins, 128), bins)
        block = wide[:, lanes]
        centre = jnp.sum(block, axis=0, keepdims=True) / channels
        away = block - centre
        spread = jnp.sum(away * away, axis=0, keepdims=True) / channels
        normed[:, lanes] = (
            away * lax.rsqrt(spread + epsilon) * columns[:, 3:4] + columns[:, 4:5]
        ).astype(jnp.bfloat16)
        return 0

    lax.fori_loop(0, RUNS, norm, 0)
    lanes = pl.ds(pl.multiple_of(s * bins, 128), bins)
    pooled_ref[...] = jnp.transpose(wide[:, lanes]).astype(jnp.bfloat16)

    for slot in range(n_units):
        holder = unit_of(slot, s) // per_shard

        @pl.when(jnp.logical_or(holder == b, holder % PLANES != y))
        def _(slot=slot):
            arrived(units.at[slot], u_recv.at[slot])

    here = HEADS // RUNS
    keys = here * KEY
    n_keys = keys // UNIT
    normed_now = normed[...]
    wq = units[0:n_keys].reshape(keys, channels)
    q_rows[...] = (
        jnp.dot(wq, normed_now, preferred_element_type=jnp.float32) * KEY ** (-0.5)
    ).astype(jnp.bfloat16)
    wk = units[n_keys : 2 * n_keys].reshape(keys, channels)
    k_rows[...] = jnp.transpose(
        jnp.dot(wk, normed_now, preferred_element_type=jnp.float32)
    ).astype(jnp.bfloat16)
    wv = units[2 * n_keys :].reshape(here * VAL, channels)
    v_rows[...] = jnp.dot(wv, normed_now, preferred_element_type=jnp.float32).astype(jnp.bfloat16)

    def attend(run):
        lanes = pl.ds(pl.multiple_of(run * bins, 128), bins)
        q_now = q_rows[:, lanes]
        row = lax.broadcasted_iota(jnp.int32, q_now.shape, 0)
        for h in range(here):
            q_head = jnp.where(row // KEY == h, q_now, jnp.zeros_like(q_now))
            scores = jnp.dot(k_rows[...], q_head, preferred_element_type=jnp.float32)
            weights = jnp.exp(scores - jnp.max(scores, axis=0, keepdims=True))
            below = jnp.sum(weights, axis=0, keepdims=True)
            above = jnp.dot(
                v_rows[h * VAL : (h + 1) * VAL, :],
                weights.astype(jnp.bfloat16),
                preferred_element_type=jnp.float32,
            )
            att_out[run, h * VAL : (h + 1) * VAL, :] = (above / below).astype(jnp.bfloat16)

    for run, k in ((across, 0), (diagonal, 1), (sibling, 2)):
        attend(run)
        go(remote(att_out.at[run], att_in.at[s], a_send.at[k], a_recv.at[s], b, run))
    attend(s)
    att_in[s] = att_out[s]
    for run in (across, diagonal, sibling):
        arrived(att_in.at[run], a_recv.at[run])
    gathered = jnp.concatenate([att_in[r].astype(jnp.float32) for r in range(RUNS)], axis=0)
    attended_ref[...] = jnp.transpose(gathered).astype(jnp.bfloat16)

    for copy in started:
        copy.wait_send()

    @pl.when(inner)
    def _():
        for c in range(CHUNKS):
            for at, line in ((1, gateway), (2, beyond)):
                relay(chunk(pieces.at[0, line], c), line, at, c).wait_send()

    for slot in range(n_units):
        holder = unit_of(slot, s) // per_shard

        @pl.when(holder % PLANES == y)
        def _(slot=slot):
            remote(
                units.at[slot], units.at[slot], u_send.at[slot, 0], u_recv.at[slot], mate, s
            ).wait_send()

        @pl.when(holder == b)
        def _(slot=slot):
            for step in range(1, LINES):
                to = ((z + step) % LINES) * PLANES + y
                remote(
                    units.at[slot], units.at[slot], u_send.at[slot, step], u_recv.at[slot], to, s
                ).wait_send()


def fused_on_device(
    sequence_input, bn_gain, bn_bias, conv_weight, conv_bias, ln_gain, ln_bias, qkv_weight
):
    _, positions, channels = sequence_input.shape
    bins = positions // 2
    rows = RUNS * bins
    n_batch = LINES * PLANES
    share = channels // RUNS
    part = share // n_batch
    s = lax.axis_index("seq")
    taps = conv_weight.shape[0]
    x = sequence_input.reshape(positions, channels)
    piece = lax.dynamic_slice_in_dim(conv_weight, s * part, part, axis=2)
    piece = piece.transpose(0, 2, 1).reshape(taps * part, channels)
    padded = -(-taps * part // 16) * 16
    piece = jnp.pad(piece, ((0, padded - taps * part), (0, 0)))

    per_shard = qkv_weight.shape[1] // UNIT
    units = qkv_weight.T.reshape(per_shard, UNIT, channels)
    n_units = per_shard * n_batch // RUNS
    keys = HEADS * KEY // RUNS
    vals = HEADS * VAL // RUNS
    bf16, f32 = jnp.bfloat16, jnp.float32
    dma = pltpu.SemaphoreType.DMA
    pooled, attended = pl.pallas_call(
        fused_kernel,
        out_shape=(
            jax.ShapeDtypeStruct((bins, channels), bf16),
            jax.ShapeDtypeStruct((bins, channels), bf16),
        ),
        in_specs=[
            *[pl.BlockSpec(memory_space=pltpu.HBM)] * 6,
            pl.BlockSpec(memory_space=pltpu.VMEM),
            pl.BlockSpec(memory_space=pltpu.HBM),
        ],
        out_specs=(pl.BlockSpec(memory_space=pltpu.VMEM),) * 2,
        scratch_shapes=[
            pltpu.VMEM((RUNS, positions, channels), bf16),
            pltpu.VMEM((RUNS, 2, channels), f32),
            pltpu.VMEM((n_batch, 2, channels), f32),
            *[pltpu.VMEM((channels,), f32)] * 5,
            pltpu.VMEM((channels, 128), f32),
            pltpu.VMEM((rows, 2 * channels), bf16),
            pltpu.VMEM((channels // 128, positions, 128), f32),
            pltpu.VMEM((LINES * padded, rows), f32),
            pltpu.VMEM((LINES * padded, rows), f32),
            pltpu.VMEM((PLANES, LINES, padded, channels), bf16),
            pltpu.VMEM((n_units, UNIT, channels), bf16),
            pltpu.VMEM((share // PLANES, rows), f32),
            pltpu.VMEM((RUNS, PLANES, share // PLANES, rows), bf16),
            pltpu.VMEM((channels, rows), f32),
            pltpu.VMEM((channels, rows), bf16),
            pltpu.VMEM((keys, rows), bf16),
            pltpu.VMEM((rows, keys), bf16),
            pltpu.VMEM((vals, rows), bf16),
            pltpu.VMEM((RUNS, vals, bins), bf16),
            pltpu.VMEM((RUNS, vals, bins), bf16),
            dma((7,)),
            dma((3,)),
            dma((RUNS,)),
            dma((RUNS,)),
            dma((RUNS,)),
            dma((n_batch,)),
            dma((n_batch,)),
            dma((3, CHUNKS)),
            dma((3, CHUNKS)),
            dma((2, CHUNKS)),
            dma((PLANES, LINES, CHUNKS)),
            dma((n_units, LINES)),
            dma((n_units,)),
            dma((PLANES, 3)),
            dma((PLANES, RUNS)),
            dma((3,)),
            dma((RUNS,)),
        ],
        compiler_params=pltpu.CompilerParams(
            collective_id=0, has_side_effects=True, vmem_limit_bytes=48 * 1024 * 1024
        ),
    )(
        x,
        bn_gain,
        bn_bias,
        conv_bias,
        ln_gain,
        ln_bias,
        piece,
        units,
    )
    return (pooled[None], attended[None])


def solution(mesh):
    placed = (
        P("batch", "seq", None),
        P(),
        P(),
        P(None, None, "batch"),
        P(),
        P(),
        P(),
        P(None, "batch"),
    )
    fused = mesh.shape["batch"] == LINES * PLANES and mesh.shape["seq"] == RUNS
    return jax.shard_map(
        fused_on_device if fused else on_device,
        mesh=mesh,
        in_specs=placed,
        out_specs=(P("batch", "seq", None), P("batch", "seq", None)),
        check_vma=False,
    )
```

```python
import jax
import jax.numpy as jnp
from jax import lax
from jax.experimental import pallas as pl
from jax.experimental.pallas import tpu as pltpu
from jax.sharding import PartitionSpec as P

HEADS = 8
KEY = 64
VAL = 96


epsilon = 1e-05


def extended(cells, sides, width):
    for axis, dim in sides:
        count = lax.axis_size(axis)
        ends = count - 1
        head = lax.slice_in_dim(cells, 0, width, axis=dim)
        tail = lax.slice_in_dim(cells, cells.shape[dim] - width, cells.shape[dim], axis=dim)
        cells = jnp.concatenate(
            [
                lax.ppermute(tail, axis, [(i, (i + 1) % count) for i in range(ends)]),
                cells,
                lax.ppermute(head, axis, [((i + 1) % count, i) for i in range(ends)]),
            ],
            axis=dim,
        )
    return cells


def conv_taps(padded, kernel, positions):
    result = None
    for tap_index in range(kernel.shape[0]):
        window = padded[:, tap_index : tap_index + positions]
        product = jnp.einsum(
            "slc,co->slo", window, kernel[tap_index], preferred_element_type=jnp.float32
        )
        result = product if result is None else result + product
    return result


def online_step(carry, query_rows, key_block, value_block):
    best, weight_sum, accum = carry
    scores = jnp.einsum(
        "sqhk,sjhk->shqj", query_rows, key_block, preferred_element_type=jnp.float32
    )
    newest = jnp.maximum(best, jnp.max(scores, axis=-1))
    fade = jnp.exp(best - newest)
    weights = jnp.exp(scores - newest[..., None])
    weight_sum = weight_sum * fade + jnp.sum(weights, axis=-1)
    accum = accum * fade[..., None] + jnp.einsum(
        "shqj,sjhv->shqv",
        weights.astype(jnp.bfloat16),
        value_block,
        preferred_element_type=jnp.float32,
    )
    return (newest, weight_sum, accum)


def blocked_attend(carry, query_rows, key_piece, value_piece):
    rows = key_piece.shape[1]
    block = min(rows, 512)
    for first in range(0, rows, block):
        carry = online_step(
            carry,
            query_rows,
            key_piece[:, first : first + block],
            value_piece[:, first : first + block],
        )
    return carry


def empty_state(seqs_here, heads_here, rows):
    return (
        jnp.full((seqs_here, heads_here, rows), -jnp.inf, jnp.float32),
        jnp.zeros((seqs_here, heads_here, rows), jnp.float32),
        jnp.zeros((seqs_here, heads_here, rows, VAL), jnp.float32),
    )


def on_device(
    sequence_input, bn_gain, bn_bias, conv_weight, conv_bias, ln_gain, ln_bias, qkv_weight
):
    seqs_here = sequence_input.shape[0]
    positions = sequence_input.shape[1]
    channels = sequence_input.shape[2]
    values_in = sequence_input.astype(jnp.float32)
    total, squares = lax.psum(
        (jnp.sum(values_in, axis=(0, 1)), jnp.sum(values_in * values_in, axis=(0, 1))),
        ("batch", "seq"),
    )
    count = float(seqs_here * positions * lax.axis_size("batch") * lax.axis_size("seq"))
    mean = total / count
    var = squares / count - mean * mean
    activated = jax.nn.gelu(
        (values_in - mean) * lax.rsqrt(var + epsilon) * bn_gain + bn_bias, approximate=True
    ).astype(jnp.bfloat16)
    padded = extended(activated, (("seq", 1),), 2)
    conv_out = conv_taps(
        padded, lax.all_gather(conv_weight, "batch", axis=2, tiled=True), positions
    )
    conv_out = conv_out + conv_bias
    bins_here = positions // 2
    pooled = conv_out.reshape(seqs_here, bins_here, 2, channels).max(axis=2).astype(jnp.bfloat16)
    pooled_wide = pooled.astype(jnp.float32)
    centre = jnp.mean(pooled_wide, axis=-1, keepdims=True)
    spread = jnp.mean((pooled_wide - centre) ** 2, axis=-1, keepdims=True)
    normed = ((pooled_wide - centre) * lax.rsqrt(spread + epsilon) * ln_gain + ln_bias).astype(
        jnp.bfloat16
    )
    proj = jnp.einsum(
        "sbd,dk->sbk",
        normed,
        lax.all_gather(qkv_weight, "batch", axis=1, tiled=True),
        preferred_element_type=jnp.float32,
    )
    head_keys = HEADS * KEY
    queries = (proj[..., :head_keys] * KEY ** (-0.5)).astype(jnp.bfloat16)
    key_rows = proj[..., head_keys : 2 * head_keys].astype(jnp.bfloat16)
    value_rows = proj[..., 2 * head_keys :].astype(jnp.bfloat16)
    query_heads = queries.reshape(seqs_here, bins_here, HEADS, KEY)
    key_piece = lax.all_gather(key_rows, "seq", axis=1, tiled=True)
    value_piece = lax.all_gather(value_rows, "seq", axis=1, tiled=True)
    width_now = key_piece.shape[1]
    best, weight_sum, accum = blocked_attend(
        empty_state(seqs_here, HEADS, bins_here),
        query_heads,
        key_piece.reshape(seqs_here, width_now, HEADS, KEY),
        value_piece.reshape(seqs_here, width_now, HEADS, VAL),
    )
    attended = (
        (accum / weight_sum[..., None])
        .transpose(0, 2, 1, 3)
        .reshape(seqs_here, bins_here, HEADS * VAL)
        .astype(jnp.bfloat16)
    )
    return (pooled, attended)


LINES = 4
PLANES = 2
RUNS = 4
TAPS = 5
CHUNKS = 4
UNIT = 32
MESH = pl.DeviceIdType.MESH
GELU_IN = 0.7978845608028654


def unit_of(slot, s):
    quarter = HEADS * KEY // RUNS // UNIT
    values = HEADS * VAL // RUNS // UNIT
    if slot < quarter:
        return quarter * s + slot
    if slot < 2 * quarter:
        return RUNS * quarter + quarter * s + slot - quarter
    return 2 * RUNS * quarter + values * s + slot - 2 * quarter


def fused_kernel(
    x_ref,
    gain_ref,
    bias_ref,
    conv_bias_ref,
    ln_gain_ref,
    ln_bias_ref,
    piece_ref,
    units_ref,
    pooled_ref,
    attended_ref,
    x_all,
    sums_seq,
    sums_batch,
    vector_0,
    vector_1,
    vector_2,
    vector_3,
    vector_4,
    columns,
    ln_wide,
    act,
    act_wide,
    even_rows,
    odd_rows,
    pieces,
    units,
    pool_wide,
    pool_all,
    wide,
    normed,
    q_rows,
    k_rows,
    v_rows,
    att_out,
    att_in,
    own_sem,
    x_send,
    x_recv,
    ss_send,
    ss_recv,
    sb_send,
    sb_recv,
    c_send,
    f_send,
    r_send,
    c_recv,
    u_send,
    u_recv,
    p_send,
    p_recv,
    a_send,
    a_recv,
):
    b = lax.axis_index("batch")
    s = lax.axis_index("seq")
    z, y = b // PLANES, b % PLANES
    positions, channels = x_ref.shape
    bins = positions // 2
    rows = RUNS * bins
    n_batch = LINES * PLANES
    share = channels // RUNS
    part = share // n_batch
    share_in = channels // n_batch
    count = float(n_batch * RUNS * bins * 2)
    n_units = units.shape[0]
    per_shard = units_ref.shape[0]

    sibling = s + 1 - 2 * (s % 2)
    across = (s + 2) % RUNS
    diagonal = (sibling + 2) % RUNS
    mate = z * PLANES + 1 - y
    partner = z + 1 - 2 * (z % 2)
    inner = jnp.logical_or(z == 1, z == 2)
    gateway = jnp.where(z < 2, 2, 1)
    beyond = 3 - 3 * (z // 2)

    def remote(src, dst, send, recv, to_b, to_s):
        return pltpu.make_async_remote_copy(
            src_ref=src,
            dst_ref=dst,
            send_sem=send,
            recv_sem=recv,
            device_id=(to_b, to_s),
            device_id_type=MESH,
        )

    own_x = pltpu.make_async_copy(x_ref, x_all.at[s], own_sem.at[0])
    own_x.start()
    vectors = (vector_0, vector_1, vector_2, vector_3, vector_4)
    given = (gain_ref, bias_ref, conv_bias_ref, ln_gain_ref, ln_bias_ref)
    fetched = [
        pltpu.make_async_copy(ref, vectors[i], own_sem.at[2 + i])
        for i, ref in enumerate(given)
    ]
    for copy in fetched:
        copy.start()
    barrier = pltpu.get_barrier_semaphore()
    for step in range(1, RUNS):
        pl.semaphore_signal(barrier, inc=1, device_id=(b, (s + step) % RUNS), device_id_type=MESH)
    for step in range(1, n_batch):
        pl.semaphore_signal(
            barrier, inc=1, device_id=((b + step) % n_batch, s), device_id_type=MESH
        )


    def add_rows(i, carry):
        total, squares = carry
        block = x_all[s, pl.ds(pl.multiple_of(i * 16, 16), 16), :].astype(jnp.float32)
        return (
            total + jnp.sum(block, axis=0, keepdims=True),
            squares + jnp.sum(block * block, axis=0, keepdims=True),
        )

    own_x.wait()
    nothing = jnp.zeros((1, channels), jnp.float32)
    total, squares = lax.fori_loop(0, positions // 16, add_rows, (nothing, nothing))
    sums_seq[s, 0:1, :] = total
    sums_seq[s, 1:2, :] = squares

    pl.semaphore_wait(barrier, RUNS - 1 + n_batch - 1)

    started = []

    def go(copy):
        copy.start()
        started.append(copy)

    for step in range(1, RUNS):
        go(
            remote(
                sums_seq.at[s],
                sums_seq.at[s],
                ss_send.at[step],
                ss_recv.at[s],
                b,
                (s + step) % RUNS,
            )
        )
    depth = piece_ref.shape[0] // CHUNKS

    def chunk(ref, c):
        return ref.at[pl.ds(c * depth, depth), :]

    def push_chunk(c):
        mine = chunk(piece_ref, c)
        for at, line in ((0, partner), (1, gateway)):
            to = line * PLANES + y
            go(remote(mine, chunk(pieces.at[0, z], c), c_send.at[at, c], c_recv.at[0, z, c], to, s))
        go(remote(mine, chunk(pieces.at[1, z], c), c_send.at[2, c], c_recv.at[1, z, c], mate, s))

    push_chunk(0)
    go(remote(x_all.at[s], x_all.at[s], x_send.at[0], x_recv.at[s], b, across))
    go(remote(x_all.at[s], x_all.at[s], x_send.at[1], x_recv.at[s], b, sibling))
    for c in range(1, CHUNKS):
        push_chunk(c)
    own_piece = pltpu.make_async_copy(piece_ref, pieces.at[0, z], own_sem.at[1])
    own_piece.start()

    def arrived(dst, sem):
        pltpu.make_async_copy(dst, dst, sem).wait()

    for step in range(1, RUNS):
        other = (s + step) % RUNS
        arrived(sums_seq.at[other], ss_recv.at[other])
    sums_batch[b] = (sums_seq[0] + sums_seq[1]) + (sums_seq[2] + sums_seq[3])
    for step in range(1, n_batch):
        go(
            remote(
                sums_batch.at[b],
                sums_batch.at[b],
                sb_send.at[step],
                sb_recv.at[b],
                (b + step) % n_batch,
                s,
            )
        )

    def forward(line, at, c):
        here = chunk(pieces.at[0, line], c)
        return remote(
            here, chunk(pieces.at[1, line], c), f_send.at[at, c], c_recv.at[1, line, c], mate, s
        )

    others = ((1, gateway), (2, beyond))

    def forward_early(c):
        @pl.when(inner)
        def _():
            for at, line in others:
                here = chunk(pieces.at[0, line], c)
                arrived(here, c_recv.at[0, line, c])
                relay(here, line, at, c).start()
                forward(line, at, c).start()

    def forward_late(c):
        arrived(chunk(pieces.at[0, partner], c), c_recv.at[0, partner, c])
        go(forward(partner, 0, c))

        @pl.when(jnp.logical_not(inner))
        def _():
            for at, line in others:
                arrived(chunk(pieces.at[0, line], c), c_recv.at[0, line, c])
                forward(line, at, c).start()

        for at, line in others:
            started.append(forward(line, at, c))

    def relay(here, line, at, c):
        return remote(
            here, here, r_send.at[at - 1, c], c_recv.at[0, line, c], partner * PLANES + y, s
        )

    forward_early(0)
    forward_early(1)
    forward_late(0)
    for copy in fetched:
        copy.wait()
    spare = jnp.zeros((128 - len(given), channels), jnp.float32)
    columns[...] = jnp.transpose(
        jnp.concatenate([v[...].reshape(1, channels) for v in vectors] + [spare], axis=0)
    )
    ln_wide[0] = jnp.broadcast_to(columns[:, 3:4], (channels, bins))
    ln_wide[1] = jnp.broadcast_to(columns[:, 4:5], (channels, bins))
    for step in range(1, n_batch):
        other = (b + step) % n_batch
        arrived(sums_batch.at[other], sb_recv.at[other])
    sums = jnp.zeros((2, channels), jnp.float32)
    for i in range(n_batch):
        sums = sums + sums_batch[i]
    mean = sums[0:1] / count
    var = sums[1:2] / count - mean * mean
    scale = lax.rsqrt(var + epsilon) * vector_0[...].reshape(1, channels)
    shift = vector_1[...].reshape(1, channels)

    def activate(run):
        def body(i, _):
            first = pl.multiple_of(i * 32, 32)
            v = x_all[run, pl.ds(first, 32), :].astype(jnp.float32)
            v = (v - mean) * scale + shift
            g = 0.5 * v * (1.0 + jnp.tanh(GELU_IN * (v + 0.044715 * (v * v * v))))
            at = pl.ds(pl.multiple_of(run * bins + i * 16, 16), 16)
            for j in range(channels // 128):
                lanes = slice(j * 128, j * 128 + 128)
                act_wide[j, pl.ds(first, 32), :] = g[:, lanes]
                even = act_wide[j, pl.ds(first, 16, stride=2), :]
                odd = act_wide[j, pl.ds(first + 1, 16, stride=2), :]
                act[at, lanes] = even.astype(jnp.bfloat16)
                act[at, channels + j * 128 : channels + j * 128 + 128] = odd.astype(jnp.bfloat16)
            return 0

        lax.fori_loop(0, bins // 16, body, 0)

    activate(s)
    forward_early(2)
    forward_early(3)
    forward_late(1)
    arrived(x_all.at[sibling], x_recv.at[sibling])
    activate(sibling)
    arrived(x_all.at[across], x_recv.at[across])
    go(
        remote(
            x_all.at[across], x_all.at[across], x_send.at[2], x_recv.at[across], b, sibling
        )
    )
    forward_late(2)
    activate(across)

    for slot in range(n_units):
        unit = unit_of(slot, s)
        holder = unit // per_shard

        @pl.when(holder == b)
        def _(slot=slot, unit=unit):
            mine = units_ref.at[unit - per_shard * b]
            for step in range(1, LINES):
                to = ((z + step) % LINES) * PLANES + y
                remote(
                    mine, units.at[slot], u_send.at[slot, step], u_recv.at[slot], to, s
                ).start()
            pltpu.make_async_copy(mine, units.at[slot], u_recv.at[slot]).start()

    forward_late(3)
    arrived(x_all.at[diagonal], x_recv.at[diagonal])
    activate(diagonal)

    def back(v):
        lane = lax.broadcasted_iota(jnp.int32, v.shape, 1)
        return jnp.where(lane == 0, 0.0, pltpu.roll(v, 1, 1))

    def ahead(v):
        lane = lax.broadcasted_iota(jnp.int32, v.shape, 1)
        return jnp.where(lane == rows - 1, 0.0, pltpu.roll(v, rows - 1, 1))

    contract_last = (((1,), (1,)), ((), ()))

    padded = piece_ref.shape[0]

    def multiply(stack, first, count):
        for result, lanes in (
            (even_rows, slice(0, channels)),
            (odd_rows, slice(channels, 2 * channels)),
        ):
            product = lax.dot_general(
                stack, act[:, lanes], contract_last, preferred_element_type=jnp.float32
            )
            for line in range(LINES):
                at = line * padded + first
                result[at : at + count, :] = product[line * count : (line + 1) * count]

    def convolve(half):
        def combine(line, _):
            taps = [
                pl.ds(pl.multiple_of(line * padded + t * part, 8), part) for t in range(TAPS)
            ]
            e = [even_rows[tap, :] for tap in taps]
            o = [odd_rows[tap, :] for tap in taps]
            first = back(e[0] + o[1]) + e[2] + o[3] + ahead(e[4])
            second = back(o[0]) + e[1] + o[2] + ahead(e[3] + o[4])
            source = line * PLANES + (y if half == 0 else 1 - y)
            at = pl.multiple_of(source * share_in + s * part, 8)
            offset = columns[pl.ds(at, part), 2:3]
            pool_wide[pl.ds(pl.multiple_of(line * part, 8), part), :] = (
                jnp.maximum(first, second) + offset
            )
            return 0

        lax.fori_loop(0, LINES, combine, 0)
        pool_all[s, half] = pool_wide[...].astype(jnp.bfloat16)
        mine = pool_all.at[s, half]
        go(remote(mine, mine, p_send.at[half, 0], p_recv.at[half, s], b, across))
        go(remote(mine, mine, p_send.at[half, 1], p_recv.at[half, s], b, sibling))

    def pass_on(half):
        theirs = pool_all.at[across, half]
        arrived(theirs, p_recv.at[half, across])
        go(remote(theirs, theirs, p_send.at[half, 2], p_recv.at[half, across], b, sibling))

    def in_order(run, half):
        block = pool_all[run, half].astype(jnp.float32)
        for line in range(LINES):
            source = line * PLANES + (y if half == 0 else 1 - y)
            at = pl.multiple_of(source * share_in + run * part, 8)
            wide[pl.ds(at, part), :] = block[line * part : (line + 1) * part]

    def pass_units():
        for slot in range(n_units):
            holder = unit_of(slot, s) // per_shard

            @pl.when(jnp.logical_and(holder != b, holder % PLANES == y))
            def _(slot=slot):
                arrived(units.at[slot], u_recv.at[slot])
                remote(
                    units.at[slot], units.at[slot], u_send.at[slot, 0], u_recv.at[slot], mate, s
                ).start()

    own_piece.wait()
    multiply(pieces[0].reshape(LINES * padded, channels), 0, padded)
    convolve(0)
    for slot in range(n_units):
        unit = unit_of(slot, s)

        @pl.when(unit // per_shard == b)
        def _(slot=slot, unit=unit):
            mine = units_ref.at[unit - per_shard * b]
            remote(mine, units.at[slot], u_send.at[slot, 0], u_recv.at[slot], mate, s).start()

    pass_on(0)
    in_order(s, 0)
    in_order(across, 0)
    for run in (sibling, diagonal):
        arrived(pool_all.at[run, 0], p_recv.at[0, run])
        in_order(run, 0)
    for c in range(CHUNKS):
        if c == CHUNKS - 1:
            pass_units()
        for line in range(LINES):
            arrived(chunk(pieces.at[1, line], c), c_recv.at[1, line, c])
        part_now = pieces[1, :, c * depth : (c + 1) * depth, :].reshape(LINES * depth, channels)
        multiply(part_now, c * depth, depth)
    convolve(1)

    in_order(s, 1)
    pass_on(1)
    in_order(across, 1)
    for run in (sibling, diagonal):
        arrived(pool_all.at[run, 1], p_recv.at[1, run])
        in_order(run, 1)

    def norm(j, _):
        lanes = pl.ds(pl.multiple_of(j * bins, 128), bins)
        block = wide[:, lanes]
        centre = jnp.sum(block, axis=0, keepdims=True) / channels
        away = block - centre
        spread = jnp.sum(away * away, axis=0, keepdims=True) / channels
        normed[:, lanes] = (
            away * lax.rsqrt(spread + epsilon) * ln_wide[0] + ln_wide[1]
        ).astype(jnp.bfloat16)
        return 0

    lax.fori_loop(0, RUNS, norm, 0)

    for slot in range(n_units):
        holder = unit_of(slot, s) // per_shard

        @pl.when(jnp.logical_or(holder == b, holder % PLANES != y))
        def _(slot=slot):
            arrived(units.at[slot], u_recv.at[slot])

    here = HEADS // RUNS
    keys = here * KEY
    n_keys = keys // UNIT
    normed_now = normed[...]
    wq = units[0:n_keys].reshape(keys, channels)
    q_rows[...] = (
        jnp.dot(wq, normed_now, preferred_element_type=jnp.float32) * KEY ** (-0.5)
    ).astype(jnp.bfloat16)
    wk = units[n_keys : 2 * n_keys].reshape(keys, channels)
    k_rows[...] = jnp.transpose(
        jnp.dot(wk, normed_now, preferred_element_type=jnp.float32)
    ).astype(jnp.bfloat16)
    wv = units[2 * n_keys :].reshape(here * VAL, channels)
    v_rows[...] = jnp.dot(wv, normed_now, preferred_element_type=jnp.float32).astype(jnp.bfloat16)

    def attend(run):
        lanes = pl.ds(pl.multiple_of(run * bins, 128), bins)
        q_now = q_rows[:, lanes]
        row = lax.broadcasted_iota(jnp.int32, q_now.shape, 0)
        for h in range(here):
            q_head = jnp.where(row // KEY == h, q_now, jnp.zeros_like(q_now))
            scores = jnp.dot(k_rows[...], q_head, preferred_element_type=jnp.float32)
            weights = jnp.exp(scores - jnp.max(scores, axis=0, keepdims=True))
            below = jnp.sum(weights, axis=0, keepdims=True)
            above = jnp.dot(
                v_rows[h * VAL : (h + 1) * VAL, :],
                weights.astype(jnp.bfloat16),
                preferred_element_type=jnp.float32,
            )
            att_out[run, h * VAL : (h + 1) * VAL, :] = (above / below).astype(jnp.bfloat16)

    for run, k in ((across, 0), (diagonal, 1), (sibling, 2)):
        attend(run)
        go(remote(att_out.at[run], att_in.at[s], a_send.at[k], a_recv.at[s], b, run))
    attend(s)
    att_in[s] = att_out[s]
    lanes = pl.ds(pl.multiple_of(s * bins, 128), bins)
    pooled_ref[...] = jnp.transpose(wide[:, lanes]).astype(jnp.bfloat16)
    for run in (across, diagonal, sibling):
        arrived(att_in.at[run], a_recv.at[run])
    gathered = jnp.concatenate([att_in[r].astype(jnp.float32) for r in range(RUNS)], axis=0)
    attended_ref[...] = jnp.transpose(gathered).astype(jnp.bfloat16)

    for copy in started:
        copy.wait_send()

    @pl.when(inner)
    def _():
        for c in range(CHUNKS):
            for at, line in ((1, gateway), (2, beyond)):
                relay(chunk(pieces.at[0, line], c), line, at, c).wait_send()

    for slot in range(n_units):
        holder = unit_of(slot, s) // per_shard

        @pl.when(holder % PLANES == y)
        def _(slot=slot):
            remote(
                units.at[slot], units.at[slot], u_send.at[slot, 0], u_recv.at[slot], mate, s
            ).wait_send()

        @pl.when(holder == b)
        def _(slot=slot):
            for step in range(1, LINES):
                to = ((z + step) % LINES) * PLANES + y
                remote(
                    units.at[slot], units.at[slot], u_send.at[slot, step], u_recv.at[slot], to, s
                ).wait_send()


def fused_on_device(
    sequence_input, bn_gain, bn_bias, conv_weight, conv_bias, ln_gain, ln_bias, qkv_weight
):
    _, positions, channels = sequence_input.shape
    bins = positions // 2
    rows = RUNS * bins
    n_batch = LINES * PLANES
    share = channels // RUNS
    part = share // n_batch
    s = lax.axis_index("seq")
    taps = conv_weight.shape[0]
    x = sequence_input.reshape(positions, channels)
    piece = lax.dynamic_slice_in_dim(conv_weight, s * part, part, axis=2)
    piece = piece.transpose(0, 2, 1).reshape(taps * part, channels)
    padded = -(-taps * part // 16) * 16
    piece = jnp.pad(piece, ((0, padded - taps * part), (0, 0)))

    per_shard = qkv_weight.shape[1] // UNIT
    units = qkv_weight.T.reshape(per_shard, UNIT, channels)
    n_units = per_shard * n_batch // RUNS
    keys = HEADS * KEY // RUNS
    vals = HEADS * VAL // RUNS
    bf16, f32 = jnp.bfloat16, jnp.float32
    dma = pltpu.SemaphoreType.DMA
    pooled, attended = pl.pallas_call(
        fused_kernel,
        out_shape=(
            jax.ShapeDtypeStruct((bins, channels), bf16),
            jax.ShapeDtypeStruct((bins, channels), bf16),
        ),
        in_specs=[
            *[pl.BlockSpec(memory_space=pltpu.HBM)] * 6,
            pl.BlockSpec(memory_space=pltpu.VMEM),
            pl.BlockSpec(memory_space=pltpu.HBM),
        ],
        out_specs=(pl.BlockSpec(memory_space=pltpu.VMEM),) * 2,
        scratch_shapes=[
            pltpu.VMEM((RUNS, positions, channels), bf16),
            pltpu.VMEM((RUNS, 2, channels), f32),
            pltpu.VMEM((n_batch, 2, channels), f32),
            *[pltpu.VMEM((channels,), f32)] * 5,
            pltpu.VMEM((channels, 128), f32),
            pltpu.VMEM((2, channels, bins), f32),
            pltpu.VMEM((rows, 2 * channels), bf16),
            pltpu.VMEM((channels // 128, positions, 128), f32),
            pltpu.VMEM((LINES * padded, rows), f32),
            pltpu.VMEM((LINES * padded, rows), f32),
            pltpu.VMEM((PLANES, LINES, padded, channels), bf16),
            pltpu.VMEM((n_units, UNIT, channels), bf16),
            pltpu.VMEM((share // PLANES, rows), f32),
            pltpu.VMEM((RUNS, PLANES, share // PLANES, rows), bf16),
            pltpu.VMEM((channels, rows), f32),
            pltpu.VMEM((channels, rows), bf16),
            pltpu.VMEM((keys, rows), bf16),
            pltpu.VMEM((rows, keys), bf16),
            pltpu.VMEM((vals, rows), bf16),
            pltpu.VMEM((RUNS, vals, bins), bf16),
            pltpu.VMEM((RUNS, vals, bins), bf16),
            dma((7,)),
            dma((3,)),
            dma((RUNS,)),
            dma((RUNS,)),
            dma((RUNS,)),
            dma((n_batch,)),
            dma((n_batch,)),
            dma((3, CHUNKS)),
            dma((3, CHUNKS)),
            dma((2, CHUNKS)),
            dma((PLANES, LINES, CHUNKS)),
            dma((n_units, LINES)),
            dma((n_units,)),
            dma((PLANES, 3)),
            dma((PLANES, RUNS)),
            dma((3,)),
            dma((RUNS,)),
        ],
        compiler_params=pltpu.CompilerParams(
            collective_id=0, has_side_effects=True, vmem_limit_bytes=48 * 1024 * 1024
        ),
    )(
        x,
        bn_gain,
        bn_bias,
        conv_bias,
        ln_gain,
        ln_bias,
        piece,
        units,
    )
    return (pooled[None], attended[None])


def solution(mesh):
    placed = (
        P("batch", "seq", None),
        P(),
        P(),
        P(None, None, "batch"),
        P(),
        P(),
        P(),
        P(None, "batch"),
    )
    fused = mesh.shape["batch"] == LINES * PLANES and mesh.shape["seq"] == RUNS
    return jax.shard_map(
        fused_on_device if fused else on_device,
        mesh=mesh,
        in_specs=placed,
        out_specs=(P("batch", "seq", None), P("batch", "seq", None)),
        check_vma=False,
    )
```

```python
import jax
import jax.numpy as jnp
from jax import lax
from jax.experimental import pallas as pl
from jax.experimental.pallas import tpu as pltpu
from jax.sharding import PartitionSpec as P

HEADS = 8
KEY = 64
VAL = 96


epsilon = 1e-05


def extended(cells, sides, width):
    for axis, dim in sides:
        count = lax.axis_size(axis)
        ends = count - 1
        head = lax.slice_in_dim(cells, 0, width, axis=dim)
        tail = lax.slice_in_dim(cells, cells.shape[dim] - width, cells.shape[dim], axis=dim)
        cells = jnp.concatenate(
            [
                lax.ppermute(tail, axis, [(i, (i + 1) % count) for i in range(ends)]),
                cells,
                lax.ppermute(head, axis, [((i + 1) % count, i) for i in range(ends)]),
            ],
            axis=dim,
        )
    return cells


def conv_taps(padded, kernel, positions):
    result = None
    for tap_index in range(kernel.shape[0]):
        window = padded[:, tap_index : tap_index + positions]
        product = jnp.einsum(
            "slc,co->slo", window, kernel[tap_index], preferred_element_type=jnp.float32
        )
        result = product if result is None else result + product
    return result


def online_step(carry, query_rows, key_block, value_block):
    best, weight_sum, accum = carry
    scores = jnp.einsum(
        "sqhk,sjhk->shqj", query_rows, key_block, preferred_element_type=jnp.float32
    )
    newest = jnp.maximum(best, jnp.max(scores, axis=-1))
    fade = jnp.exp(best - newest)
    weights = jnp.exp(scores - newest[..., None])
    weight_sum = weight_sum * fade + jnp.sum(weights, axis=-1)
    accum = accum * fade[..., None] + jnp.einsum(
        "shqj,sjhv->shqv",
        weights.astype(jnp.bfloat16),
        value_block,
        preferred_element_type=jnp.float32,
    )
    return (newest, weight_sum, accum)


def blocked_attend(carry, query_rows, key_piece, value_piece):
    rows = key_piece.shape[1]
    block = min(rows, 512)
    for first in range(0, rows, block):
        carry = online_step(
            carry,
            query_rows,
            key_piece[:, first : first + block],
            value_piece[:, first : first + block],
        )
    return carry


def empty_state(seqs_here, heads_here, rows):
    return (
        jnp.full((seqs_here, heads_here, rows), -jnp.inf, jnp.float32),
        jnp.zeros((seqs_here, heads_here, rows), jnp.float32),
        jnp.zeros((seqs_here, heads_here, rows, VAL), jnp.float32),
    )


def on_device(
    sequence_input, bn_gain, bn_bias, conv_weight, conv_bias, ln_gain, ln_bias, qkv_weight
):
    seqs_here = sequence_input.shape[0]
    positions = sequence_input.shape[1]
    channels = sequence_input.shape[2]
    values_in = sequence_input.astype(jnp.float32)
    total, squares = lax.psum(
        (jnp.sum(values_in, axis=(0, 1)), jnp.sum(values_in * values_in, axis=(0, 1))),
        ("batch", "seq"),
    )
    count = float(seqs_here * positions * lax.axis_size("batch") * lax.axis_size("seq"))
    mean = total / count
    var = squares / count - mean * mean
    activated = jax.nn.gelu(
        (values_in - mean) * lax.rsqrt(var + epsilon) * bn_gain + bn_bias, approximate=True
    ).astype(jnp.bfloat16)
    padded = extended(activated, (("seq", 1),), 2)
    conv_out = conv_taps(
        padded, lax.all_gather(conv_weight, "batch", axis=2, tiled=True), positions
    )
    conv_out = conv_out + conv_bias
    bins_here = positions // 2
    pooled = conv_out.reshape(seqs_here, bins_here, 2, channels).max(axis=2).astype(jnp.bfloat16)
    pooled_wide = pooled.astype(jnp.float32)
    centre = jnp.mean(pooled_wide, axis=-1, keepdims=True)
    spread = jnp.mean((pooled_wide - centre) ** 2, axis=-1, keepdims=True)
    normed = ((pooled_wide - centre) * lax.rsqrt(spread + epsilon) * ln_gain + ln_bias).astype(
        jnp.bfloat16
    )
    proj = jnp.einsum(
        "sbd,dk->sbk",
        normed,
        lax.all_gather(qkv_weight, "batch", axis=1, tiled=True),
        preferred_element_type=jnp.float32,
    )
    head_keys = HEADS * KEY
    queries = (proj[..., :head_keys] * KEY ** (-0.5)).astype(jnp.bfloat16)
    key_rows = proj[..., head_keys : 2 * head_keys].astype(jnp.bfloat16)
    value_rows = proj[..., 2 * head_keys :].astype(jnp.bfloat16)
    query_heads = queries.reshape(seqs_here, bins_here, HEADS, KEY)
    key_piece = lax.all_gather(key_rows, "seq", axis=1, tiled=True)
    value_piece = lax.all_gather(value_rows, "seq", axis=1, tiled=True)
    width_now = key_piece.shape[1]
    best, weight_sum, accum = blocked_attend(
        empty_state(seqs_here, HEADS, bins_here),
        query_heads,
        key_piece.reshape(seqs_here, width_now, HEADS, KEY),
        value_piece.reshape(seqs_here, width_now, HEADS, VAL),
    )
    attended = (
        (accum / weight_sum[..., None])
        .transpose(0, 2, 1, 3)
        .reshape(seqs_here, bins_here, HEADS * VAL)
        .astype(jnp.bfloat16)
    )
    return (pooled, attended)


LINES = 4
PLANES = 2
RUNS = 4
TAPS = 5
CHUNKS = 4
UNIT = 32
MESH = pl.DeviceIdType.MESH
GELU_IN = 0.7978845608028654


def unit_of(slot, s):
    quarter = HEADS * KEY // RUNS // UNIT
    values = HEADS * VAL // RUNS // UNIT
    if slot < quarter:
        return quarter * s + slot
    if slot < 2 * quarter:
        return RUNS * quarter + quarter * s + slot - quarter
    return 2 * RUNS * quarter + values * s + slot - 2 * quarter


def fused_kernel(
    x_ref,
    gain_ref,
    bias_ref,
    conv_bias_ref,
    ln_gain_ref,
    ln_bias_ref,
    piece_ref,
    units_ref,
    pooled_ref,
    attended_ref,
    x_all,
    sums_seq,
    sums_batch,
    vector_0,
    vector_1,
    vector_2,
    vector_3,
    vector_4,
    columns,
    ln_wide,
    act,
    act_wide,
    even_rows,
    odd_rows,
    pieces,
    units,
    pool_wide,
    pool_all,
    wide,
    normed,
    q_rows,
    k_rows,
    v_rows,
    att_out,
    att_in,
    own_sem,
    x_send,
    x_recv,
    ss_send,
    ss_recv,
    sb_send,
    sb_recv,
    c_send,
    f_send,
    r_send,
    c_recv,
    u_send,
    u_recv,
    p_send,
    p_recv,
    a_send,
    a_recv,
):
    b = lax.axis_index("batch")
    s = lax.axis_index("seq")
    z, y = b // PLANES, b % PLANES
    positions, channels = x_ref.shape
    bins = positions // 2
    rows = RUNS * bins
    n_batch = LINES * PLANES
    share = channels // RUNS
    part = share // n_batch
    share_in = channels // n_batch
    count = float(n_batch * RUNS * bins * 2)
    n_units = units.shape[0]
    per_shard = units_ref.shape[0]

    sibling = s + 1 - 2 * (s % 2)
    across = (s + 2) % RUNS
    diagonal = (sibling + 2) % RUNS
    mate = z * PLANES + 1 - y
    partner = z + 1 - 2 * (z % 2)
    inner = jnp.logical_or(z == 1, z == 2)
    gateway = jnp.where(z < 2, 2, 1)
    beyond = 3 - 3 * (z // 2)

    def remote(src, dst, send, recv, to_b, to_s):
        return pltpu.make_async_remote_copy(
            src_ref=src,
            dst_ref=dst,
            send_sem=send,
            recv_sem=recv,
            device_id=(to_b, to_s),
            device_id_type=MESH,
        )

    own_x = pltpu.make_async_copy(x_ref, x_all.at[s], own_sem.at[0])
    own_x.start()
    vectors = (vector_0, vector_1, vector_2, vector_3, vector_4)
    given = (gain_ref, bias_ref, conv_bias_ref, ln_gain_ref, ln_bias_ref)
    fetched = [
        pltpu.make_async_copy(ref, vectors[i], own_sem.at[2 + i])
        for i, ref in enumerate(given)
    ]
    for copy in fetched:
        copy.start()
    barrier = pltpu.get_barrier_semaphore()
    for step in range(1, RUNS):
        pl.semaphore_signal(barrier, inc=1, device_id=(b, (s + step) % RUNS), device_id_type=MESH)
    for step in range(1, n_batch):
        pl.semaphore_signal(
            barrier, inc=1, device_id=((b + step) % n_batch, s), device_id_type=MESH
        )


    def add_rows(i, carry):
        total, squares = carry
        block = x_all[s, pl.ds(pl.multiple_of(i * 16, 16), 16), :].astype(jnp.float32)
        return (
            total + jnp.sum(block, axis=0, keepdims=True),
            squares + jnp.sum(block * block, axis=0, keepdims=True),
        )

    own_x.wait()
    nothing = jnp.zeros((1, channels), jnp.float32)
    total, squares = lax.fori_loop(0, positions // 16, add_rows, (nothing, nothing))
    sums_seq[s, 0:1, :] = total
    sums_seq[s, 1:2, :] = squares

    pl.semaphore_wait(barrier, RUNS - 1 + n_batch - 1)

    started = []

    def go(copy):
        copy.start()
        started.append(copy)

    for step in range(1, RUNS):
        go(
            remote(
                sums_seq.at[s],
                sums_seq.at[s],
                ss_send.at[step],
                ss_recv.at[s],
                b,
                (s + step) % RUNS,
            )
        )
    depth = piece_ref.shape[0] // CHUNKS

    def chunk(ref, c):
        return ref.at[pl.ds(c * depth, depth), :]

    def push_chunk(c):
        mine = chunk(piece_ref, c)
        for at, line in ((0, partner), (1, gateway)):
            to = line * PLANES + y
            go(remote(mine, chunk(pieces.at[0, z], c), c_send.at[at, c], c_recv.at[0, z, c], to, s))
        go(remote(mine, chunk(pieces.at[1, z], c), c_send.at[2, c], c_recv.at[1, z, c], mate, s))

    push_chunk(0)
    go(remote(x_all.at[s], x_all.at[s], x_send.at[0], x_recv.at[s], b, across))
    go(remote(x_all.at[s], x_all.at[s], x_send.at[1], x_recv.at[s], b, sibling))
    for c in range(1, CHUNKS):
        push_chunk(c)
    own_piece = pltpu.make_async_copy(piece_ref, pieces.at[0, z], own_sem.at[1])
    own_piece.start()

    def arrived(dst, sem):
        pltpu.make_async_copy(dst, dst, sem).wait()

    for step in range(1, RUNS):
        other = (s + step) % RUNS
        arrived(sums_seq.at[other], ss_recv.at[other])
    sums_batch[b] = (sums_seq[0] + sums_seq[1]) + (sums_seq[2] + sums_seq[3])
    for step in range(1, n_batch):
        go(
            remote(
                sums_batch.at[b],
                sums_batch.at[b],
                sb_send.at[step],
                sb_recv.at[b],
                (b + step) % n_batch,
                s,
            )
        )

    def forward(line, at, c):
        here = chunk(pieces.at[0, line], c)
        return remote(
            here, chunk(pieces.at[1, line], c), f_send.at[at, c], c_recv.at[1, line, c], mate, s
        )

    others = ((1, gateway), (2, beyond))

    def forward_early(c):
        @pl.when(inner)
        def _():
            for at, line in others:
                here = chunk(pieces.at[0, line], c)
                arrived(here, c_recv.at[0, line, c])
                relay(here, line, at, c).start()
                forward(line, at, c).start()

    def forward_late(c):
        arrived(chunk(pieces.at[0, partner], c), c_recv.at[0, partner, c])
        go(forward(partner, 0, c))

        @pl.when(jnp.logical_not(inner))
        def _():
            for at, line in others:
                arrived(chunk(pieces.at[0, line], c), c_recv.at[0, line, c])
                forward(line, at, c).start()

        for at, line in others:
            started.append(forward(line, at, c))

    def relay(here, line, at, c):
        return remote(
            here, here, r_send.at[at - 1, c], c_recv.at[0, line, c], partner * PLANES + y, s
        )

    forward_early(0)
    forward_early(1)
    forward_late(0)
    for copy in fetched:
        copy.wait()
    spare = jnp.zeros((128 - len(given), channels), jnp.float32)
    columns[...] = jnp.transpose(
        jnp.concatenate([v[...].reshape(1, channels) for v in vectors] + [spare], axis=0)
    )
    ln_wide[0] = jnp.broadcast_to(columns[:, 3:4], (channels, bins))
    ln_wide[1] = jnp.broadcast_to(columns[:, 4:5], (channels, bins))
    for step in range(1, n_batch):
        other = (b + step) % n_batch
        arrived(sums_batch.at[other], sb_recv.at[other])
    sums = jnp.zeros((2, channels), jnp.float32)
    for i in range(n_batch):
        sums = sums + sums_batch[i]
    mean = sums[0:1] / count
    var = sums[1:2] / count - mean * mean
    scale = lax.rsqrt(var + epsilon) * vector_0[...].reshape(1, channels)
    shift = vector_1[...].reshape(1, channels)

    def activate(run):
        def body(i, _):
            first = pl.multiple_of(i * 32, 32)
            v = x_all[run, pl.ds(first, 32), :].astype(jnp.float32)
            v = (v - mean) * scale + shift
            g = 0.5 * v * (1.0 + jnp.tanh(GELU_IN * (v + 0.044715 * (v * v * v))))
            for j in range(channels // 128):
                act_wide[j, pl.ds(first, 32), :] = g[:, j * 128 : j * 128 + 128]
            return 0

        lax.fori_loop(0, positions // 32, body, 0)
        lanes = pl.ds(pl.multiple_of(run * bins, 128), bins)
        for j in range(channels // 128):
            for parity in range(2):
                block = act_wide[j, pl.ds(parity, bins, stride=2), :]
                at = parity * channels + j * 128
                act[at : at + 128, lanes] = jnp.transpose(block).astype(jnp.bfloat16)

    activate(s)
    forward_early(2)
    forward_early(3)
    forward_late(1)
    arrived(x_all.at[sibling], x_recv.at[sibling])
    activate(sibling)
    arrived(x_all.at[across], x_recv.at[across])
    go(
        remote(
            x_all.at[across], x_all.at[across], x_send.at[2], x_recv.at[across], b, sibling
        )
    )
    forward_late(2)
    activate(across)

    for slot in range(n_units):
        unit = unit_of(slot, s)
        holder = unit // per_shard

        @pl.when(holder == b)
        def _(slot=slot, unit=unit):
            mine = units_ref.at[unit - per_shard * b]
            for step in range(1, LINES):
                to = ((z + step) % LINES) * PLANES + y
                remote(
                    mine, units.at[slot], u_send.at[slot, step], u_recv.at[slot], to, s
                ).start()
            pltpu.make_async_copy(mine, units.at[slot], u_recv.at[slot]).start()

    forward_late(3)
    arrived(x_all.at[diagonal], x_recv.at[diagonal])
    activate(diagonal)

    def back(v):
        lane = lax.broadcasted_iota(jnp.int32, v.shape, 1)
        return jnp.where(lane == 0, 0.0, pltpu.roll(v, 1, 1))

    def ahead(v):
        lane = lax.broadcasted_iota(jnp.int32, v.shape, 1)
        return jnp.where(lane == rows - 1, 0.0, pltpu.roll(v, rows - 1, 1))

    padded = piece_ref.shape[0]

    def multiply(stack, first, count):
        for result, lanes in (
            (even_rows, slice(0, channels)),
            (odd_rows, slice(channels, 2 * channels)),
        ):
            product = jnp.dot(stack, act[lanes, :], preferred_element_type=jnp.float32)
            for line in range(LINES):
                at = line * padded + first
                result[at : at + count, :] = product[line * count : (line + 1) * count]

    def convolve(half):
        def combine(line, _):
            taps = [
                pl.ds(pl.multiple_of(line * padded + t * part, 8), part) for t in range(TAPS)
            ]
            e = [even_rows[tap, :] for tap in taps]
            o = [odd_rows[tap, :] for tap in taps]
            first = back(e[0] + o[1]) + e[2] + o[3] + ahead(e[4])
            second = back(o[0]) + e[1] + o[2] + ahead(e[3] + o[4])
            source = line * PLANES + (y if half == 0 else 1 - y)
            at = pl.multiple_of(source * share_in + s * part, 8)
            offset = columns[pl.ds(at, part), 2:3]
            pool_wide[pl.ds(pl.multiple_of(line * part, 8), part), :] = (
                jnp.maximum(first, second) + offset
            )
            return 0

        lax.fori_loop(0, LINES, combine, 0)
        pool_all[s, half] = pool_wide[...].astype(jnp.bfloat16)
        mine = pool_all.at[s, half]
        go(remote(mine, mine, p_send.at[half, 0], p_recv.at[half, s], b, across))
        go(remote(mine, mine, p_send.at[half, 1], p_recv.at[half, s], b, sibling))

    def pass_on(half):
        theirs = pool_all.at[across, half]
        arrived(theirs, p_recv.at[half, across])
        go(remote(theirs, theirs, p_send.at[half, 2], p_recv.at[half, across], b, sibling))

    def in_order(run, half):
        block = pool_all[run, half].astype(jnp.float32)
        for line in range(LINES):
            source = line * PLANES + (y if half == 0 else 1 - y)
            at = pl.multiple_of(source * share_in + run * part, 8)
            wide[pl.ds(at, part), :] = block[line * part : (line + 1) * part]

    def pass_units():
        for slot in range(n_units):
            holder = unit_of(slot, s) // per_shard

            @pl.when(jnp.logical_and(holder != b, holder % PLANES == y))
            def _(slot=slot):
                arrived(units.at[slot], u_recv.at[slot])
                remote(
                    units.at[slot], units.at[slot], u_send.at[slot, 0], u_recv.at[slot], mate, s
                ).start()

    own_piece.wait()
    multiply(pieces[0].reshape(LINES * padded, channels), 0, padded)
    convolve(0)
    for slot in range(n_units):
        unit = unit_of(slot, s)

        @pl.when(unit // per_shard == b)
        def _(slot=slot, unit=unit):
            mine = units_ref.at[unit - per_shard * b]
            remote(mine, units.at[slot], u_send.at[slot, 0], u_recv.at[slot], mate, s).start()

    pass_on(0)
    in_order(s, 0)
    in_order(across, 0)
    for run in (sibling, diagonal):
        arrived(pool_all.at[run, 0], p_recv.at[0, run])
        in_order(run, 0)
    for c in range(CHUNKS):
        if c == CHUNKS - 1:
            pass_units()
        for line in range(LINES):
            arrived(chunk(pieces.at[1, line], c), c_recv.at[1, line, c])
        part_now = pieces[1, :, c * depth : (c + 1) * depth, :].reshape(LINES * depth, channels)
        multiply(part_now, c * depth, depth)
    convolve(1)

    in_order(s, 1)
    pass_on(1)
    in_order(across, 1)
    for run in (sibling, diagonal):
        arrived(pool_all.at[run, 1], p_recv.at[1, run])
        in_order(run, 1)

    def norm(j, _):
        lanes = pl.ds(pl.multiple_of(j * bins, 128), bins)
        block = wide[:, lanes]
        centre = jnp.sum(block, axis=0, keepdims=True) / channels
        away = block - centre
        spread = jnp.sum(away * away, axis=0, keepdims=True) / channels
        normed[:, lanes] = (
            away * lax.rsqrt(spread + epsilon) * ln_wide[0] + ln_wide[1]
        ).astype(jnp.bfloat16)
        return 0

    lax.fori_loop(0, RUNS, norm, 0)

    for slot in range(n_units):
        holder = unit_of(slot, s) // per_shard

        @pl.when(jnp.logical_or(holder == b, holder % PLANES != y))
        def _(slot=slot):
            arrived(units.at[slot], u_recv.at[slot])

    here = HEADS // RUNS
    keys = here * KEY
    projected = jnp.dot(
        units[...].reshape(n_units * UNIT, channels),
        normed[...],
        preferred_element_type=jnp.float32,
    )
    q_rows[...] = (projected[:keys] * KEY ** (-0.5)).astype(jnp.bfloat16)
    k_rows[...] = jnp.transpose(projected[keys : 2 * keys]).astype(jnp.bfloat16)
    v_rows[...] = projected[2 * keys :].astype(jnp.bfloat16)

    def attend(run):
        lanes = pl.ds(pl.multiple_of(run * bins, 128), bins)
        q_now = q_rows[:, lanes]
        row = lax.broadcasted_iota(jnp.int32, q_now.shape, 0)
        apart = [jnp.where(row // KEY == h, q_now, jnp.zeros_like(q_now)) for h in range(here)]
        scores = jnp.dot(
            k_rows[...], jnp.concatenate(apart, axis=1), preferred_element_type=jnp.float32
        )
        weights = jnp.exp(scores - jnp.max(scores, axis=0, keepdims=True))
        below = jnp.sum(weights, axis=0, keepdims=True)
        rounded = weights.astype(jnp.bfloat16)
        for h in range(here):
            mine = slice(h * bins, (h + 1) * bins)
            above = jnp.dot(
                v_rows[h * VAL : (h + 1) * VAL, :],
                rounded[:, mine],
                preferred_element_type=jnp.float32,
            )
            att_out[run, h * VAL : (h + 1) * VAL, :] = (above / below[:, mine]).astype(
                jnp.bfloat16
            )

    for run, k in ((across, 0), (diagonal, 1), (sibling, 2)):
        attend(run)
        go(remote(att_out.at[run], att_in.at[s], a_send.at[k], a_recv.at[s], b, run))
    attend(s)
    att_in[s] = att_out[s]
    lanes = pl.ds(pl.multiple_of(s * bins, 128), bins)
    pooled_ref[...] = jnp.transpose(wide[:, lanes]).astype(jnp.bfloat16)
    for run in (across, diagonal, sibling):
        arrived(att_in.at[run], a_recv.at[run])
    gathered = jnp.concatenate([att_in[r].astype(jnp.float32) for r in range(RUNS)], axis=0)
    attended_ref[...] = jnp.transpose(gathered).astype(jnp.bfloat16)

    for copy in started:
        copy.wait_send()

    @pl.when(inner)
    def _():
        for c in range(CHUNKS):
            for at, line in ((1, gateway), (2, beyond)):
                relay(chunk(pieces.at[0, line], c), line, at, c).wait_send()

    for slot in range(n_units):
        holder = unit_of(slot, s) // per_shard

        @pl.when(holder % PLANES == y)
        def _(slot=slot):
            remote(
                units.at[slot], units.at[slot], u_send.at[slot, 0], u_recv.at[slot], mate, s
            ).wait_send()

        @pl.when(holder == b)
        def _(slot=slot):
            for step in range(1, LINES):
                to = ((z + step) % LINES) * PLANES + y
                remote(
                    units.at[slot], units.at[slot], u_send.at[slot, step], u_recv.at[slot], to, s
                ).wait_send()


def fused_on_device(
    sequence_input, bn_gain, bn_bias, conv_weight, conv_bias, ln_gain, ln_bias, qkv_weight
):
    _, positions, channels = sequence_input.shape
    bins = positions // 2
    rows = RUNS * bins
    n_batch = LINES * PLANES
    share = channels // RUNS
    part = share // n_batch
    s = lax.axis_index("seq")
    taps = conv_weight.shape[0]
    x = sequence_input.reshape(positions, channels)
    piece = lax.dynamic_slice_in_dim(conv_weight, s * part, part, axis=2)
    piece = piece.transpose(0, 2, 1).reshape(taps * part, channels)
    padded = -(-taps * part // 16) * 16
    piece = jnp.pad(piece, ((0, padded - taps * part), (0, 0)))

    per_shard = qkv_weight.shape[1] // UNIT
    units = qkv_weight.T.reshape(per_shard, UNIT, channels)
    n_units = per_shard * n_batch // RUNS
    keys = HEADS * KEY // RUNS
    vals = HEADS * VAL // RUNS
    bf16, f32 = jnp.bfloat16, jnp.float32
    dma = pltpu.SemaphoreType.DMA
    pooled, attended = pl.pallas_call(
        fused_kernel,
        out_shape=(
            jax.ShapeDtypeStruct((bins, channels), bf16),
            jax.ShapeDtypeStruct((bins, channels), bf16),
        ),
        in_specs=[
            *[pl.BlockSpec(memory_space=pltpu.HBM)] * 6,
            pl.BlockSpec(memory_space=pltpu.VMEM),
            pl.BlockSpec(memory_space=pltpu.HBM),
        ],
        out_specs=(pl.BlockSpec(memory_space=pltpu.VMEM),) * 2,
        scratch_shapes=[
            pltpu.VMEM((RUNS, positions, channels), bf16),
            pltpu.VMEM((RUNS, 2, channels), f32),
            pltpu.VMEM((n_batch, 2, channels), f32),
            *[pltpu.VMEM((channels,), f32)] * 5,
            pltpu.VMEM((channels, 128), f32),
            pltpu.VMEM((2, channels, bins), f32),
            pltpu.VMEM((2 * channels, rows), bf16),
            pltpu.VMEM((channels // 128, positions, 128), f32),
            pltpu.VMEM((LINES * padded, rows), f32),
            pltpu.VMEM((LINES * padded, rows), f32),
            pltpu.VMEM((PLANES, LINES, padded, channels), bf16),
            pltpu.VMEM((n_units, UNIT, channels), bf16),
            pltpu.VMEM((share // PLANES, rows), f32),
            pltpu.VMEM((RUNS, PLANES, share // PLANES, rows), bf16),
            pltpu.VMEM((channels, rows), f32),
            pltpu.VMEM((channels, rows), bf16),
            pltpu.VMEM((keys, rows), bf16),
            pltpu.VMEM((rows, keys), bf16),
            pltpu.VMEM((vals, rows), bf16),
            pltpu.VMEM((RUNS, vals, bins), bf16),
            pltpu.VMEM((RUNS, vals, bins), bf16),
            dma((7,)),
            dma((3,)),
            dma((RUNS,)),
            dma((RUNS,)),
            dma((RUNS,)),
            dma((n_batch,)),
            dma((n_batch,)),
            dma((3, CHUNKS)),
            dma((3, CHUNKS)),
            dma((2, CHUNKS)),
            dma((PLANES, LINES, CHUNKS)),
            dma((n_units, LINES)),
            dma((n_units,)),
            dma((PLANES, 3)),
            dma((PLANES, RUNS)),
            dma((3,)),
            dma((RUNS,)),
        ],
        compiler_params=pltpu.CompilerParams(
            collective_id=0, has_side_effects=True, vmem_limit_bytes=48 * 1024 * 1024
        ),
    )(
        x,
        bn_gain,
        bn_bias,
        conv_bias,
        ln_gain,
        ln_bias,
        piece,
        units,
    )
    return (pooled[None], attended[None])


def solution(mesh):
    placed = (
        P("batch", "seq", None),
        P(),
        P(),
        P(None, None, "batch"),
        P(),
        P(),
        P(),
        P(None, "batch"),
    )
    fused = mesh.shape["batch"] == LINES * PLANES and mesh.shape["seq"] == RUNS
    return jax.shard_map(
        fused_on_device if fused else on_device,
        mesh=mesh,
        in_specs=placed,
        out_specs=(P("batch", "seq", None), P("batch", "seq", None)),
        check_vma=False,
    )
```

```python
import jax
import jax.numpy as jnp
from jax import lax
from jax.experimental import pallas as pl
from jax.experimental.pallas import tpu as pltpu
from jax.sharding import PartitionSpec as P

HEADS = 8
KEY = 64
VAL = 96


epsilon = 1e-05


def extended(cells, sides, width):
    for axis, dim in sides:
        count = lax.axis_size(axis)
        ends = count - 1
        head = lax.slice_in_dim(cells, 0, width, axis=dim)
        tail = lax.slice_in_dim(cells, cells.shape[dim] - width, cells.shape[dim], axis=dim)
        cells = jnp.concatenate(
            [
                lax.ppermute(tail, axis, [(i, (i + 1) % count) for i in range(ends)]),
                cells,
                lax.ppermute(head, axis, [((i + 1) % count, i) for i in range(ends)]),
            ],
            axis=dim,
        )
    return cells


def conv_taps(padded, kernel, positions):
    result = None
    for tap_index in range(kernel.shape[0]):
        window = padded[:, tap_index : tap_index + positions]
        product = jnp.einsum(
            "slc,co->slo", window, kernel[tap_index], preferred_element_type=jnp.float32
        )
        result = product if result is None else result + product
    return result


def online_step(carry, query_rows, key_block, value_block):
    best, weight_sum, accum = carry
    scores = jnp.einsum(
        "sqhk,sjhk->shqj", query_rows, key_block, preferred_element_type=jnp.float32
    )
    newest = jnp.maximum(best, jnp.max(scores, axis=-1))
    fade = jnp.exp(best - newest)
    weights = jnp.exp(scores - newest[..., None])
    weight_sum = weight_sum * fade + jnp.sum(weights, axis=-1)
    accum = accum * fade[..., None] + jnp.einsum(
        "shqj,sjhv->shqv",
        weights.astype(jnp.bfloat16),
        value_block,
        preferred_element_type=jnp.float32,
    )
    return (newest, weight_sum, accum)


def blocked_attend(carry, query_rows, key_piece, value_piece):
    rows = key_piece.shape[1]
    block = min(rows, 512)
    for first in range(0, rows, block):
        carry = online_step(
            carry,
            query_rows,
            key_piece[:, first : first + block],
            value_piece[:, first : first + block],
        )
    return carry


def empty_state(seqs_here, heads_here, rows):
    return (
        jnp.full((seqs_here, heads_here, rows), -jnp.inf, jnp.float32),
        jnp.zeros((seqs_here, heads_here, rows), jnp.float32),
        jnp.zeros((seqs_here, heads_here, rows, VAL), jnp.float32),
    )


def on_device(
    sequence_input, bn_gain, bn_bias, conv_weight, conv_bias, ln_gain, ln_bias, qkv_weight
):
    seqs_here = sequence_input.shape[0]
    positions = sequence_input.shape[1]
    channels = sequence_input.shape[2]
    values_in = sequence_input.astype(jnp.float32)
    total, squares = lax.psum(
        (jnp.sum(values_in, axis=(0, 1)), jnp.sum(values_in * values_in, axis=(0, 1))),
        ("batch", "seq"),
    )
    count = float(seqs_here * positions * lax.axis_size("batch") * lax.axis_size("seq"))
    mean = total / count
    var = squares / count - mean * mean
    activated = jax.nn.gelu(
        (values_in - mean) * lax.rsqrt(var + epsilon) * bn_gain + bn_bias, approximate=True
    ).astype(jnp.bfloat16)
    padded = extended(activated, (("seq", 1),), 2)
    conv_out = conv_taps(
        padded, lax.all_gather(conv_weight, "batch", axis=2, tiled=True), positions
    )
    conv_out = conv_out + conv_bias
    bins_here = positions // 2
    pooled = conv_out.reshape(seqs_here, bins_here, 2, channels).max(axis=2).astype(jnp.bfloat16)
    pooled_wide = pooled.astype(jnp.float32)
    centre = jnp.mean(pooled_wide, axis=-1, keepdims=True)
    spread = jnp.mean((pooled_wide - centre) ** 2, axis=-1, keepdims=True)
    normed = ((pooled_wide - centre) * lax.rsqrt(spread + epsilon) * ln_gain + ln_bias).astype(
        jnp.bfloat16
    )
    proj = jnp.einsum(
        "sbd,dk->sbk",
        normed,
        lax.all_gather(qkv_weight, "batch", axis=1, tiled=True),
        preferred_element_type=jnp.float32,
    )
    head_keys = HEADS * KEY
    queries = (proj[..., :head_keys] * KEY ** (-0.5)).astype(jnp.bfloat16)
    key_rows = proj[..., head_keys : 2 * head_keys].astype(jnp.bfloat16)
    value_rows = proj[..., 2 * head_keys :].astype(jnp.bfloat16)
    query_heads = queries.reshape(seqs_here, bins_here, HEADS, KEY)
    key_piece = lax.all_gather(key_rows, "seq", axis=1, tiled=True)
    value_piece = lax.all_gather(value_rows, "seq", axis=1, tiled=True)
    width_now = key_piece.shape[1]
    best, weight_sum, accum = blocked_attend(
        empty_state(seqs_here, HEADS, bins_here),
        query_heads,
        key_piece.reshape(seqs_here, width_now, HEADS, KEY),
        value_piece.reshape(seqs_here, width_now, HEADS, VAL),
    )
    attended = (
        (accum / weight_sum[..., None])
        .transpose(0, 2, 1, 3)
        .reshape(seqs_here, bins_here, HEADS * VAL)
        .astype(jnp.bfloat16)
    )
    return (pooled, attended)


LINES = 4
PLANES = 2
RUNS = 4
TAPS = 5
CHUNKS = 4
CROSSED = (2, 3)
UNIT = 32
MESH = pl.DeviceIdType.MESH
GELU_IN = 0.7978845608028654


def unit_of(slot, s):
    quarter = HEADS * KEY // RUNS // UNIT
    values = HEADS * VAL // RUNS // UNIT
    if slot < quarter:
        return quarter * s + slot
    if slot < 2 * quarter:
        return RUNS * quarter + quarter * s + slot - quarter
    return 2 * RUNS * quarter + values * s + slot - 2 * quarter


def fused_kernel(
    x_ref,
    gain_ref,
    bias_ref,
    conv_bias_ref,
    ln_gain_ref,
    ln_bias_ref,
    piece_ref,
    units_ref,
    pooled_ref,
    attended_ref,
    x_all,
    sums_seq,
    sums_batch,
    vector_0,
    vector_1,
    vector_2,
    vector_3,
    vector_4,
    columns,
    ln_wide,
    act,
    act_wide,
    even_rows,
    odd_rows,
    pieces,
    units,
    pool_wide,
    pool_all,
    wide,
    normed,
    q_rows,
    k_rows,
    v_rows,
    att_out,
    att_in,
    own_sem,
    x_send,
    x_recv,
    ss_send,
    ss_recv,
    sb_send,
    sb_recv,
    c_send,
    f_send,
    r_send,
    c_recv,
    u_send,
    u_recv,
    p_send,
    p_recv,
    a_send,
    a_recv,
):
    b = lax.axis_index("batch")
    s = lax.axis_index("seq")
    z, y = b // PLANES, b % PLANES
    positions, channels = x_ref.shape
    bins = positions // 2
    rows = RUNS * bins
    n_batch = LINES * PLANES
    share = channels // RUNS
    part = share // n_batch
    share_in = channels // n_batch
    count = float(n_batch * RUNS * bins * 2)
    n_units = units.shape[0]
    per_shard = units_ref.shape[0]

    sibling = s + 1 - 2 * (s % 2)
    across = (s + 2) % RUNS
    diagonal = (sibling + 2) % RUNS
    mate = z * PLANES + 1 - y
    partner = z + 1 - 2 * (z % 2)
    inner = jnp.logical_or(z == 1, z == 2)
    gateway = jnp.where(z < 2, 2, 1)
    beyond = 3 - 3 * (z // 2)

    def remote(src, dst, send, recv, to_b, to_s):
        return pltpu.make_async_remote_copy(
            src_ref=src,
            dst_ref=dst,
            send_sem=send,
            recv_sem=recv,
            device_id=(to_b, to_s),
            device_id_type=MESH,
        )

    own_x = pltpu.make_async_copy(x_ref, x_all.at[s], own_sem.at[0])
    own_x.start()
    vectors = (vector_0, vector_1, vector_2, vector_3, vector_4)
    given = (gain_ref, bias_ref, conv_bias_ref, ln_gain_ref, ln_bias_ref)
    fetched = [
        pltpu.make_async_copy(ref, vectors[i], own_sem.at[2 + i])
        for i, ref in enumerate(given)
    ]
    for copy in fetched:
        copy.start()
    barrier = pltpu.get_barrier_semaphore()
    for step in range(1, RUNS):
        pl.semaphore_signal(barrier, inc=1, device_id=(b, (s + step) % RUNS), device_id_type=MESH)
    for step in range(1, n_batch):
        pl.semaphore_signal(
            barrier, inc=1, device_id=((b + step) % n_batch, s), device_id_type=MESH
        )


    def add_rows(i, carry):
        total, squares = carry
        block = x_all[s, pl.ds(pl.multiple_of(i * 16, 16), 16), :].astype(jnp.float32)
        return (
            total + jnp.sum(block, axis=0, keepdims=True),
            squares + jnp.sum(block * block, axis=0, keepdims=True),
        )

    own_x.wait()
    nothing = jnp.zeros((1, channels), jnp.float32)
    total, squares = lax.fori_loop(0, positions // 16, add_rows, (nothing, nothing))
    sums_seq[s, 0:1, :] = total
    sums_seq[s, 1:2, :] = squares

    pl.semaphore_wait(barrier, RUNS - 1 + n_batch - 1)

    started = []

    def go(copy):
        copy.start()
        started.append(copy)

    for step in range(1, RUNS):
        go(
            remote(
                sums_seq.at[s],
                sums_seq.at[s],
                ss_send.at[step],
                ss_recv.at[s],
                b,
                (s + step) % RUNS,
            )
        )
    depth = piece_ref.shape[0] // CHUNKS

    def chunk(ref, c):
        return ref.at[pl.ds(c * depth, depth), :]

    def push_chunk(c):
        mine = chunk(piece_ref, c)
        for at, line in ((0, partner), (1, gateway)):
            to = line * PLANES + y
            go(remote(mine, chunk(pieces.at[0, z], c), c_send.at[at, c], c_recv.at[0, z, c], to, s))
        go(remote(mine, chunk(pieces.at[1, z], c), c_send.at[2, c], c_recv.at[1, z, c], mate, s))

    push_chunk(0)
    go(remote(x_all.at[s], x_all.at[s], x_send.at[0], x_recv.at[s], b, across))
    go(remote(x_all.at[s], x_all.at[s], x_send.at[1], x_recv.at[s], b, sibling))
    for c in range(1, CHUNKS):
        push_chunk(c)
    own_piece = pltpu.make_async_copy(piece_ref, pieces.at[0, z], own_sem.at[1])
    own_piece.start()

    def arrived(dst, sem):
        pltpu.make_async_copy(dst, dst, sem).wait()

    for step in range(1, RUNS):
        other = (s + step) % RUNS
        arrived(sums_seq.at[other], ss_recv.at[other])
    sums_batch[b] = (sums_seq[0] + sums_seq[1]) + (sums_seq[2] + sums_seq[3])
    for step in range(1, n_batch):
        go(
            remote(
                sums_batch.at[b],
                sums_batch.at[b],
                sb_send.at[step],
                sb_recv.at[b],
                (b + step) % n_batch,
                s,
            )
        )

    def forward(line, at, c):
        here = chunk(pieces.at[0, line], c)
        return remote(
            here, chunk(pieces.at[1, line], c), f_send.at[at, c], c_recv.at[1, line, c], mate, s
        )

    others = ((1, gateway), (2, beyond))

    def forward_early(c):
        @pl.when(inner)
        def _():
            for at, line in others:
                here = chunk(pieces.at[0, line], c)
                arrived(here, c_recv.at[0, line, c])
                relay(here, line, at, c).start()
                forward(line, at, c).start()

    def forward_late(c):
        arrived(chunk(pieces.at[0, partner], c), c_recv.at[0, partner, c])
        if c not in CROSSED:
            go(forward(partner, 0, c))

        @pl.when(jnp.logical_not(inner))
        def _():
            for at, line in others:
                arrived(chunk(pieces.at[0, line], c), c_recv.at[0, line, c])
                forward(line, at, c).start()

        for at, line in others:
            started.append(forward(line, at, c))

    def relay(here, line, at, c):
        return remote(
            here, here, r_send.at[at - 1, c], c_recv.at[0, line, c], partner * PLANES + y, s
        )

    def forward_crossed(c):
        here = chunk(pieces.at[1, z], c)
        arrived(here, c_recv.at[1, z, c])
        go(remote(here, here, r_send.at[2, c], c_recv.at[1, z, c], partner * PLANES + y, s))

    forward_early(0)
    forward_early(1)
    forward_late(0)
    for copy in fetched:
        copy.wait()
    spare = jnp.zeros((128 - len(given), channels), jnp.float32)
    columns[...] = jnp.transpose(
        jnp.concatenate([v[...].reshape(1, channels) for v in vectors] + [spare], axis=0)
    )
    ln_wide[0] = jnp.broadcast_to(columns[:, 3:4], (channels, bins))
    ln_wide[1] = jnp.broadcast_to(columns[:, 4:5], (channels, bins))
    for step in range(1, n_batch):
        other = (b + step) % n_batch
        arrived(sums_batch.at[other], sb_recv.at[other])
    sums = jnp.zeros((2, channels), jnp.float32)
    for i in range(n_batch):
        sums = sums + sums_batch[i]
    mean = sums[0:1] / count
    var = sums[1:2] / count - mean * mean
    scale = lax.rsqrt(var + epsilon) * vector_0[...].reshape(1, channels)
    shift = vector_1[...].reshape(1, channels)

    def activate(run):
        def body(i, _):
            first = pl.multiple_of(i * 32, 32)
            v = x_all[run, pl.ds(first, 32), :].astype(jnp.float32)
            v = (v - mean) * scale + shift
            g = 0.5 * v * (1.0 + jnp.tanh(GELU_IN * (v + 0.044715 * (v * v * v))))
            for j in range(channels // 128):
                act_wide[j, pl.ds(first, 32), :] = g[:, j * 128 : j * 128 + 128]
            return 0

        lax.fori_loop(0, positions // 32, body, 0)
        lanes = pl.ds(pl.multiple_of(run * bins, 128), bins)
        for j in range(channels // 128):
            for parity in range(2):
                block = act_wide[j, pl.ds(parity, bins, stride=2), :]
                at = parity * channels + j * 128
                act[at : at + 128, lanes] = jnp.transpose(block).astype(jnp.bfloat16)

    activate(s)
    forward_early(2)
    forward_early(3)
    for c in CROSSED:
        forward_crossed(c)
    forward_late(1)

    for slot in range(n_units):
        unit = unit_of(slot, s)
        holder = unit // per_shard

        @pl.when(holder == b)
        def _(slot=slot, unit=unit):
            mine = units_ref.at[unit - per_shard * b]
            for step in range(1, LINES):
                to = ((z + step) % LINES) * PLANES + y
                remote(
                    mine, units.at[slot], u_send.at[slot, step], u_recv.at[slot], to, s
                ).start()
            pltpu.make_async_copy(mine, units.at[slot], u_recv.at[slot]).start()
    arrived(x_all.at[sibling], x_recv.at[sibling])
    activate(sibling)
    arrived(x_all.at[across], x_recv.at[across])
    go(
        remote(
            x_all.at[across], x_all.at[across], x_send.at[2], x_recv.at[across], b, sibling
        )
    )
    forward_late(2)
    activate(across)
    forward_late(3)
    arrived(x_all.at[diagonal], x_recv.at[diagonal])
    activate(diagonal)

    def back(v):
        lane = lax.broadcasted_iota(jnp.int32, v.shape, 1)
        return jnp.where(lane == 0, 0.0, pltpu.roll(v, 1, 1))

    def ahead(v):
        lane = lax.broadcasted_iota(jnp.int32, v.shape, 1)
        return jnp.where(lane == rows - 1, 0.0, pltpu.roll(v, rows - 1, 1))

    padded = piece_ref.shape[0]

    def multiply(stack, first, count):
        for result, lanes in (
            (even_rows, slice(0, channels)),
            (odd_rows, slice(channels, 2 * channels)),
        ):
            product = jnp.dot(stack, act[lanes, :], preferred_element_type=jnp.float32)
            for line in range(LINES):
                at = line * padded + first
                result[at : at + count, :] = product[line * count : (line + 1) * count]

    def convolve(half):
        def combine(line, _):
            taps = [
                pl.ds(pl.multiple_of(line * padded + t * part, 8), part) for t in range(TAPS)
            ]
            e = [even_rows[tap, :] for tap in taps]
            o = [odd_rows[tap, :] for tap in taps]
            first = back(e[0] + o[1]) + e[2] + o[3] + ahead(e[4])
            second = back(o[0]) + e[1] + o[2] + ahead(e[3] + o[4])
            source = line * PLANES + (y if half == 0 else 1 - y)
            at = pl.multiple_of(source * share_in + s * part, 8)
            offset = columns[pl.ds(at, part), 2:3]
            pool_wide[pl.ds(pl.multiple_of(line * part, 8), part), :] = (
                jnp.maximum(first, second) + offset
            )
            return 0

        lax.fori_loop(0, LINES, combine, 0)
        pool_all[s, half] = pool_wide[...].astype(jnp.bfloat16)
        mine = pool_all.at[s, half]
        go(remote(mine, mine, p_send.at[half, 0], p_recv.at[half, s], b, across))
        go(remote(mine, mine, p_send.at[half, 1], p_recv.at[half, s], b, sibling))

    def pass_on(half):
        theirs = pool_all.at[across, half]
        arrived(theirs, p_recv.at[half, across])
        go(remote(theirs, theirs, p_send.at[half, 2], p_recv.at[half, across], b, sibling))

    def in_order(run, half):
        block = pool_all[run, half].astype(jnp.float32)
        for line in range(LINES):
            source = line * PLANES + (y if half == 0 else 1 - y)
            at = pl.multiple_of(source * share_in + run * part, 8)
            wide[pl.ds(at, part), :] = block[line * part : (line + 1) * part]

    def pass_units():
        for slot in range(n_units):
            holder = unit_of(slot, s) // per_shard

            @pl.when(jnp.logical_and(holder != b, holder % PLANES == y))
            def _(slot=slot):
                arrived(units.at[slot], u_recv.at[slot])
                remote(
                    units.at[slot], units.at[slot], u_send.at[slot, 0], u_recv.at[slot], mate, s
                ).start()

    own_piece.wait()
    multiply(pieces[0].reshape(LINES * padded, channels), 0, padded)
    convolve(0)
    for slot in range(n_units):
        unit = unit_of(slot, s)

        @pl.when(unit // per_shard == b)
        def _(slot=slot, unit=unit):
            mine = units_ref.at[unit - per_shard * b]
            remote(mine, units.at[slot], u_send.at[slot, 0], u_recv.at[slot], mate, s).start()

    pass_on(0)
    in_order(s, 0)
    in_order(across, 0)
    for run in (sibling, diagonal):
        arrived(pool_all.at[run, 0], p_recv.at[0, run])
        in_order(run, 0)
    for c in range(CHUNKS):
        if c == CHUNKS - 1:
            pass_units()
        for line in (z, partner, gateway, beyond)[1 if c in CROSSED else 0 :]:
            arrived(chunk(pieces.at[1, line], c), c_recv.at[1, line, c])
        part_now = pieces[1, :, c * depth : (c + 1) * depth, :].reshape(LINES * depth, channels)
        multiply(part_now, c * depth, depth)
    convolve(1)

    in_order(s, 1)
    pass_on(1)
    in_order(across, 1)
    for run in (sibling, diagonal):
        arrived(pool_all.at[run, 1], p_recv.at[1, run])
        in_order(run, 1)

    def norm(j, _):
        lanes = pl.ds(pl.multiple_of(j * bins, 128), bins)
        block = wide[:, lanes]
        centre = jnp.sum(block, axis=0, keepdims=True) / channels
        away = block - centre
        spread = jnp.sum(away * away, axis=0, keepdims=True) / channels
        normed[:, lanes] = (
            away * lax.rsqrt(spread + epsilon) * ln_wide[0] + ln_wide[1]
        ).astype(jnp.bfloat16)
        return 0

    lax.fori_loop(0, RUNS, norm, 0)

    for slot in range(n_units):
        holder = unit_of(slot, s) // per_shard

        @pl.when(jnp.logical_or(holder == b, holder % PLANES != y))
        def _(slot=slot):
            arrived(units.at[slot], u_recv.at[slot])

    here = HEADS // RUNS
    keys = here * KEY
    projected = jnp.dot(
        units[...].reshape(n_units * UNIT, channels),
        normed[...],
        preferred_element_type=jnp.float32,
    )
    q_rows[...] = (projected[:keys] * KEY ** (-0.5)).astype(jnp.bfloat16)
    k_rows[...] = jnp.transpose(projected[keys : 2 * keys]).astype(jnp.bfloat16)
    v_rows[...] = projected[2 * keys :].astype(jnp.bfloat16)

    def attend(run):
        lanes = pl.ds(pl.multiple_of(run * bins, 128), bins)
        q_now = q_rows[:, lanes]
        row = lax.broadcasted_iota(jnp.int32, q_now.shape, 0)
        apart = [jnp.where(row // KEY == h, q_now, jnp.zeros_like(q_now)) for h in range(here)]
        scores = jnp.dot(
            k_rows[...], jnp.concatenate(apart, axis=1), preferred_element_type=jnp.float32
        )
        weights = jnp.exp(scores - jnp.max(scores, axis=0, keepdims=True))
        below = jnp.sum(weights, axis=0, keepdims=True)
        rounded = weights.astype(jnp.bfloat16)
        for h in range(here):
            mine = slice(h * bins, (h + 1) * bins)
            above = jnp.dot(
                v_rows[h * VAL : (h + 1) * VAL, :],
                rounded[:, mine],
                preferred_element_type=jnp.float32,
            )
            att_out[run, h * VAL : (h + 1) * VAL, :] = (above / below[:, mine]).astype(
                jnp.bfloat16
            )

    for run, k in ((across, 0), (diagonal, 1), (sibling, 2)):
        attend(run)
        go(remote(att_out.at[run], att_in.at[s], a_send.at[k], a_recv.at[s], b, run))
    attend(s)
    att_in[s] = att_out[s]
    lanes = pl.ds(pl.multiple_of(s * bins, 128), bins)
    pooled_ref[...] = jnp.transpose(wide[:, lanes]).astype(jnp.bfloat16)
    for run in (across, diagonal, sibling):
        arrived(att_in.at[run], a_recv.at[run])
    gathered = jnp.concatenate([att_in[r].astype(jnp.float32) for r in range(RUNS)], axis=0)
    attended_ref[...] = jnp.transpose(gathered).astype(jnp.bfloat16)

    for copy in started:
        copy.wait_send()

    @pl.when(inner)
    def _():
        for c in range(CHUNKS):
            for at, line in ((1, gateway), (2, beyond)):
                relay(chunk(pieces.at[0, line], c), line, at, c).wait_send()

    for slot in range(n_units):
        holder = unit_of(slot, s) // per_shard

        @pl.when(holder % PLANES == y)
        def _(slot=slot):
            remote(
                units.at[slot], units.at[slot], u_send.at[slot, 0], u_recv.at[slot], mate, s
            ).wait_send()

        @pl.when(holder == b)
        def _(slot=slot):
            for step in range(1, LINES):
                to = ((z + step) % LINES) * PLANES + y
                remote(
                    units.at[slot], units.at[slot], u_send.at[slot, step], u_recv.at[slot], to, s
                ).wait_send()


def fused_on_device(
    sequence_input, bn_gain, bn_bias, conv_weight, conv_bias, ln_gain, ln_bias, qkv_weight
):
    _, positions, channels = sequence_input.shape
    bins = positions // 2
    rows = RUNS * bins
    n_batch = LINES * PLANES
    share = channels // RUNS
    part = share // n_batch
    s = lax.axis_index("seq")
    taps = conv_weight.shape[0]
    x = sequence_input.reshape(positions, channels)
    piece = lax.dynamic_slice_in_dim(conv_weight, s * part, part, axis=2)
    piece = piece.transpose(0, 2, 1).reshape(taps * part, channels)
    padded = -(-taps * part // 16) * 16
    piece = jnp.pad(piece, ((0, padded - taps * part), (0, 0)))

    per_shard = qkv_weight.shape[1] // UNIT
    units = qkv_weight.T.reshape(per_shard, UNIT, channels)
    n_units = per_shard * n_batch // RUNS
    keys = HEADS * KEY // RUNS
    vals = HEADS * VAL // RUNS
    bf16, f32 = jnp.bfloat16, jnp.float32
    dma = pltpu.SemaphoreType.DMA
    pooled, attended = pl.pallas_call(
        fused_kernel,
        out_shape=(
            jax.ShapeDtypeStruct((bins, channels), bf16),
            jax.ShapeDtypeStruct((bins, channels), bf16),
        ),
        in_specs=[
            *[pl.BlockSpec(memory_space=pltpu.HBM)] * 6,
            pl.BlockSpec(memory_space=pltpu.VMEM),
            pl.BlockSpec(memory_space=pltpu.HBM),
        ],
        out_specs=(pl.BlockSpec(memory_space=pltpu.VMEM),) * 2,
        scratch_shapes=[
            pltpu.VMEM((RUNS, positions, channels), bf16),
            pltpu.VMEM((RUNS, 2, channels), f32),
            pltpu.VMEM((n_batch, 2, channels), f32),
            *[pltpu.VMEM((channels,), f32)] * 5,
            pltpu.VMEM((channels, 128), f32),
            pltpu.VMEM((2, channels, bins), f32),
            pltpu.VMEM((2 * channels, rows), bf16),
            pltpu.VMEM((channels // 128, positions, 128), f32),
            pltpu.VMEM((LINES * padded, rows), f32),
            pltpu.VMEM((LINES * padded, rows), f32),
            pltpu.VMEM((PLANES, LINES, padded, channels), bf16),
            pltpu.VMEM((n_units, UNIT, channels), bf16),
            pltpu.VMEM((share // PLANES, rows), f32),
            pltpu.VMEM((RUNS, PLANES, share // PLANES, rows), bf16),
            pltpu.VMEM((channels, rows), f32),
            pltpu.VMEM((channels, rows), bf16),
            pltpu.VMEM((keys, rows), bf16),
            pltpu.VMEM((rows, keys), bf16),
            pltpu.VMEM((vals, rows), bf16),
            pltpu.VMEM((RUNS, vals, bins), bf16),
            pltpu.VMEM((RUNS, vals, bins), bf16),
            dma((7,)),
            dma((3,)),
            dma((RUNS,)),
            dma((RUNS,)),
            dma((RUNS,)),
            dma((n_batch,)),
            dma((n_batch,)),
            dma((3, CHUNKS)),
            dma((3, CHUNKS)),
            dma((3, CHUNKS)),
            dma((PLANES, LINES, CHUNKS)),
            dma((n_units, LINES)),
            dma((n_units,)),
            dma((PLANES, 3)),
            dma((PLANES, RUNS)),
            dma((3,)),
            dma((RUNS,)),
        ],
        compiler_params=pltpu.CompilerParams(
            collective_id=0, has_side_effects=True, vmem_limit_bytes=48 * 1024 * 1024
        ),
    )(
        x,
        bn_gain,
        bn_bias,
        conv_bias,
        ln_gain,
        ln_bias,
        piece,
        units,
    )
    return (pooled[None], attended[None])


def solution(mesh):
    placed = (
        P("batch", "seq", None),
        P(),
        P(),
        P(None, None, "batch"),
        P(),
        P(),
        P(),
        P(None, "batch"),
    )
    fused = mesh.shape["batch"] == LINES * PLANES and mesh.shape["seq"] == RUNS
    return jax.shard_map(
        fused_on_device if fused else on_device,
        mesh=mesh,
        in_specs=placed,
        out_specs=(P("batch", "seq", None), P("batch", "seq", None)),
        check_vma=False,
    )
```

```python
import jax
import jax.numpy as jnp
from jax import lax
from jax.experimental import pallas as pl
from jax.experimental.pallas import tpu as pltpu
from jax.sharding import PartitionSpec as P

HEADS = 8
KEY = 64
VAL = 96


epsilon = 1e-05


def extended(cells, sides, width):
    for axis, dim in sides:
        count = lax.axis_size(axis)
        ends = count - 1
        head = lax.slice_in_dim(cells, 0, width, axis=dim)
        tail = lax.slice_in_dim(cells, cells.shape[dim] - width, cells.shape[dim], axis=dim)
        cells = jnp.concatenate(
            [
                lax.ppermute(tail, axis, [(i, (i + 1) % count) for i in range(ends)]),
                cells,
                lax.ppermute(head, axis, [((i + 1) % count, i) for i in range(ends)]),
            ],
            axis=dim,
        )
    return cells


def conv_taps(padded, kernel, positions):
    result = None
    for tap_index in range(kernel.shape[0]):
        window = padded[:, tap_index : tap_index + positions]
        product = jnp.einsum(
            "slc,co->slo", window, kernel[tap_index], preferred_element_type=jnp.float32
        )
        result = product if result is None else result + product
    return result


def online_step(carry, query_rows, key_block, value_block):
    best, weight_sum, accum = carry
    scores = jnp.einsum(
        "sqhk,sjhk->shqj", query_rows, key_block, preferred_element_type=jnp.float32
    )
    newest = jnp.maximum(best, jnp.max(scores, axis=-1))
    fade = jnp.exp(best - newest)
    weights = jnp.exp(scores - newest[..., None])
    weight_sum = weight_sum * fade + jnp.sum(weights, axis=-1)
    accum = accum * fade[..., None] + jnp.einsum(
        "shqj,sjhv->shqv",
        weights.astype(jnp.bfloat16),
        value_block,
        preferred_element_type=jnp.float32,
    )
    return (newest, weight_sum, accum)


def blocked_attend(carry, query_rows, key_piece, value_piece):
    rows = key_piece.shape[1]
    block = min(rows, 512)
    for first in range(0, rows, block):
        carry = online_step(
            carry,
            query_rows,
            key_piece[:, first : first + block],
            value_piece[:, first : first + block],
        )
    return carry


def empty_state(seqs_here, heads_here, rows):
    return (
        jnp.full((seqs_here, heads_here, rows), -jnp.inf, jnp.float32),
        jnp.zeros((seqs_here, heads_here, rows), jnp.float32),
        jnp.zeros((seqs_here, heads_here, rows, VAL), jnp.float32),
    )


def on_device(
    sequence_input, bn_gain, bn_bias, conv_weight, conv_bias, ln_gain, ln_bias, qkv_weight
):
    seqs_here = sequence_input.shape[0]
    positions = sequence_input.shape[1]
    channels = sequence_input.shape[2]
    values_in = sequence_input.astype(jnp.float32)
    total, squares = lax.psum(
        (jnp.sum(values_in, axis=(0, 1)), jnp.sum(values_in * values_in, axis=(0, 1))),
        ("batch", "seq"),
    )
    count = float(seqs_here * positions * lax.axis_size("batch") * lax.axis_size("seq"))
    mean = total / count
    var = squares / count - mean * mean
    activated = jax.nn.gelu(
        (values_in - mean) * lax.rsqrt(var + epsilon) * bn_gain + bn_bias, approximate=True
    ).astype(jnp.bfloat16)
    padded = extended(activated, (("seq", 1),), 2)
    conv_out = conv_taps(
        padded, lax.all_gather(conv_weight, "batch", axis=2, tiled=True), positions
    )
    conv_out = conv_out + conv_bias
    bins_here = positions // 2
    pooled = conv_out.reshape(seqs_here, bins_here, 2, channels).max(axis=2).astype(jnp.bfloat16)
    pooled_wide = pooled.astype(jnp.float32)
    centre = jnp.mean(pooled_wide, axis=-1, keepdims=True)
    spread = jnp.mean((pooled_wide - centre) ** 2, axis=-1, keepdims=True)
    normed = ((pooled_wide - centre) * lax.rsqrt(spread + epsilon) * ln_gain + ln_bias).astype(
        jnp.bfloat16
    )
    proj = jnp.einsum(
        "sbd,dk->sbk",
        normed,
        lax.all_gather(qkv_weight, "batch", axis=1, tiled=True),
        preferred_element_type=jnp.float32,
    )
    head_keys = HEADS * KEY
    queries = (proj[..., :head_keys] * KEY ** (-0.5)).astype(jnp.bfloat16)
    key_rows = proj[..., head_keys : 2 * head_keys].astype(jnp.bfloat16)
    value_rows = proj[..., 2 * head_keys :].astype(jnp.bfloat16)
    query_heads = queries.reshape(seqs_here, bins_here, HEADS, KEY)
    key_piece = lax.all_gather(key_rows, "seq", axis=1, tiled=True)
    value_piece = lax.all_gather(value_rows, "seq", axis=1, tiled=True)
    width_now = key_piece.shape[1]
    best, weight_sum, accum = blocked_attend(
        empty_state(seqs_here, HEADS, bins_here),
        query_heads,
        key_piece.reshape(seqs_here, width_now, HEADS, KEY),
        value_piece.reshape(seqs_here, width_now, HEADS, VAL),
    )
    attended = (
        (accum / weight_sum[..., None])
        .transpose(0, 2, 1, 3)
        .reshape(seqs_here, bins_here, HEADS * VAL)
        .astype(jnp.bfloat16)
    )
    return (pooled, attended)


LINES = 4
PLANES = 2
RUNS = 4
TAPS = 5
CHUNKS = 4
CROSSED = (2, 3)
UNIT = 32
MESH = pl.DeviceIdType.MESH
GELU_IN = 0.7978845608028654


def unit_of(slot, s):
    quarter = HEADS * KEY // RUNS // UNIT
    values = HEADS * VAL // RUNS // UNIT
    if slot < quarter:
        return quarter * s + slot
    if slot < 2 * quarter:
        return RUNS * quarter + quarter * s + slot - quarter
    return 2 * RUNS * quarter + values * s + slot - 2 * quarter


def fused_kernel(
    x_ref,
    gain_ref,
    bias_ref,
    conv_bias_ref,
    ln_gain_ref,
    ln_bias_ref,
    piece_ref,
    units_ref,
    pooled_ref,
    attended_ref,
    x_all,
    sums_seq,
    sums_batch,
    vector_0,
    vector_1,
    vector_2,
    vector_3,
    vector_4,
    columns,
    ln_wide,
    act,
    act_wide,
    even_rows,
    odd_rows,
    pieces,
    units,
    pool_wide,
    pool_all,
    wide,
    normed,
    q_rows,
    k_rows,
    v_rows,
    att_out,
    att_in,
    own_sem,
    x_send,
    x_recv,
    ss_send,
    ss_recv,
    sb_send,
    sb_recv,
    c_send,
    f_send,
    r_send,
    c_recv,
    u_send,
    u_recv,
    p_send,
    p_recv,
    a_send,
    a_recv,
):
    b = lax.axis_index("batch")
    s = lax.axis_index("seq")
    z, y = b // PLANES, b % PLANES
    positions, channels = x_ref.shape
    bins = positions // 2
    rows = RUNS * bins
    n_batch = LINES * PLANES
    share = channels // RUNS
    part = share // n_batch
    share_in = channels // n_batch
    count = float(n_batch * RUNS * bins * 2)
    n_units = units.shape[0]
    per_shard = units_ref.shape[0]

    sibling = s + 1 - 2 * (s % 2)
    across = (s + 2) % RUNS
    diagonal = (sibling + 2) % RUNS
    mate = z * PLANES + 1 - y
    partner = z + 1 - 2 * (z % 2)
    inner = jnp.logical_or(z == 1, z == 2)
    gateway = jnp.where(z < 2, 2, 1)
    beyond = 3 - 3 * (z // 2)

    def remote(src, dst, send, recv, to_b, to_s):
        return pltpu.make_async_remote_copy(
            src_ref=src,
            dst_ref=dst,
            send_sem=send,
            recv_sem=recv,
            device_id=(to_b, to_s),
            device_id_type=MESH,
        )

    own_x = pltpu.make_async_copy(x_ref, x_all.at[s], own_sem.at[0])
    own_x.start()
    vectors = (vector_0, vector_1, vector_2, vector_3, vector_4)
    given = (gain_ref, bias_ref, conv_bias_ref, ln_gain_ref, ln_bias_ref)
    fetched = [
        pltpu.make_async_copy(ref, vectors[i], own_sem.at[2 + i])
        for i, ref in enumerate(given)
    ]
    for copy in fetched:
        copy.start()
    barrier = pltpu.get_barrier_semaphore()
    for step in range(1, RUNS):
        pl.semaphore_signal(barrier, inc=1, device_id=(b, (s + step) % RUNS), device_id_type=MESH)
    for step in range(1, n_batch):
        pl.semaphore_signal(
            barrier, inc=1, device_id=((b + step) % n_batch, s), device_id_type=MESH
        )


    def add_rows(i, carry):
        total, squares = carry
        block = x_all[s, pl.ds(pl.multiple_of(i * 16, 16), 16), :].astype(jnp.float32)
        return (
            total + jnp.sum(block, axis=0, keepdims=True),
            squares + jnp.sum(block * block, axis=0, keepdims=True),
        )

    own_x.wait()
    nothing = jnp.zeros((1, channels), jnp.float32)
    total, squares = lax.fori_loop(0, positions // 16, add_rows, (nothing, nothing))
    sums_seq[s, 0:1, :] = total
    sums_seq[s, 1:2, :] = squares

    pl.semaphore_wait(barrier, RUNS - 1 + n_batch - 1)

    started = []

    def go(copy):
        copy.start()
        started.append(copy)

    for step in range(1, RUNS):
        go(
            remote(
                sums_seq.at[s],
                sums_seq.at[s],
                ss_send.at[step],
                ss_recv.at[s],
                b,
                (s + step) % RUNS,
            )
        )
    depth = piece_ref.shape[0] // CHUNKS

    def chunk(ref, c):
        return ref.at[pl.ds(c * depth, depth), :]

    def push_chunk(c):
        mine = chunk(piece_ref, c)
        for at, line in ((0, partner), (1, gateway)):
            to = line * PLANES + y
            go(remote(mine, chunk(pieces.at[0, z], c), c_send.at[at, c], c_recv.at[0, z, c], to, s))
        go(remote(mine, chunk(pieces.at[1, z], c), c_send.at[2, c], c_recv.at[1, z, c], mate, s))

    push_chunk(0)
    go(remote(x_all.at[s], x_all.at[s], x_send.at[0], x_recv.at[s], b, across))
    go(remote(x_all.at[s], x_all.at[s], x_send.at[1], x_recv.at[s], b, sibling))
    for c in range(1, CHUNKS):
        push_chunk(c)
    own_piece = pltpu.make_async_copy(piece_ref, pieces.at[0, z], own_sem.at[1])
    own_piece.start()

    def arrived(dst, sem):
        pltpu.make_async_copy(dst, dst, sem).wait()

    for step in range(1, RUNS):
        other = (s + step) % RUNS
        arrived(sums_seq.at[other], ss_recv.at[other])
    sums_batch[b] = (sums_seq[0] + sums_seq[1]) + (sums_seq[2] + sums_seq[3])
    for step in range(1, n_batch):
        go(
            remote(
                sums_batch.at[b],
                sums_batch.at[b],
                sb_send.at[step],
                sb_recv.at[b],
                (b + step) % n_batch,
                s,
            )
        )

    def forward(line, at, c):
        here = chunk(pieces.at[0, line], c)
        return remote(
            here, chunk(pieces.at[1, line], c), f_send.at[at, c], c_recv.at[1, line, c], mate, s
        )

    others = ((1, gateway), (2, beyond))

    def forward_early(c):
        @pl.when(inner)
        def _():
            for at, line in others:
                here = chunk(pieces.at[0, line], c)
                arrived(here, c_recv.at[0, line, c])
                relay(here, line, at, c).start()
                forward(line, at, c).start()

    def forward_late(c):
        arrived(chunk(pieces.at[0, partner], c), c_recv.at[0, partner, c])
        if c not in CROSSED:
            go(forward(partner, 0, c))

        @pl.when(jnp.logical_not(inner))
        def _():
            for at, line in others:
                arrived(chunk(pieces.at[0, line], c), c_recv.at[0, line, c])
                forward(line, at, c).start()

        for at, line in others:
            started.append(forward(line, at, c))

    def relay(here, line, at, c):
        return remote(
            here, here, r_send.at[at - 1, c], c_recv.at[0, line, c], partner * PLANES + y, s
        )

    def forward_crossed(c):
        here = chunk(pieces.at[1, z], c)
        arrived(here, c_recv.at[1, z, c])
        go(remote(here, here, r_send.at[2, c], c_recv.at[1, z, c], partner * PLANES + y, s))

    forward_early(0)
    forward_early(1)
    forward_late(0)
    for copy in fetched:
        copy.wait()
    spare = jnp.zeros((128 - len(given), channels), jnp.float32)
    columns[...] = jnp.transpose(
        jnp.concatenate([v[...].reshape(1, channels) for v in vectors] + [spare], axis=0)
    )
    ln_wide[0] = jnp.broadcast_to(columns[:, 3:4], (channels, bins))
    ln_wide[1] = jnp.broadcast_to(columns[:, 4:5], (channels, bins))
    for step in range(1, n_batch):
        other = (b + step) % n_batch
        arrived(sums_batch.at[other], sb_recv.at[other])
    sums = jnp.zeros((2, channels), jnp.float32)
    for i in range(n_batch):
        sums = sums + sums_batch[i]
    mean = sums[0:1] / count
    var = sums[1:2] / count - mean * mean
    scale = lax.rsqrt(var + epsilon) * vector_0[...].reshape(1, channels)
    shift = vector_1[...].reshape(1, channels)

    def activate(run):
        def body(i, _):
            first = pl.multiple_of(i * 32, 32)
            v = x_all[run, pl.ds(first, 32), :].astype(jnp.float32)
            v = (v - mean) * scale + shift
            g = 0.5 * v * (1.0 + jnp.tanh(GELU_IN * (v + 0.044715 * (v * v * v))))
            for j in range(channels // 128):
                act_wide[j, pl.ds(first, 32), :] = g[:, j * 128 : j * 128 + 128]
            return 0

        lax.fori_loop(0, positions // 32, body, 0)
        lanes = pl.ds(pl.multiple_of(run * bins, 128), bins)
        for j in range(channels // 128):
            for parity in range(2):
                block = act_wide[j, pl.ds(parity, bins, stride=2), :]
                at = parity * channels + j * 128
                act[at : at + 128, lanes] = jnp.transpose(block).astype(jnp.bfloat16)

    activate(s)
    forward_early(2)
    forward_early(3)
    for c in CROSSED:
        forward_crossed(c)
    forward_late(1)
    arrived(x_all.at[sibling], x_recv.at[sibling])
    activate(sibling)
    arrived(x_all.at[across], x_recv.at[across])
    go(
        remote(
            x_all.at[across], x_all.at[across], x_send.at[2], x_recv.at[across], b, sibling
        )
    )
    forward_late(2)
    activate(across)

    for slot in range(n_units):
        unit = unit_of(slot, s)
        holder = unit // per_shard

        @pl.when(holder == b)
        def _(slot=slot, unit=unit):
            mine = units_ref.at[unit - per_shard * b]
            for step in range(1, LINES):
                to = ((z + step) % LINES) * PLANES + y
                remote(
                    mine, units.at[slot], u_send.at[slot, step], u_recv.at[slot], to, s
                ).start()
            pltpu.make_async_copy(mine, units.at[slot], u_recv.at[slot]).start()

    forward_late(3)
    arrived(x_all.at[diagonal], x_recv.at[diagonal])
    activate(diagonal)

    def back(v):
        lane = lax.broadcasted_iota(jnp.int32, v.shape, 1)
        return jnp.where(lane == 0, 0.0, pltpu.roll(v, 1, 1))

    def ahead(v):
        lane = lax.broadcasted_iota(jnp.int32, v.shape, 1)
        return jnp.where(lane == rows - 1, 0.0, pltpu.roll(v, rows - 1, 1))

    padded = piece_ref.shape[0]

    def multiply(stack, first, count):
        for result, lanes in (
            (even_rows, slice(0, channels)),
            (odd_rows, slice(channels, 2 * channels)),
        ):
            product = jnp.dot(stack, act[lanes, :], preferred_element_type=jnp.float32)
            for line in range(LINES):
                at = line * padded + first
                result[at : at + count, :] = product[line * count : (line + 1) * count]

    def convolve(half):
        def combine(line, _):
            taps = [
                pl.ds(pl.multiple_of(line * padded + t * part, 8), part) for t in range(TAPS)
            ]
            e = [even_rows[tap, :] for tap in taps]
            o = [odd_rows[tap, :] for tap in taps]
            first = back(e[0] + o[1]) + e[2] + o[3] + ahead(e[4])
            second = back(o[0]) + e[1] + o[2] + ahead(e[3] + o[4])
            source = line * PLANES + (y if half == 0 else 1 - y)
            at = pl.multiple_of(source * share_in + s * part, 8)
            offset = columns[pl.ds(at, part), 2:3]
            pool_wide[pl.ds(pl.multiple_of(line * part, 8), part), :] = (
                jnp.maximum(first, second) + offset
            )
            return 0

        lax.fori_loop(0, LINES, combine, 0)
        pool_all[s, half] = pool_wide[...].astype(jnp.bfloat16)
        mine = pool_all.at[s, half]
        go(remote(mine, mine, p_send.at[half, 0], p_recv.at[half, s], b, across))
        go(remote(mine, mine, p_send.at[half, 1], p_recv.at[half, s], b, sibling))

    def pass_on(half):
        theirs = pool_all.at[across, half]
        arrived(theirs, p_recv.at[half, across])
        go(remote(theirs, theirs, p_send.at[half, 2], p_recv.at[half, across], b, sibling))

    def in_order(run, half):
        block = pool_all[run, half].astype(jnp.float32)
        for line in range(LINES):
            source = line * PLANES + (y if half == 0 else 1 - y)
            at = pl.multiple_of(source * share_in + run * part, 8)
            wide[pl.ds(at, part), :] = block[line * part : (line + 1) * part]

    def pass_units():
        for slot in range(n_units):
            holder = unit_of(slot, s) // per_shard

            @pl.when(jnp.logical_and(holder != b, holder % PLANES == y))
            def _(slot=slot):
                arrived(units.at[slot], u_recv.at[slot])
                remote(
                    units.at[slot], units.at[slot], u_send.at[slot, 0], u_recv.at[slot], mate, s
                ).start()

    own_piece.wait()
    multiply(pieces[0].reshape(LINES * padded, channels), 0, padded)
    convolve(0)
    for slot in range(n_units):
        unit = unit_of(slot, s)

        @pl.when(unit // per_shard == b)
        def _(slot=slot, unit=unit):
            mine = units_ref.at[unit - per_shard * b]
            remote(mine, units.at[slot], u_send.at[slot, 0], u_recv.at[slot], mate, s).start()

    pass_on(0)
    in_order(s, 0)
    in_order(across, 0)
    for run in (sibling, diagonal):
        arrived(pool_all.at[run, 0], p_recv.at[0, run])
        in_order(run, 0)
    for c in range(CHUNKS):
        for line in (z, partner, gateway, beyond)[1 if c in CROSSED else 0 :]:
            arrived(chunk(pieces.at[1, line], c), c_recv.at[1, line, c])
        part_now = pieces[1, :, c * depth : (c + 1) * depth, :].reshape(LINES * depth, channels)
        multiply(part_now, c * depth, depth)
    convolve(1)

    in_order(s, 1)
    pass_units()
    pass_on(1)
    in_order(across, 1)
    for run in (sibling, diagonal):
        arrived(pool_all.at[run, 1], p_recv.at[1, run])
        in_order(run, 1)

    def norm(j, _):
        lanes = pl.ds(pl.multiple_of(j * bins, 128), bins)
        block = wide[:, lanes]
        centre = jnp.sum(block, axis=0, keepdims=True) / channels
        away = block - centre
        spread = jnp.sum(away * away, axis=0, keepdims=True) / channels
        normed[:, lanes] = (
            away * lax.rsqrt(spread + epsilon) * ln_wide[0] + ln_wide[1]
        ).astype(jnp.bfloat16)
        return 0

    lax.fori_loop(0, RUNS, norm, 0)

    for slot in range(n_units):
        holder = unit_of(slot, s) // per_shard

        @pl.when(jnp.logical_or(holder == b, holder % PLANES != y))
        def _(slot=slot):
            arrived(units.at[slot], u_recv.at[slot])

    here = HEADS // RUNS
    keys = here * KEY
    projected = jnp.dot(
        units[...].reshape(n_units * UNIT, channels),
        normed[...],
        preferred_element_type=jnp.float32,
    )
    q_rows[...] = (projected[:keys] * KEY ** (-0.5)).astype(jnp.bfloat16)
    k_rows[...] = jnp.transpose(projected[keys : 2 * keys]).astype(jnp.bfloat16)
    v_rows[...] = projected[2 * keys :].astype(jnp.bfloat16)

    def attend(run):
        lanes = pl.ds(pl.multiple_of(run * bins, 128), bins)
        q_now = q_rows[:, lanes]
        row = lax.broadcasted_iota(jnp.int32, q_now.shape, 0)
        apart = [jnp.where(row // KEY == h, q_now, jnp.zeros_like(q_now)) for h in range(here)]
        scores = jnp.dot(
            k_rows[...], jnp.concatenate(apart, axis=1), preferred_element_type=jnp.float32
        )
        weights = jnp.exp(scores - jnp.max(scores, axis=0, keepdims=True))
        below = jnp.sum(weights, axis=0, keepdims=True)
        rounded = weights.astype(jnp.bfloat16)
        for h in range(here):
            mine = slice(h * bins, (h + 1) * bins)
            above = jnp.dot(
                v_rows[h * VAL : (h + 1) * VAL, :],
                rounded[:, mine],
                preferred_element_type=jnp.float32,
            )
            att_out[run, h * VAL : (h + 1) * VAL, :] = (above / below[:, mine]).astype(
                jnp.bfloat16
            )

    for run, k in ((across, 0), (diagonal, 1), (sibling, 2)):
        attend(run)
        go(remote(att_out.at[run], att_in.at[s], a_send.at[k], a_recv.at[s], b, run))
    attend(s)
    att_in[s] = att_out[s]
    lanes = pl.ds(pl.multiple_of(s * bins, 128), bins)
    pooled_ref[...] = jnp.transpose(wide[:, lanes]).astype(jnp.bfloat16)
    for run in (across, diagonal, sibling):
        arrived(att_in.at[run], a_recv.at[run])
    gathered = jnp.concatenate([att_in[r].astype(jnp.float32) for r in range(RUNS)], axis=0)
    attended_ref[...] = jnp.transpose(gathered).astype(jnp.bfloat16)

    for copy in started:
        copy.wait_send()

    @pl.when(inner)
    def _():
        for c in range(CHUNKS):
            for at, line in ((1, gateway), (2, beyond)):
                relay(chunk(pieces.at[0, line], c), line, at, c).wait_send()

    for slot in range(n_units):
        holder = unit_of(slot, s) // per_shard

        @pl.when(holder % PLANES == y)
        def _(slot=slot):
            remote(
                units.at[slot], units.at[slot], u_send.at[slot, 0], u_recv.at[slot], mate, s
            ).wait_send()

        @pl.when(holder == b)
        def _(slot=slot):
            for step in range(1, LINES):
                to = ((z + step) % LINES) * PLANES + y
                remote(
                    units.at[slot], units.at[slot], u_send.at[slot, step], u_recv.at[slot], to, s
                ).wait_send()


def fused_on_device(
    sequence_input, bn_gain, bn_bias, conv_weight, conv_bias, ln_gain, ln_bias, qkv_weight
):
    _, positions, channels = sequence_input.shape
    bins = positions // 2
    rows = RUNS * bins
    n_batch = LINES * PLANES
    share = channels // RUNS
    part = share // n_batch
    s = lax.axis_index("seq")
    taps = conv_weight.shape[0]
    x = sequence_input.reshape(positions, channels)
    piece = lax.dynamic_slice_in_dim(conv_weight, s * part, part, axis=2)
    piece = piece.transpose(0, 2, 1).reshape(taps * part, channels)
    padded = -(-taps * part // 16) * 16
    piece = jnp.pad(piece, ((0, padded - taps * part), (0, 0)))

    per_shard = qkv_weight.shape[1] // UNIT
    units = qkv_weight.T.reshape(per_shard, UNIT, channels)
    n_units = per_shard * n_batch // RUNS
    keys = HEADS * KEY // RUNS
    vals = HEADS * VAL // RUNS
    bf16, f32 = jnp.bfloat16, jnp.float32
    dma = pltpu.SemaphoreType.DMA
    pooled, attended = pl.pallas_call(
        fused_kernel,
        out_shape=(
            jax.ShapeDtypeStruct((bins, channels), bf16),
            jax.ShapeDtypeStruct((bins, channels), bf16),
        ),
        in_specs=[
            *[pl.BlockSpec(memory_space=pltpu.HBM)] * 6,
            pl.BlockSpec(memory_space=pltpu.VMEM),
            pl.BlockSpec(memory_space=pltpu.HBM),
        ],
        out_specs=(pl.BlockSpec(memory_space=pltpu.VMEM),) * 2,
        scratch_shapes=[
            pltpu.VMEM((RUNS, positions, channels), bf16),
            pltpu.VMEM((RUNS, 2, channels), f32),
            pltpu.VMEM((n_batch, 2, channels), f32),
            *[pltpu.VMEM((channels,), f32)] * 5,
            pltpu.VMEM((channels, 128), f32),
            pltpu.VMEM((2, channels, bins), f32),
            pltpu.VMEM((2 * channels, rows), bf16),
            pltpu.VMEM((channels // 128, positions, 128), f32),
            pltpu.VMEM((LINES * padded, rows), f32),
            pltpu.VMEM((LINES * padded, rows), f32),
            pltpu.VMEM((PLANES, LINES, padded, channels), bf16),
            pltpu.VMEM((n_units, UNIT, channels), bf16),
            pltpu.VMEM((share // PLANES, rows), f32),
            pltpu.VMEM((RUNS, PLANES, share // PLANES, rows), bf16),
            pltpu.VMEM((channels, rows), f32),
            pltpu.VMEM((channels, rows), bf16),
            pltpu.VMEM((keys, rows), bf16),
            pltpu.VMEM((rows, keys), bf16),
            pltpu.VMEM((vals, rows), bf16),
            pltpu.VMEM((RUNS, vals, bins), bf16),
            pltpu.VMEM((RUNS, vals, bins), bf16),
            dma((7,)),
            dma((3,)),
            dma((RUNS,)),
            dma((RUNS,)),
            dma((RUNS,)),
            dma((n_batch,)),
            dma((n_batch,)),
            dma((3, CHUNKS)),
            dma((3, CHUNKS)),
            dma((3, CHUNKS)),
            dma((PLANES, LINES, CHUNKS)),
            dma((n_units, LINES)),
            dma((n_units,)),
            dma((PLANES, 3)),
            dma((PLANES, RUNS)),
            dma((3,)),
            dma((RUNS,)),
        ],
        compiler_params=pltpu.CompilerParams(
            collective_id=0, has_side_effects=True, vmem_limit_bytes=48 * 1024 * 1024
        ),
    )(
        x,
        bn_gain,
        bn_bias,
        conv_bias,
        ln_gain,
        ln_bias,
        piece,
        units,
    )
    return (pooled[None], attended[None])


def solution(mesh):
    placed = (
        P("batch", "seq", None),
        P(),
        P(),
        P(None, None, "batch"),
        P(),
        P(),
        P(),
        P(None, "batch"),
    )
    fused = mesh.shape["batch"] == LINES * PLANES and mesh.shape["seq"] == RUNS
    return jax.shard_map(
        fused_on_device if fused else on_device,
        mesh=mesh,
        in_specs=placed,
        out_specs=(P("batch", "seq", None), P("batch", "seq", None)),
        check_vma=False,
    )
```

```python
import jax
import jax.numpy as jnp
from jax import lax
from jax.experimental import pallas as pl
from jax.experimental.pallas import tpu as pltpu
from jax.sharding import PartitionSpec as P

HEADS = 8
KEY = 64
VAL = 96


epsilon = 1e-05


def extended(cells, sides, width):
    for axis, dim in sides:
        count = lax.axis_size(axis)
        ends = count - 1
        head = lax.slice_in_dim(cells, 0, width, axis=dim)
        tail = lax.slice_in_dim(cells, cells.shape[dim] - width, cells.shape[dim], axis=dim)
        cells = jnp.concatenate(
            [
                lax.ppermute(tail, axis, [(i, (i + 1) % count) for i in range(ends)]),
                cells,
                lax.ppermute(head, axis, [((i + 1) % count, i) for i in range(ends)]),
            ],
            axis=dim,
        )
    return cells


def conv_taps(padded, kernel, positions):
    result = None
    for tap_index in range(kernel.shape[0]):
        window = padded[:, tap_index : tap_index + positions]
        product = jnp.einsum(
            "slc,co->slo", window, kernel[tap_index], preferred_element_type=jnp.float32
        )
        result = product if result is None else result + product
    return result


def online_step(carry, query_rows, key_block, value_block):
    best, weight_sum, accum = carry
    scores = jnp.einsum(
        "sqhk,sjhk->shqj", query_rows, key_block, preferred_element_type=jnp.float32
    )
    newest = jnp.maximum(best, jnp.max(scores, axis=-1))
    fade = jnp.exp(best - newest)
    weights = jnp.exp(scores - newest[..., None])
    weight_sum = weight_sum * fade + jnp.sum(weights, axis=-1)
    accum = accum * fade[..., None] + jnp.einsum(
        "shqj,sjhv->shqv",
        weights.astype(jnp.bfloat16),
        value_block,
        preferred_element_type=jnp.float32,
    )
    return (newest, weight_sum, accum)


def blocked_attend(carry, query_rows, key_piece, value_piece):
    rows = key_piece.shape[1]
    block = min(rows, 512)
    for first in range(0, rows, block):
        carry = online_step(
            carry,
            query_rows,
            key_piece[:, first : first + block],
            value_piece[:, first : first + block],
        )
    return carry


def empty_state(seqs_here, heads_here, rows):
    return (
        jnp.full((seqs_here, heads_here, rows), -jnp.inf, jnp.float32),
        jnp.zeros((seqs_here, heads_here, rows), jnp.float32),
        jnp.zeros((seqs_here, heads_here, rows, VAL), jnp.float32),
    )


def on_device(
    sequence_input, bn_gain, bn_bias, conv_weight, conv_bias, ln_gain, ln_bias, qkv_weight
):
    seqs_here = sequence_input.shape[0]
    positions = sequence_input.shape[1]
    channels = sequence_input.shape[2]
    values_in = sequence_input.astype(jnp.float32)
    total, squares = lax.psum(
        (jnp.sum(values_in, axis=(0, 1)), jnp.sum(values_in * values_in, axis=(0, 1))),
        ("batch", "seq"),
    )
    count = float(seqs_here * positions * lax.axis_size("batch") * lax.axis_size("seq"))
    mean = total / count
    var = squares / count - mean * mean
    activated = jax.nn.gelu(
        (values_in - mean) * lax.rsqrt(var + epsilon) * bn_gain + bn_bias, approximate=True
    ).astype(jnp.bfloat16)
    padded = extended(activated, (("seq", 1),), 2)
    conv_out = conv_taps(
        padded, lax.all_gather(conv_weight, "batch", axis=2, tiled=True), positions
    )
    conv_out = conv_out + conv_bias
    bins_here = positions // 2
    pooled = conv_out.reshape(seqs_here, bins_here, 2, channels).max(axis=2).astype(jnp.bfloat16)
    pooled_wide = pooled.astype(jnp.float32)
    centre = jnp.mean(pooled_wide, axis=-1, keepdims=True)
    spread = jnp.mean((pooled_wide - centre) ** 2, axis=-1, keepdims=True)
    normed = ((pooled_wide - centre) * lax.rsqrt(spread + epsilon) * ln_gain + ln_bias).astype(
        jnp.bfloat16
    )
    proj = jnp.einsum(
        "sbd,dk->sbk",
        normed,
        lax.all_gather(qkv_weight, "batch", axis=1, tiled=True),
        preferred_element_type=jnp.float32,
    )
    head_keys = HEADS * KEY
    queries = (proj[..., :head_keys] * KEY ** (-0.5)).astype(jnp.bfloat16)
    key_rows = proj[..., head_keys : 2 * head_keys].astype(jnp.bfloat16)
    value_rows = proj[..., 2 * head_keys :].astype(jnp.bfloat16)
    query_heads = queries.reshape(seqs_here, bins_here, HEADS, KEY)
    key_piece = lax.all_gather(key_rows, "seq", axis=1, tiled=True)
    value_piece = lax.all_gather(value_rows, "seq", axis=1, tiled=True)
    width_now = key_piece.shape[1]
    best, weight_sum, accum = blocked_attend(
        empty_state(seqs_here, HEADS, bins_here),
        query_heads,
        key_piece.reshape(seqs_here, width_now, HEADS, KEY),
        value_piece.reshape(seqs_here, width_now, HEADS, VAL),
    )
    attended = (
        (accum / weight_sum[..., None])
        .transpose(0, 2, 1, 3)
        .reshape(seqs_here, bins_here, HEADS * VAL)
        .astype(jnp.bfloat16)
    )
    return (pooled, attended)


LINES = 4
PLANES = 2
RUNS = 4
TAPS = 5
CHUNKS = 4
CROSSED = (2, 3)
UNIT = 32
MESH = pl.DeviceIdType.MESH
GELU_IN = 0.7978845608028654


def unit_of(slot, s):
    quarter = HEADS * KEY // RUNS // UNIT
    values = HEADS * VAL // RUNS // UNIT
    if slot < quarter:
        return quarter * s + slot
    if slot < 2 * quarter:
        return RUNS * quarter + quarter * s + slot - quarter
    return 2 * RUNS * quarter + values * s + slot - 2 * quarter


def fused_kernel(
    x_ref,
    gain_ref,
    bias_ref,
    conv_bias_ref,
    ln_gain_ref,
    ln_bias_ref,
    piece_ref,
    units_ref,
    pooled_ref,
    attended_ref,
    x_all,
    sums_seq,
    sums_batch,
    vector_0,
    vector_1,
    vector_2,
    vector_3,
    vector_4,
    columns,
    ln_wide,
    act,
    act_wide,
    even_rows,
    odd_rows,
    pieces,
    units,
    pool_wide,
    pool_all,
    wide,
    normed,
    q_rows,
    k_rows,
    v_rows,
    att_out,
    att_in,
    own_sem,
    x_send,
    x_recv,
    ss_send,
    ss_recv,
    sb_send,
    sb_recv,
    c_send,
    f_send,
    r_send,
    c_recv,
    u_send,
    u_recv,
    p_send,
    p_recv,
    a_send,
    a_recv,
):
    b = lax.axis_index("batch")
    s = lax.axis_index("seq")
    z, y = b // PLANES, b % PLANES
    positions, channels = x_ref.shape
    bins = positions // 2
    rows = RUNS * bins
    n_batch = LINES * PLANES
    share = channels // RUNS
    part = share // n_batch
    share_in = channels // n_batch
    count = float(n_batch * RUNS * bins * 2)
    n_units = units.shape[0]
    per_shard = units_ref.shape[0]

    sibling = s + 1 - 2 * (s % 2)
    across = (s + 2) % RUNS
    diagonal = (sibling + 2) % RUNS
    mate = z * PLANES + 1 - y
    partner = z + 1 - 2 * (z % 2)
    inner = jnp.logical_or(z == 1, z == 2)
    gateway = jnp.where(z < 2, 2, 1)
    beyond = 3 - 3 * (z // 2)

    def remote(src, dst, send, recv, to_b, to_s):
        return pltpu.make_async_remote_copy(
            src_ref=src,
            dst_ref=dst,
            send_sem=send,
            recv_sem=recv,
            device_id=(to_b, to_s),
            device_id_type=MESH,
        )

    own_x = pltpu.make_async_copy(x_ref, x_all.at[s], own_sem.at[0])
    own_x.start()
    vectors = (vector_0, vector_1, vector_2, vector_3, vector_4)
    given = (gain_ref, bias_ref, conv_bias_ref, ln_gain_ref, ln_bias_ref)
    fetched = [
        pltpu.make_async_copy(ref, vectors[i], own_sem.at[2 + i])
        for i, ref in enumerate(given)
    ]
    for copy in fetched:
        copy.start()
    barrier = pltpu.get_barrier_semaphore()
    for step in range(1, RUNS):
        pl.semaphore_signal(barrier, inc=1, device_id=(b, (s + step) % RUNS), device_id_type=MESH)
    for step in range(1, n_batch):
        pl.semaphore_signal(
            barrier, inc=1, device_id=((b + step) % n_batch, s), device_id_type=MESH
        )


    def add_rows(i, carry):
        total, squares = carry
        block = x_all[s, pl.ds(pl.multiple_of(i * 16, 16), 16), :].astype(jnp.float32)
        return (
            total + jnp.sum(block, axis=0, keepdims=True),
            squares + jnp.sum(block * block, axis=0, keepdims=True),
        )

    own_x.wait()
    nothing = jnp.zeros((1, channels), jnp.float32)
    total, squares = lax.fori_loop(0, positions // 16, add_rows, (nothing, nothing))
    sums_seq[s, 0:1, :] = total
    sums_seq[s, 1:2, :] = squares

    pl.semaphore_wait(barrier, RUNS - 1 + n_batch - 1)

    started = []

    def go(copy):
        copy.start()
        started.append(copy)

    for step in range(1, RUNS):
        go(
            remote(
                sums_seq.at[s],
                sums_seq.at[s],
                ss_send.at[step],
                ss_recv.at[s],
                b,
                (s + step) % RUNS,
            )
        )
    depth = piece_ref.shape[0] // CHUNKS

    def chunk(ref, c):
        return ref.at[pl.ds(c * depth, depth), :]

    def push_chunk(c):
        mine = chunk(piece_ref, c)
        for at, line in ((0, partner), (1, gateway)):
            to = line * PLANES + y
            go(remote(mine, chunk(pieces.at[0, z], c), c_send.at[at, c], c_recv.at[0, z, c], to, s))
        go(remote(mine, chunk(pieces.at[1, z], c), c_send.at[2, c], c_recv.at[1, z, c], mate, s))

    push_chunk(0)
    go(remote(x_all.at[s], x_all.at[s], x_send.at[0], x_recv.at[s], b, across))
    go(remote(x_all.at[s], x_all.at[s], x_send.at[1], x_recv.at[s], b, sibling))
    for c in range(1, CHUNKS):
        push_chunk(c)
    own_piece = pltpu.make_async_copy(piece_ref, pieces.at[0, z], own_sem.at[1])
    own_piece.start()

    def arrived(dst, sem):
        pltpu.make_async_copy(dst, dst, sem).wait()

    for step in range(1, RUNS):
        other = (s + step) % RUNS
        arrived(sums_seq.at[other], ss_recv.at[other])
    sums_batch[b] = (sums_seq[0] + sums_seq[1]) + (sums_seq[2] + sums_seq[3])
    for step in range(1, n_batch):
        go(
            remote(
                sums_batch.at[b],
                sums_batch.at[b],
                sb_send.at[step],
                sb_recv.at[b],
                (b + step) % n_batch,
                s,
            )
        )

    def forward(line, at, c):
        here = chunk(pieces.at[0, line], c)
        return remote(
            here, chunk(pieces.at[1, line], c), f_send.at[at, c], c_recv.at[1, line, c], mate, s
        )

    others = ((1, gateway), (2, beyond))

    def forward_early(c):
        @pl.when(inner)
        def _():
            for at, line in others:
                here = chunk(pieces.at[0, line], c)
                arrived(here, c_recv.at[0, line, c])
                relay(here, line, at, c).start()
                forward(line, at, c).start()

    def forward_late(c):
        arrived(chunk(pieces.at[0, partner], c), c_recv.at[0, partner, c])
        if c not in CROSSED:
            go(forward(partner, 0, c))

        @pl.when(jnp.logical_not(inner))
        def _():
            for at, line in others:
                arrived(chunk(pieces.at[0, line], c), c_recv.at[0, line, c])
                forward(line, at, c).start()

        for at, line in others:
            started.append(forward(line, at, c))

    def relay(here, line, at, c):
        return remote(
            here, here, r_send.at[at - 1, c], c_recv.at[0, line, c], partner * PLANES + y, s
        )

    def forward_crossed(c):
        here = chunk(pieces.at[1, z], c)
        arrived(here, c_recv.at[1, z, c])
        go(remote(here, here, r_send.at[2, c], c_recv.at[1, z, c], partner * PLANES + y, s))

    forward_early(0)
    forward_early(1)
    forward_late(0)
    for copy in fetched:
        copy.wait()
    spare = jnp.zeros((128 - len(given), channels), jnp.float32)
    columns[...] = jnp.transpose(
        jnp.concatenate([v[...].reshape(1, channels) for v in vectors] + [spare], axis=0)
    )
    ln_wide[0] = jnp.broadcast_to(columns[:, 3:4], (channels, bins))
    ln_wide[1] = jnp.broadcast_to(columns[:, 4:5], (channels, bins))
    for step in range(1, n_batch):
        other = (b + step) % n_batch
        arrived(sums_batch.at[other], sb_recv.at[other])
    sums = jnp.zeros((2, channels), jnp.float32)
    for i in range(n_batch):
        sums = sums + sums_batch[i]
    mean = sums[0:1] / count
    var = sums[1:2] / count - mean * mean
    scale = lax.rsqrt(var + epsilon) * vector_0[...].reshape(1, channels)
    shift = vector_1[...].reshape(1, channels)

    def activate(run):
        def body(i, _):
            first = pl.multiple_of(i * 32, 32)
            v = x_all[run, pl.ds(first, 32), :].astype(jnp.float32)
            v = (v - mean) * scale + shift
            g = 0.5 * v * (1.0 + jnp.tanh(GELU_IN * (v + 0.044715 * (v * v * v))))
            for j in range(channels // 128):
                act_wide[j, pl.ds(first, 32), :] = g[:, j * 128 : j * 128 + 128]
            return 0

        lax.fori_loop(0, positions // 32, body, 0)
        lanes = pl.ds(pl.multiple_of(run * bins, 128), bins)
        for j in range(channels // 128):
            for parity in range(2):
                block = act_wide[j, pl.ds(parity, bins, stride=2), :]
                at = parity * channels + j * 128
                act[at : at + 128, lanes] = jnp.transpose(block).astype(jnp.bfloat16)

    activate(s)

    for slot in range(n_units):
        unit = unit_of(slot, s)
        holder = unit // per_shard

        @pl.when(holder == b)
        def _(slot=slot, unit=unit):
            mine = units_ref.at[unit - per_shard * b]
            for step in range(1, LINES):
                to = ((z + step) % LINES) * PLANES + y
                remote(
                    mine, units.at[slot], u_send.at[slot, step], u_recv.at[slot], to, s
                ).start()
            pltpu.make_async_copy(mine, units.at[slot], u_recv.at[slot]).start()

    forward_early(2)
    forward_early(3)
    for c in CROSSED:
        forward_crossed(c)
    forward_late(1)
    arrived(x_all.at[sibling], x_recv.at[sibling])
    activate(sibling)
    arrived(x_all.at[across], x_recv.at[across])
    go(
        remote(
            x_all.at[across], x_all.at[across], x_send.at[2], x_recv.at[across], b, sibling
        )
    )
    forward_late(2)
    activate(across)
    forward_late(3)
    arrived(x_all.at[diagonal], x_recv.at[diagonal])
    activate(diagonal)

    def back(v):
        lane = lax.broadcasted_iota(jnp.int32, v.shape, 1)
        return jnp.where(lane == 0, 0.0, pltpu.roll(v, 1, 1))

    def ahead(v):
        lane = lax.broadcasted_iota(jnp.int32, v.shape, 1)
        return jnp.where(lane == rows - 1, 0.0, pltpu.roll(v, rows - 1, 1))

    padded = piece_ref.shape[0]

    def multiply(stack, first, count):
        for result, lanes in (
            (even_rows, slice(0, channels)),
            (odd_rows, slice(channels, 2 * channels)),
        ):
            product = jnp.dot(stack, act[lanes, :], preferred_element_type=jnp.float32)
            for line in range(LINES):
                at = line * padded + first
                result[at : at + count, :] = product[line * count : (line + 1) * count]

    def convolve(half):
        def combine(line, _):
            taps = [
                pl.ds(pl.multiple_of(line * padded + t * part, 8), part) for t in range(TAPS)
            ]
            e = [even_rows[tap, :] for tap in taps]
            o = [odd_rows[tap, :] for tap in taps]
            first = back(e[0] + o[1]) + e[2] + o[3] + ahead(e[4])
            second = back(o[0]) + e[1] + o[2] + ahead(e[3] + o[4])
            source = line * PLANES + (y if half == 0 else 1 - y)
            at = pl.multiple_of(source * share_in + s * part, 8)
            offset = columns[pl.ds(at, part), 2:3]
            pool_wide[pl.ds(pl.multiple_of(line * part, 8), part), :] = (
                jnp.maximum(first, second) + offset
            )
            return 0

        lax.fori_loop(0, LINES, combine, 0)
        pool_all[s, half] = pool_wide[...].astype(jnp.bfloat16)
        mine = pool_all.at[s, half]
        go(remote(mine, mine, p_send.at[half, 0], p_recv.at[half, s], b, across))
        go(remote(mine, mine, p_send.at[half, 1], p_recv.at[half, s], b, sibling))

    def pass_on(half):
        theirs = pool_all.at[across, half]
        arrived(theirs, p_recv.at[half, across])
        go(remote(theirs, theirs, p_send.at[half, 2], p_recv.at[half, across], b, sibling))

    def in_order(run, half):
        block = pool_all[run, half].astype(jnp.float32)
        for line in range(LINES):
            source = line * PLANES + (y if half == 0 else 1 - y)
            at = pl.multiple_of(source * share_in + run * part, 8)
            wide[pl.ds(at, part), :] = block[line * part : (line + 1) * part]

    def pass_units():
        for slot in range(n_units):
            holder = unit_of(slot, s) // per_shard

            @pl.when(jnp.logical_and(holder != b, holder % PLANES == y))
            def _(slot=slot):
                arrived(units.at[slot], u_recv.at[slot])
                remote(
                    units.at[slot], units.at[slot], u_send.at[slot, 0], u_recv.at[slot], mate, s
                ).start()

    for slot in range(n_units):
        unit = unit_of(slot, s)

        @pl.when(unit // per_shard == b)
        def _(slot=slot, unit=unit):
            mine = units_ref.at[unit - per_shard * b]
            remote(mine, units.at[slot], u_send.at[slot, 0], u_recv.at[slot], mate, s).start()

    own_piece.wait()
    multiply(pieces[0].reshape(LINES * padded, channels), 0, padded)
    convolve(0)
    pass_on(0)
    in_order(s, 0)
    in_order(across, 0)
    for run in (sibling, diagonal):
        arrived(pool_all.at[run, 0], p_recv.at[0, run])
        in_order(run, 0)
    for c in range(CHUNKS):
        if c == CHUNKS - 1:
            pass_units()
        for line in (z, partner, gateway, beyond)[1 if c in CROSSED else 0 :]:
            arrived(chunk(pieces.at[1, line], c), c_recv.at[1, line, c])
        part_now = pieces[1, :, c * depth : (c + 1) * depth, :].reshape(LINES * depth, channels)
        multiply(part_now, c * depth, depth)
    convolve(1)

    in_order(s, 1)
    pass_on(1)
    in_order(across, 1)
    for run in (sibling, diagonal):
        arrived(pool_all.at[run, 1], p_recv.at[1, run])
        in_order(run, 1)

    def norm(j, _):
        lanes = pl.ds(pl.multiple_of(j * bins, 128), bins)
        block = wide[:, lanes]
        centre = jnp.sum(block, axis=0, keepdims=True) / channels
        away = block - centre
        spread = jnp.sum(away * away, axis=0, keepdims=True) / channels
        normed[:, lanes] = (
            away * lax.rsqrt(spread + epsilon) * ln_wide[0] + ln_wide[1]
        ).astype(jnp.bfloat16)
        return 0

    lax.fori_loop(0, RUNS, norm, 0)

    for slot in range(n_units):
        holder = unit_of(slot, s) // per_shard

        @pl.when(jnp.logical_or(holder == b, holder % PLANES != y))
        def _(slot=slot):
            arrived(units.at[slot], u_recv.at[slot])

    here = HEADS // RUNS
    keys = here * KEY
    projected = jnp.dot(
        units[...].reshape(n_units * UNIT, channels),
        normed[...],
        preferred_element_type=jnp.float32,
    )
    q_rows[...] = (projected[:keys] * KEY ** (-0.5)).astype(jnp.bfloat16)
    k_rows[...] = jnp.transpose(projected[keys : 2 * keys]).astype(jnp.bfloat16)
    v_rows[...] = projected[2 * keys :].astype(jnp.bfloat16)

    def attend(run):
        lanes = pl.ds(pl.multiple_of(run * bins, 128), bins)
        q_now = q_rows[:, lanes]
        row = lax.broadcasted_iota(jnp.int32, q_now.shape, 0)
        apart = [jnp.where(row // KEY == h, q_now, jnp.zeros_like(q_now)) for h in range(here)]
        scores = jnp.dot(
            k_rows[...], jnp.concatenate(apart, axis=1), preferred_element_type=jnp.float32
        )
        weights = jnp.exp(scores - jnp.max(scores, axis=0, keepdims=True))
        below = jnp.sum(weights, axis=0, keepdims=True)
        rounded = weights.astype(jnp.bfloat16)
        for h in range(here):
            mine = slice(h * bins, (h + 1) * bins)
            above = jnp.dot(
                v_rows[h * VAL : (h + 1) * VAL, :],
                rounded[:, mine],
                preferred_element_type=jnp.float32,
            )
            att_out[run, h * VAL : (h + 1) * VAL, :] = (above / below[:, mine]).astype(
                jnp.bfloat16
            )

    for run, k in ((across, 0), (diagonal, 1), (sibling, 2)):
        attend(run)
        go(remote(att_out.at[run], att_in.at[s], a_send.at[k], a_recv.at[s], b, run))
    attend(s)
    att_in[s] = att_out[s]
    lanes = pl.ds(pl.multiple_of(s * bins, 128), bins)
    pooled_ref[...] = jnp.transpose(wide[:, lanes]).astype(jnp.bfloat16)
    for run in (across, diagonal, sibling):
        arrived(att_in.at[run], a_recv.at[run])
    gathered = jnp.concatenate([att_in[r].astype(jnp.float32) for r in range(RUNS)], axis=0)
    attended_ref[...] = jnp.transpose(gathered).astype(jnp.bfloat16)

    for copy in started:
        copy.wait_send()

    @pl.when(inner)
    def _():
        for c in range(CHUNKS):
            for at, line in ((1, gateway), (2, beyond)):
                relay(chunk(pieces.at[0, line], c), line, at, c).wait_send()

    for slot in range(n_units):
        holder = unit_of(slot, s) // per_shard

        @pl.when(holder % PLANES == y)
        def _(slot=slot):
            remote(
                units.at[slot], units.at[slot], u_send.at[slot, 0], u_recv.at[slot], mate, s
            ).wait_send()

        @pl.when(holder == b)
        def _(slot=slot):
            for step in range(1, LINES):
                to = ((z + step) % LINES) * PLANES + y
                remote(
                    units.at[slot], units.at[slot], u_send.at[slot, step], u_recv.at[slot], to, s
                ).wait_send()


def fused_on_device(
    sequence_input, bn_gain, bn_bias, conv_weight, conv_bias, ln_gain, ln_bias, qkv_weight
):
    _, positions, channels = sequence_input.shape
    bins = positions // 2
    rows = RUNS * bins
    n_batch = LINES * PLANES
    share = channels // RUNS
    part = share // n_batch
    s = lax.axis_index("seq")
    taps = conv_weight.shape[0]
    x = sequence_input.reshape(positions, channels)
    piece = lax.dynamic_slice_in_dim(conv_weight, s * part, part, axis=2)
    piece = piece.transpose(0, 2, 1).reshape(taps * part, channels)
    padded = -(-taps * part // 16) * 16
    piece = jnp.pad(piece, ((0, padded - taps * part), (0, 0)))

    per_shard = qkv_weight.shape[1] // UNIT
    units = qkv_weight.T.reshape(per_shard, UNIT, channels)
    n_units = per_shard * n_batch // RUNS
    keys = HEADS * KEY // RUNS
    vals = HEADS * VAL // RUNS
    bf16, f32 = jnp.bfloat16, jnp.float32
    dma = pltpu.SemaphoreType.DMA
    pooled, attended = pl.pallas_call(
        fused_kernel,
        out_shape=(
            jax.ShapeDtypeStruct((bins, channels), bf16),
            jax.ShapeDtypeStruct((bins, channels), bf16),
        ),
        in_specs=[
            *[pl.BlockSpec(memory_space=pltpu.HBM)] * 6,
            pl.BlockSpec(memory_space=pltpu.VMEM),
            pl.BlockSpec(memory_space=pltpu.HBM),
        ],
        out_specs=(pl.BlockSpec(memory_space=pltpu.VMEM),) * 2,
        scratch_shapes=[
            pltpu.VMEM((RUNS, positions, channels), bf16),
            pltpu.VMEM((RUNS, 2, channels), f32),
            pltpu.VMEM((n_batch, 2, channels), f32),
            *[pltpu.VMEM((channels,), f32)] * 5,
            pltpu.VMEM((channels, 128), f32),
            pltpu.VMEM((2, channels, bins), f32),
            pltpu.VMEM((2 * channels, rows), bf16),
            pltpu.VMEM((channels // 128, positions, 128), f32),
            pltpu.VMEM((LINES * padded, rows), f32),
            pltpu.VMEM((LINES * padded, rows), f32),
            pltpu.VMEM((PLANES, LINES, padded, channels), bf16),
            pltpu.VMEM((n_units, UNIT, channels), bf16),
            pltpu.VMEM((share // PLANES, rows), f32),
            pltpu.VMEM((RUNS, PLANES, share // PLANES, rows), bf16),
            pltpu.VMEM((channels, rows), f32),
            pltpu.VMEM((channels, rows), bf16),
            pltpu.VMEM((keys, rows), bf16),
            pltpu.VMEM((rows, keys), bf16),
            pltpu.VMEM((vals, rows), bf16),
            pltpu.VMEM((RUNS, vals, bins), bf16),
            pltpu.VMEM((RUNS, vals, bins), bf16),
            dma((7,)),
            dma((3,)),
            dma((RUNS,)),
            dma((RUNS,)),
            dma((RUNS,)),
            dma((n_batch,)),
            dma((n_batch,)),
            dma((3, CHUNKS)),
            dma((3, CHUNKS)),
            dma((3, CHUNKS)),
            dma((PLANES, LINES, CHUNKS)),
            dma((n_units, LINES)),
            dma((n_units,)),
            dma((PLANES, 3)),
            dma((PLANES, RUNS)),
            dma((3,)),
            dma((RUNS,)),
        ],
        compiler_params=pltpu.CompilerParams(
            collective_id=0, has_side_effects=True, vmem_limit_bytes=48 * 1024 * 1024
        ),
    )(
        x,
        bn_gain,
        bn_bias,
        conv_bias,
        ln_gain,
        ln_bias,
        piece,
        units,
    )
    return (pooled[None], attended[None])


def solution(mesh):
    placed = (
        P("batch", "seq", None),
        P(),
        P(),
        P(None, None, "batch"),
        P(),
        P(),
        P(),
        P(None, "batch"),
    )
    fused = mesh.shape["batch"] == LINES * PLANES and mesh.shape["seq"] == RUNS
    return jax.shard_map(
        fused_on_device if fused else on_device,
        mesh=mesh,
        in_specs=placed,
        out_specs=(P("batch", "seq", None), P("batch", "seq", None)),
        check_vma=False,
    )
```
